512 devices in a mesh: dom: 64 (over z, x, core), feat: 8 (over y).
Axes of the slice: x: 4, y: 8, z: 8, core: 2. Of those that a mesh axis runs over, the one named last changes fastest.
Arguments:
- features: bfloat16 [128, 131072], P('feat', 'dom'), may hold values from -6 to 6
- self_weight: bfloat16 [128, 256], replicated, may hold values from -0.5 to 0.5
- neigh_weight: bfloat16 [128, 256], replicated, may hold values from -0.5 to 0.5
- bias_vector: float32 [256], replicated, may hold values from -3 to 3
- tile_values: bfloat16 [4096, 128, 128], P('dom'), may hold values from -0.625 to 0.625
- tile_rows: int32 [4096], P('dom'), may hold values from 0 to 15
- tile_cols: int32 [4096], P('dom'), may hold values from 0 to 271, as said below
- send_blocks: int32 [64, 64, 4], P('dom'), may hold values from -1 to 15, as said below
- cotangent: bfloat16 [256, 131072], P('feat', 'dom'), may hold values from -6 to 6
Outputs:
- activated: bfloat16 [256, 131072], P('feat', 'dom')
- grad_features: bfloat16 [128, 131072], P('feat', 'dom')
- grad_self: float32 [128, 256], replicated
- grad_neigh: float32 [128, 256], replicated
- grad_bias: float32 [256], replicated
The draws below stay inside these ranges and needn't reach their ends.
Inputs may be any that keep to these rules, and one draw needn't show every extreme that they name: `send_blocks`: entry [s, d, c] is the local block (0 to 15) that partition s sends to partition d in slot c, or -1 for an empty slot. Only d = s + 1, s + 2, s - 1 and s + 64 / 2 (modulo 64) have live slots; live slots come first. Partition 0 sends 4 blocks to each of its four neighbours and receives 4 from each. `tile_cols`: values under 16 name a local column block; 16 + s * 4 + c names the block that partition s sends to this partition in slot c, which is always a live slot. Every live slot is named by some tile.
All inputs are finite; a program needn't handle non-finite values.
Results may differ from the reference program's by a relative error of at most 0.009.
Values may be sent and summed in bfloat16 or wider, within the bound.
A program may use at most 64 MiB of HBM per device.

```python
import math
import jax
import jax.numpy as jnp
from jax import lax

F_IN = 128
HIDDEN_DIM = 256
BLOCK = 128
NB_DEV = 16
CAP = 4
TILES_DEV = 64
NODES = 131072
N_DOM = 64


def offset_list():
    return (1, 2, -1, N_DOM // 2)


def boundary_counts(key):
    sub_key = jax.random.fold_in(key, 101)
    counts = jax.random.randint(sub_key, (N_DOM, 4), 0, CAP + 1)
    senders = jnp.arange(N_DOM, dtype=jnp.int32)[:, None]
    offsets = jnp.array(offset_list(), dtype=jnp.int32)[None, :]
    dests = (senders + offsets) % N_DOM
    forced = (senders == 0) | (dests == 0)
    return jnp.where(forced, CAP, counts).astype(jnp.int32)


def draw_send_blocks(key, part):
    counts = boundary_counts(key)
    key = jax.random.fold_in(key, 3)
    picks = jax.random.randint(key, (N_DOM, 4, CAP), 0, NB_DEV)
    full_table = -jnp.ones((N_DOM, N_DOM, CAP), jnp.int32)
    senders = jnp.arange(N_DOM, dtype=jnp.int32)
    slots = jnp.arange(CAP, dtype=jnp.int32)[None, :]
    offsets = offset_list()
    for position in range(4):
        dests = (senders + offsets[position]) % N_DOM
        live = slots < counts[:, position][:, None]
        values = jnp.where(live, picks[:, position, :], -1).astype(jnp.int32)
        full_table = full_table.at[senders, dests].set(values)
    return full_table


def draw_tile_rows(key, part):
    key = jax.random.fold_in(key, 5)
    return jax.random.randint(key, (N_DOM * TILES_DEV,), 0, NB_DEV).astype(jnp.int32)


def draw_tile_cols(key, part):
    counts = boundary_counts(key)
    key = jax.random.fold_in(key, 7)
    local_cols = jax.random.randint(key, (N_DOM, TILES_DEV), 0, NB_DEV).astype(jnp.int32)
    receivers = jnp.arange(N_DOM, dtype=jnp.int32)
    offsets = offset_list()
    columns = []
    for position in range(4):
        source = (receivers - offsets[position]) % N_DOM
        for slot in range(CAP):
            tile_index = position * CAP + slot
            live = slot < counts[source, position]
            named = NB_DEV + source * CAP + slot
            columns.append(jnp.where(live, named, local_cols[:, tile_index]))
    near_part = jnp.stack(columns, axis=1).astype(jnp.int32)
    whole = jnp.concatenate([near_part, local_cols[:, 4 * CAP:]], axis=1)
    return whole.reshape(N_DOM * TILES_DEV).astype(jnp.int32)


def shard_levels(stream_key, extent, cuts, low, high):
    factor_of, own = 1.0, jax.random.fold_in(stream_key, 6)
    for axis_at, shards_of in cuts:
        steps = jnp.exp(jax.random.uniform(jax.random.fold_in(own, axis_at), (shards_of,), jnp.float32, low / len(cuts), high / len(cuts)))
        factor_of = factor_of * jnp.repeat(steps, extent[axis_at] // shards_of).reshape([-1 if axis == axis_at else 1 for axis in range(len(extent))])
    return factor_of


def gaussian(own_key, shape, deviation, reach, cuts=(), held_as=jnp.bfloat16):
    drawn = jax.random.normal(own_key, shape, jnp.float32) * deviation
    if len(cuts) > 0:
        drawn = shard_levels(own_key, shape, cuts, -0.22, 0.18) * drawn
    return jnp.clip(drawn, min=-reach, max=reach).astype(held_as)


def setup_inputs(seed: int = 0) -> dict:
    key_of = jax.random.split(jax.random.key(seed), 10)
    return {
        "features": gaussian(key_of[0], (F_IN, NODES), 1.0, 6.0, ((0, 8), (1, 64))),
        "self_weight": gaussian(key_of[1], (F_IN, HIDDEN_DIM), F_IN ** -0.5, 0.5),
        "neigh_weight": gaussian(key_of[2], (F_IN, HIDDEN_DIM), F_IN ** -0.5, 0.5),
        "bias_vector": gaussian(key_of[3], (HIDDEN_DIM,), 0.5, 3.0, (), jnp.float32),
        "tile_values": gaussian(key_of[4], (N_DOM * TILES_DEV, BLOCK, BLOCK), ((BLOCK * 4) ** -0.5), 0.625, ((0, 64),)),
        "tile_rows": draw_tile_rows(jax.random.fold_in(key_of[9], 71), 0),
        "tile_cols": draw_tile_cols(jax.random.fold_in(key_of[9], 71), 0),
        "send_blocks": draw_send_blocks(jax.random.fold_in(key_of[9], 71), 0),
        "cotangent": gaussian(key_of[8], (HIDDEN_DIM, NODES), 1.0, 6.0, ((0, 8), (1, 64))),
    }


def reference(features, self_weight, neigh_weight, bias_vector, tile_values, tile_rows, tile_cols, send_blocks, cotangent):
    count_all = N_DOM * TILES_DEV
    device_of = jnp.arange(count_all, dtype=jnp.int32) // TILES_DEV
    remote = tile_cols - NB_DEV
    source = jnp.clip(remote // CAP, 0, N_DOM - 1).astype(jnp.int32)
    slot_of = jnp.clip(remote % CAP, 0, CAP - 1).astype(jnp.int32)
    picked = send_blocks[source, device_of, slot_of]
    global_cols = jnp.where(tile_cols < NB_DEV, device_of * NB_DEV + tile_cols, source * NB_DEV + picked).astype(jnp.int32)
    global_rows = (device_of * NB_DEV + tile_rows).astype(jnp.int32)
    total_blocks = N_DOM * NB_DEV
    feat_blocks = features.reshape(F_IN, total_blocks, BLOCK).transpose(1, 0, 2)
    tiles_dev = tile_values.reshape(N_DOM, TILES_DEV, BLOCK, BLOCK)
    rows_dev = tile_rows.reshape(N_DOM, TILES_DEV)
    cols_dev = global_cols.reshape(N_DOM, TILES_DEV)

    def aggregate(item):
        tiles_here, rows_here, cols_here = item
        pieces = feat_blocks[cols_here].astype(jnp.float32)
        products = jnp.einsum('tfk,tjk->tfj', pieces, tiles_here.astype(jnp.float32))
        return jax.ops.segment_sum(products, rows_here, num_segments=NB_DEV)
    agg_blocks = lax.map(aggregate, (tiles_dev, rows_dev, cols_dev))
    agg = agg_blocks.reshape(total_blocks, F_IN, BLOCK).transpose(1, 0, 2).reshape(F_IN, NODES).astype(jnp.bfloat16)
    pre = jnp.dot(self_weight.T, features, preferred_element_type=jnp.float32)
    pre = pre + jnp.dot(neigh_weight.T, agg, preferred_element_type=jnp.float32) + bias_vector[:, None]
    sigma = jax.nn.sigmoid(pre)
    activated = (pre * sigma).astype(jnp.bfloat16)
    dpre = (cotangent.astype(jnp.float32) * sigma * (1.0 + pre * (1.0 - sigma))).astype(jnp.bfloat16)
    norm_scale = 1.0 / math.sqrt(NODES)
    grad_self = jnp.dot(features, dpre.T, preferred_element_type=jnp.float32) * norm_scale
    grad_neigh = jnp.dot(agg, dpre.T, preferred_element_type=jnp.float32) * norm_scale
    grad_bias = lax.optimization_barrier(jnp.sum(dpre.astype(jnp.float32), axis=1)) * norm_scale
    back_self = jnp.dot(self_weight, dpre, preferred_element_type=jnp.float32).astype(jnp.bfloat16)
    back_neigh = jnp.dot(neigh_weight, dpre, preferred_element_type=jnp.float32).astype(jnp.bfloat16)
    neigh_blocks = back_neigh.reshape(F_IN, total_blocks, BLOCK).transpose(1, 0, 2)
    grows_dev = global_rows.reshape(N_DOM, TILES_DEV)

    def spread(accum, item):
        tiles_here, grows_here, cols_here = item
        selected = neigh_blocks[grows_here].astype(jnp.float32)
        contrib = jnp.einsum('tfj,tjk->tfk', selected, tiles_here.astype(jnp.float32))
        return (accum.at[cols_here].add(contrib), None)
    start_acc = jnp.zeros((total_blocks, F_IN, BLOCK), jnp.float32)
    spread_blocks, unused = lax.scan(spread, start_acc, (tiles_dev, grows_dev, cols_dev))
    through_graph = spread_blocks.transpose(1, 0, 2).reshape(F_IN, NODES)
    grad_features = (back_self.astype(jnp.float32) + through_graph).astype(jnp.bfloat16)
    return (activated, grad_features, grad_self, grad_neigh, grad_bias)
```

```python
import functools
import math

import jax
import jax.numpy as jnp
from jax import lax
from jax.experimental import pallas as pl
from jax.experimental.pallas import tpu as pltpu
from jax.sharding import PartitionSpec as P

X_SIZE = 4
CORES = 2
BLOCK = 128
MESH = pl.DeviceIdType.MESH
F32 = jnp.float32
BF16 = jnp.bfloat16


def remote(src, dst, send_sem, recv_sem, device):
    return pltpu.make_async_remote_copy(
        src_ref=src,
        dst_ref=dst,
        send_sem=send_sem,
        recv_sem=recv_sem,
        device_id=device,
        device_id_type=MESH,
    )


def dot_nt(a, b):
    return lax.dot_general(a, b, (((1,), (1,)), ((), ())), preferred_element_type=F32)


def dot_nn(a, b):
    return lax.dot_general(a, b, (((1,), (0,)), ((), ())), preferred_element_type=F32)


def kernel(
    dims,
    tile_rows,
    tile_cols,
    send_blocks,
    features,
    self_weight,
    neigh_weight,
    bias,
    tile_values,
    cotangent,
    activated,
    grad_features,
    grad_self,
    grad_neigh,
    grad_bias,
    slots,
    fv,
    tiles,
    w_self,
    w_neigh,
    w_cat,
    w_t,
    bias_row,
    bias_mat,
    xg,
    ct,
    own_tab,
    tab,
    stage,
    agg,
    act,
    bk,
    bkr,
    btab,
    prod,
    rb_send,
    rb_recv,
    part,
    part_recv,
    rs_src,
    rs_recv,
    y_src,
    y_recv,
    g_full,
    b_full,
    local_sem,
    own_sem,
    halo_sem,
    feat_sem,
    cot_sem,
    agg_sem,
    back_sem,
    act_sem,
    ret_sem,
    core_sem,
    rs_sem,
    yr_sem,
    ag_sem,
):
    dom_size, y_size, nb, tile_count, in_dim, hidden, norm_scale = dims
    z_size = dom_size // (X_SIZE * CORES)
    xz = X_SIZE * z_size
    fr = in_dim // y_size
    hr = hidden // y_size
    vb = nb // y_size
    vc = vb * BLOCK
    tpq = (in_dim // 8) * (hidden // 128) // xz

    dom = lax.axis_index("dom")
    fy = lax.axis_index("feat")
    core = lax.rem(dom, CORES)
    q = dom // CORES
    my_z = q // X_SIZE
    my_x = lax.rem(q, X_SIZE)

    offsets = (1, 2, dom_size - 1, dom_size // 2)
    y_peers = [lax.rem(fy + i, y_size) for i in range(1, y_size)]
    sibling = (q * CORES + 1 - core, fy)
    xz_peers = []
    for dz in range(z_size):
        for dx in range(X_SIZE):
            if dz or dx:
                pz = lax.rem(my_z + dz, z_size)
                px = lax.rem(my_x + dx, X_SIZE)
                xz_peers.append(pz * X_SIZE + px)

    loads = [
        pltpu.make_async_copy(features, fv, local_sem.at[0]),
        pltpu.make_async_copy(self_weight, w_self, local_sem.at[1]),
        pltpu.make_async_copy(neigh_weight, w_neigh, local_sem.at[2]),
        pltpu.make_async_copy(bias, bias_row, local_sem.at[3]),
        pltpu.make_async_copy(tile_values, tiles, local_sem.at[4]),
    ]
    for copy in loads:
        copy.start()

    barrier = pltpu.get_barrier_semaphore()
    greeted = 0
    for p in y_peers:
        pl.semaphore_signal(barrier, inc=1, device_id=(dom, p), device_id_type=MESH)
        greeted += 1
    for off in (1, 2, dom_size - 1, dom_size - 2, dom_size // 2):
        pl.semaphore_signal(
            barrier, inc=1, device_id=(lax.rem(dom + off, dom_size), fy), device_id_type=MESH
        )
        greeted += 1
    pl.semaphore_signal(barrier, inc=1, device_id=sibling, device_id_type=MESH)
    greeted += 1
    for p in xz_peers:
        pl.semaphore_signal(
            barrier, inc=1, device_id=(p * CORES + core, fy), device_id_type=MESH
        )
        greeted += 1

    def slot_body(t, carry):
        col = tile_cols[t]
        far = jnp.maximum(col - nb, 0)
        back = lax.rem(dom + dom_size - far // 4, dom_size)
        place = jnp.where(
            back == offsets[0],
            0,
            jnp.where(back == offsets[1], 1, jnp.where(back == offsets[2], 2, 3)),
        )
        slots[t] = jnp.where(col < nb, col, nb + place * 4 + lax.rem(far, 4))
        return carry

    lax.fori_loop(0, tile_count, slot_body, 0)

    owners = []
    for pos in range(4):
        to = lax.rem(dom + offsets[pos], dom_size)
        owners.append([send_blocks[0, to, c] for c in range(4)])
    loads[0].wait()
    for b in range(nb):
        own_tab[b] = fv[:, b * BLOCK : (b + 1) * BLOCK]
        tab[b] = fv[:, b * BLOCK : (b + 1) * BLOCK]
    for pos in range(4):
        for c in range(4):
            stage[pos, c] = own_tab[jnp.maximum(owners[pos][c], 0)]

    pl.semaphore_wait(barrier, greeted)

    sends = []
    halo = []
    for pos in range(4):
        to = lax.rem(dom + offsets[pos], dom_size)
        halo.append(
            remote(
                stage.at[pos],
                tab.at[pl.ds(nb + 4 * pos, 4)],
                halo_sem.at[0, pos],
                halo_sem.at[1, pos],
                (to, fy),
            )
        )
        halo[-1].start()
    sends += halo
    feat_in = []
    for i, p in enumerate(y_peers):
        feat_in.append(
            remote(
                fv.at[:, pl.ds(pl.multiple_of(p * vc, vc), vc)],
                xg.at[fy, 0],
                feat_sem.at[0, i],
                feat_sem.at[1, i],
                (dom, p),
            )
        )
        feat_in[-1].start()
    sends += feat_in
    cot_in = []
    for i, p in enumerate(y_peers):
        cot_in.append(
            remote(
                cotangent.at[:, pl.ds(pl.multiple_of(p * vc, vc), vc)],
                ct.at[fy],
                cot_sem.at[0, i],
                cot_sem.at[1, i],
                (dom, p),
            )
        )
        cot_in[-1].start()
    sends += cot_in
    own_feat = pltpu.make_async_copy(
        fv.at[:, pl.ds(pl.multiple_of(fy * vc, vc), vc)], xg.at[fy, 0], own_sem.at[0]
    )
    own_feat.start()
    own_cot = pltpu.make_async_copy(
        cotangent.at[:, pl.ds(pl.multiple_of(fy * vc, vc), vc)], ct.at[fy], own_sem.at[1]
    )
    own_cot.start()

    for copy in loads[1:4]:
        copy.wait()
    for y in range(y_size):
        w_cat[y, 0] = w_self[y * fr : (y + 1) * fr, :]
        w_cat[y, 1] = w_neigh[y * fr : (y + 1) * fr, :]
    weights = w_cat[...].reshape(2 * in_dim, hidden)
    w_t[...] = weights.astype(F32).T.astype(BF16)
    bias_mat[...] = jnp.broadcast_to(bias_row[...], (128, hidden)).T
    loads[4].wait()

    for copy in halo:
        copy.wait_recv()

    zero = jnp.zeros((fr, BLOCK), F32)

    def agg_body(t, sums):
        p = dot_nt(tab[slots[t]], tiles[t])
        r = tile_rows[t]
        return tuple(jnp.where(r == b, s + p, s) for b, s in enumerate(sums))

    sums = lax.fori_loop(0, tile_count, agg_body, (zero,) * nb, unroll=8)
    for b in range(nb):
        agg[b // vb, :, (b % vb) * BLOCK : (b % vb + 1) * BLOCK] = sums[b].astype(BF16)

    agg_in = []
    for i, p in enumerate(y_peers):
        agg_in.append(
            remote(agg.at[p], xg.at[fy, 1], agg_sem.at[0, i], agg_sem.at[1, i], (dom, p))
        )
        agg_in[-1].start()
    sends += agg_in
    xg[fy, 1] = agg[fy]

    own_feat.wait()
    own_cot.wait()
    for copy in feat_in + cot_in + agg_in:
        copy.wait_recv()

    both = xg[...].reshape(2 * in_dim, vc)
    pre = dot_nn(w_t[...], both) + jnp.concatenate([bias_mat[...]] * vb, axis=1)
    sigma = jax.nn.sigmoid(pre)
    cot = ct[...].reshape(hidden, vc).astype(F32)
    dpre = (cot * sigma * (1.0 + pre * (1.0 - sigma))).astype(BF16)
    act[...] = (pre * sigma).astype(BF16).reshape(y_size, hr, vc)
    bk[...] = dot_nn(weights, dpre).astype(BF16).reshape(y_size, 2 * fr, vc)

    back_in = []
    for i, p in enumerate(y_peers):
        back_in.append(
            remote(bk.at[p], bkr.at[fy], back_sem.at[0, i], back_sem.at[1, i], (dom, p))
        )
        back_in[-1].start()
    sends += back_in
    bkr[fy] = bk[fy]

    grads = dot_nt(both, dpre)
    ones = jnp.ones((16, vc), BF16)
    bias_part = dot_nt(ones, dpre)
    row_tiles = in_dim // 8
    for kind in range(2):
        for rt in range(row_tiles):
            src = (rt * 8 // fr) * 2 * fr + kind * fr + (rt * 8) % fr
            for c in range(2):
                n = rt * 2 + c
                part[kind, n // tpq, (n % tpq) * 8 : (n % tpq + 1) * 8, :] = grads[
                    src : src + 8, c * 128 : (c + 1) * 128
                ]
        for n in range(xz):
            part[kind, n, 8 * tpq : 8 * tpq + 1, :] = bias_part[
                0:1, kind * 128 : (kind + 1) * 128
            ]
    swap = remote(part.at[1 - core], part_recv, core_sem.at[0], core_sem.at[1], sibling)
    swap.start()
    sends.append(swap)

    act_in = []
    for i, p in enumerate(y_peers):
        act_in.append(
            remote(
                act.at[p],
                activated.at[:, pl.ds(pl.multiple_of(fy * vc, vc), vc)],
                act_sem.at[0, i],
                act_sem.at[1, i],
                (dom, p),
            )
        )
        act_in[-1].start()
    sends += act_in
    own_act = pltpu.make_async_copy(
        act.at[fy], activated.at[:, pl.ds(pl.multiple_of(fy * vc, vc), vc)], own_sem.at[2]
    )
    own_act.start()

    swap.wait_recv()
    rs_src[...] = part[core] + part_recv[...]
    rs_in = []
    for i, p in enumerate(xz_peers):
        rs_in.append(
            remote(
                rs_src.at[p],
                rs_recv.at[q],
                rs_sem.at[0, i],
                rs_sem.at[1, i],
                (p * CORES + core, fy),
            )
        )
        rs_in[-1].start()
    sends += rs_in
    rs_recv[q] = rs_src[q]

    for copy in back_in:
        copy.wait_recv()
    for b in range(nb):
        btab[b] = bkr[b // vb, fr : 2 * fr, (b % vb) * BLOCK : (b % vb + 1) * BLOCK]

    def far_body(t, sums):
        p = dot_nn(btab[tile_rows[t]], tiles[t])
        prod[t] = p
        s = slots[t] - nb
        return tuple(jnp.where(s == b, v + p, v) for b, v in enumerate(sums))

    sums = lax.fori_loop(0, tile_count, far_body, (zero,) * 16, unroll=8)
    for n in range(16):
        rb_send[n // 4, n % 4] = sums[n]
    ret = []
    for pos in range(4):
        to = lax.rem(dom + dom_size - offsets[pos], dom_size)
        ret.append(
            remote(
                rb_send.at[pos],
                rb_recv.at[pos],
                ret_sem.at[0, pos],
                ret_sem.at[1, pos],
                (to, fy),
            )
        )
        ret[-1].start()
    sends += ret

    for copy in rs_in:
        copy.wait_recv()
    total = rs_recv[0]
    for n in range(1, xz):
        total = total + rs_recv[n]
    y_src[...] = total
    y_recv[fy] = total
    y_in = []
    for i, p in enumerate(y_peers):
        y_in.append(
            remote(y_src, y_recv.at[fy], yr_sem.at[0, i], yr_sem.at[1, i], (dom, p))
        )
        y_in[-1].start()
    sends += y_in

    def near_body(t, sums):
        p = prod[t]
        s = slots[t]
        return tuple(jnp.where(s == b, v + p, v) for b, v in enumerate(sums))

    start = tuple(
        bkr[b // vb, 0:fr, (b % vb) * BLOCK : (b % vb + 1) * BLOCK].astype(F32)
        for b in range(nb)
    )
    sums = lax.fori_loop(0, tile_count, near_body, start, unroll=8)

    for copy in ret:
        copy.wait_recv()
    for pos in range(4):
        for c in range(4):
            term = rb_recv[pos, c]
            sums = tuple(
                jnp.where(owners[pos][c] == b, v + term, v) for b, v in enumerate(sums)
            )
    for b in range(nb):
        grad_features[:, b * BLOCK : (b + 1) * BLOCK] = sums[b].astype(BF16)

    for copy in y_in:
        copy.wait_recv()
    total = y_recv[0]
    for n in range(1, y_size):
        total = total + y_recv[n]
    total = total * norm_scale
    g_full[core, q] = total[: 8 * tpq]
    b_full[core] = total[8 * tpq : 8 * tpq + 1]
    bias_swap = remote(
        b_full.at[core], b_full.at[core], core_sem.at[2], core_sem.at[3], sibling
    )
    bias_swap.start()
    sends.append(bias_swap)
    ag_in = []
    for i, p in enumerate(xz_peers):
        ag_in.append(
            remote(
                g_full.at[core, q],
                g_full.at[core, q],
                ag_sem.at[0, i],
                ag_sem.at[1, i],
                (p * CORES + core, fy),
            )
        )
        ag_in[-1].start()
    sends += ag_in
    for copy in ag_in:
        copy.wait_recv()
    full_swap = remote(
        g_full.at[core], g_full.at[core], core_sem.at[4], core_sem.at[5], sibling
    )
    full_swap.start()
    sends.append(full_swap)
    own_act.wait()
    for copy in act_in:
        copy.wait_recv()
    bias_swap.wait_recv()
    for kind in range(2):
        grad_bias[:, kind * 128 : (kind + 1) * 128] = b_full[kind]
    full_swap.wait_recv()
    for kind, out in ((0, grad_self), (1, grad_neigh)):
        for rt in range(row_tiles):
            for c in range(2):
                n = rt * 2 + c
                out[rt * 8 : (rt + 1) * 8, c * 128 : (c + 1) * 128] = g_full[
                    kind, n // tpq, (n % tpq) * 8 : (n % tpq + 1) * 8, :
                ]
    for copy in sends:
        copy.wait_send()


def local(
    features,
    self_weight,
    neigh_weight,
    bias_vector,
    tile_values,
    tile_rows,
    tile_cols,
    send_blocks,
    cotangent,
):
    dom_size = lax.axis_size("dom")
    y_size = lax.axis_size("feat")
    xz = dom_size // CORES
    fr, vertices = features.shape
    hr = cotangent.shape[0]
    in_dim, hidden = self_weight.shape
    tile_count = tile_values.shape[0]
    nb = vertices // BLOCK
    vc = vertices // y_size
    tpq = (in_dim // 8) * (hidden // 128) // xz
    ext = 8 * tpq + 1
    dims = (
        dom_size,
        y_size,
        nb,
        tile_count,
        in_dim,
        hidden,
        1.0 / math.sqrt(vertices * dom_size),
    )
    smem = pl.BlockSpec(memory_space=pltpu.SMEM)
    hbm = pl.BlockSpec(memory_space=pl.ANY)
    vmem = pl.BlockSpec(memory_space=pltpu.VMEM)
    dma = pltpu.SemaphoreType.DMA
    outs = pl.pallas_call(
        functools.partial(kernel, dims),
        out_shape=(
            jax.ShapeDtypeStruct((hr, vertices), BF16),
            jax.ShapeDtypeStruct((fr, vertices), BF16),
            jax.ShapeDtypeStruct((in_dim, hidden), F32),
            jax.ShapeDtypeStruct((in_dim, hidden), F32),
            jax.ShapeDtypeStruct((1, hidden), F32),
        ),
        in_specs=[smem, smem, smem] + [hbm] * 6,
        out_specs=(hbm, vmem, vmem, vmem, vmem),
        scratch_shapes=[
            pltpu.SMEM((tile_count,), jnp.int32),
            pltpu.VMEM((fr, vertices), BF16),
            pltpu.VMEM((tile_count, BLOCK, BLOCK), BF16),
            pltpu.VMEM((in_dim, hidden), BF16),
            pltpu.VMEM((in_dim, hidden), BF16),
            pltpu.VMEM((y_size, 2, fr, hidden), BF16),
            pltpu.VMEM((hidden, 2 * in_dim), BF16),
            pltpu.VMEM((1, hidden), F32),
            pltpu.VMEM((hidden, 128), F32),
            pltpu.VMEM((y_size, 2, fr, vc), BF16),
            pltpu.VMEM((y_size, hr, vc), BF16),
            pltpu.VMEM((nb, fr, BLOCK), BF16),
            pltpu.VMEM((nb + 16, fr, BLOCK), BF16),
            pltpu.VMEM((4, 4, fr, BLOCK), BF16),
            pltpu.VMEM((y_size, fr, vc), BF16),
            pltpu.VMEM((y_size, hr, vc), BF16),
            pltpu.VMEM((y_size, 2 * fr, vc), BF16),
            pltpu.VMEM((y_size, 2 * fr, vc), BF16),
            pltpu.VMEM((nb, fr, BLOCK), BF16),
            pltpu.VMEM((tile_count, fr, BLOCK), F32),
            pltpu.VMEM((4, 4, fr, BLOCK), F32),
            pltpu.VMEM((4, 4, fr, BLOCK), F32),
            pltpu.VMEM((2, xz, ext, 128), F32),
            pltpu.VMEM((xz, ext, 128), F32),
            pltpu.VMEM((xz, ext, 128), F32),
            pltpu.VMEM((xz, ext, 128), F32),
            pltpu.VMEM((ext, 128), F32),
            pltpu.VMEM((y_size, ext, 128), F32),
            pltpu.VMEM((2, xz, 8 * tpq, 128), F32),
            pltpu.VMEM((2, 1, 128), F32),
            dma((5,)),
            dma((3,)),
            dma((2, 4)),
            dma((2, y_size - 1)),
            dma((2, y_size - 1)),
            dma((2, y_size - 1)),
            dma((2, y_size - 1)),
            dma((2, y_size - 1)),
            dma((2, 4)),
            dma((6,)),
            dma((2, xz - 1)),
            dma((2, y_size - 1)),
            dma((2, xz - 1)),
        ],
        compiler_params=pltpu.CompilerParams(
            collective_id=0, has_side_effects=True, vmem_limit_bytes=32 * 1024 * 1024
        ),
        name="graph_layer",
    )(
        tile_rows,
        tile_cols,
        send_blocks,
        features,
        self_weight,
        neigh_weight,
        bias_vector.reshape(1, hidden),
        tile_values,
        cotangent,
    )
    activated, grad_features, grad_self, grad_neigh, grad_bias = outs
    return (activated, grad_features, grad_self, grad_neigh, grad_bias.reshape(hidden))


def solution(mesh):
    in_specs = (
        P("feat", "dom"),
        P(),
        P(),
        P(),
        P("dom", None, None),
        P("dom"),
        P("dom"),
        P("dom", None, None),
        P("feat", "dom"),
    )
    out_specs = (P("feat", "dom"), P("feat", "dom"), P(), P(), P())
    return jax.shard_map(local, mesh=mesh, in_specs=in_specs, out_specs=out_specs, check_vma=False)
```

```python
import functools
import math

import jax
import jax.numpy as jnp
from jax import lax
from jax.experimental import pallas as pl
from jax.experimental.pallas import tpu as pltpu
from jax.sharding import PartitionSpec as P

X_SIZE = 4
CORES = 2
BLOCK = 128
MESH = pl.DeviceIdType.MESH
F32 = jnp.float32
BF16 = jnp.bfloat16


def remote(src, dst, send_sem, recv_sem, device):
    return pltpu.make_async_remote_copy(
        src_ref=src,
        dst_ref=dst,
        send_sem=send_sem,
        recv_sem=recv_sem,
        device_id=device,
        device_id_type=MESH,
    )


def dot_nt(a, b):
    return lax.dot_general(a, b, (((1,), (1,)), ((), ())), preferred_element_type=F32)


def dot_nn(a, b):
    return lax.dot_general(a, b, (((1,), (0,)), ((), ())), preferred_element_type=F32)


def kernel(
    dims,
    rows_in,
    cols_in,
    blocks_in,
    features,
    self_weight,
    neigh_weight,
    bias,
    tile_values,
    cotangent,
    activated,
    grad_features,
    grad_self,
    grad_neigh,
    grad_bias,
    tile_rows,
    tile_cols,
    send_blocks,
    slots,
    gf,
    gs,
    gn,
    gb,
    fv,
    tiles,
    w_self,
    w_neigh,
    w_cat,
    w_t,
    bias_row,
    bias_mat,
    xg,
    ct,
    own_tab,
    tab,
    stage,
    agg,
    act,
    bk,
    bkr,
    btab,
    prod,
    rb_send,
    rb_recv,
    part,
    part_recv,
    rs_src,
    rs_recv,
    y_src,
    y_recv,
    g_full,
    b_full,
    local_sem,
    own_sem,
    halo_sem,
    feat_sem,
    cot_sem,
    agg_sem,
    back_sem,
    act_sem,
    ret_sem,
    core_sem,
    rs_sem,
    yr_sem,
    ag_sem,
    swap_sem,
):
    dom_size, y_size, nb, tile_count, in_dim, hidden, norm_scale = dims
    z_size = dom_size // (X_SIZE * CORES)
    xz = X_SIZE * z_size
    fr = in_dim // y_size
    hr = hidden // y_size
    vb = nb // y_size
    vc = vb * BLOCK
    tpq = (in_dim // 8) * (hidden // 128) // xz

    dom = lax.axis_index("dom")
    fy = lax.axis_index("feat")
    core = lax.rem(dom, CORES)
    q = dom // CORES
    my_z = q // X_SIZE
    my_x = lax.rem(q, X_SIZE)

    offsets = (1, 2, dom_size - 1, dom_size // 2)
    y_peers = [lax.rem(fy + i, y_size) for i in range(1, y_size)]
    sibling = (q * CORES + 1 - core, fy)
    xz_peers = []
    for dz in range(z_size):
        for dx in range(X_SIZE):
            if dz or dx:
                pz = lax.rem(my_z + dz, z_size)
                px = lax.rem(my_x + dx, X_SIZE)
                xz_peers.append(pz * X_SIZE + px)

    loads = [
        pltpu.make_async_copy(blocks_in, send_blocks, local_sem.at[5]),
        pltpu.make_async_copy(features, fv, local_sem.at[0]),
        pltpu.make_async_copy(cols_in, tile_cols, local_sem.at[6]),
        pltpu.make_async_copy(rows_in, tile_rows, local_sem.at[7]),
        pltpu.make_async_copy(self_weight, w_self, local_sem.at[1]),
        pltpu.make_async_copy(neigh_weight, w_neigh, local_sem.at[2]),
        pltpu.make_async_copy(bias, bias_row, local_sem.at[3]),
        pltpu.make_async_copy(tile_values, tiles, local_sem.at[4]),
    ]
    for copy in loads:
        copy.start()

    barrier = pltpu.get_barrier_semaphore()
    greeted = 0
    for p in y_peers:
        pl.semaphore_signal(barrier, inc=1, device_id=(dom, p), device_id_type=MESH)
        greeted += 1
    for off in (1, 2, dom_size - 1, dom_size - 2, dom_size // 2):
        pl.semaphore_signal(
            barrier, inc=1, device_id=(lax.rem(dom + off, dom_size), fy), device_id_type=MESH
        )
        greeted += 1
    pl.semaphore_signal(barrier, inc=1, device_id=sibling, device_id_type=MESH)
    greeted += 1
    for p in xz_peers:
        pl.semaphore_signal(
            barrier, inc=1, device_id=(p * CORES + core, fy), device_id_type=MESH
        )
        greeted += 1

    loads[0].wait()
    owners = []
    for pos in range(4):
        to = lax.rem(dom + offsets[pos], dom_size)
        owners.append([send_blocks[0, c, to] for c in range(4)])
    loads[1].wait()
    for b in range(nb):
        own_tab[b] = fv[:, b * BLOCK : (b + 1) * BLOCK]
    for pos in range(4):
        for c in range(4):
            stage[pos, c] = own_tab[jnp.maximum(owners[pos][c], 0)]

    pl.semaphore_wait(barrier, greeted)

    sends = []
    halo = []
    for pos in range(4):
        to = lax.rem(dom + offsets[pos], dom_size)
        halo.append(
            remote(
                stage.at[pos],
                tab.at[pl.ds(nb + 4 * pos, 4)],
                halo_sem.at[0, pos],
                halo_sem.at[1, pos],
                (to, fy),
            )
        )
        halo[-1].start()
    sends += halo
    feat_in = []
    for i, p in enumerate(y_peers):
        feat_in.append(
            remote(
                fv.at[:, pl.ds(pl.multiple_of(p * vc, vc), vc)],
                xg.at[fy, 0],
                feat_sem.at[0, i],
                feat_sem.at[1, i],
                (dom, p),
            )
        )
        feat_in[-1].start()
    sends += feat_in
    cot_in = []
    for i, p in enumerate(y_peers):
        cot_in.append(
            remote(
                cotangent.at[:, pl.ds(pl.multiple_of(p * vc, vc), vc)],
                ct.at[fy],
                cot_sem.at[0, i],
                cot_sem.at[1, i],
                (dom, p),
            )
        )
        cot_in[-1].start()
    sends += cot_in
    own_feat = pltpu.make_async_copy(
        fv.at[:, pl.ds(pl.multiple_of(fy * vc, vc), vc)], xg.at[fy, 0], own_sem.at[0]
    )
    own_feat.start()
    own_cot = pltpu.make_async_copy(
        cotangent.at[:, pl.ds(pl.multiple_of(fy * vc, vc), vc)], ct.at[fy], own_sem.at[1]
    )
    own_cot.start()

    def slot_body(t, carry):
        col = tile_cols[t]
        far = jnp.maximum(col - nb, 0)
        back = lax.rem(dom + dom_size - far // 4, dom_size)
        place = jnp.where(
            back == offsets[0],
            0,
            jnp.where(back == offsets[1], 1, jnp.where(back == offsets[2], 2, 3)),
        )
        slots[t] = jnp.where(col < nb, col, nb + place * 4 + lax.rem(far, 4))
        return carry

    loads[2].wait()
    loads[3].wait()
    lax.fori_loop(0, tile_count, slot_body, 0, unroll=4)

    for b in range(nb):
        tab[b] = fv[:, b * BLOCK : (b + 1) * BLOCK]

    for copy in loads[4:7]:
        copy.wait()
    for y in range(y_size):
        w_cat[y, 0] = w_self[y * fr : (y + 1) * fr, :]
        w_cat[y, 1] = w_neigh[y * fr : (y + 1) * fr, :]
    weights = w_cat[...].reshape(2 * in_dim, hidden)
    w_t[...] = weights.astype(F32).T.astype(BF16)
    bias_mat[...] = jnp.broadcast_to(bias_row[...], (128, hidden)).T
    loads[7].wait()

    for copy in halo:
        copy.wait_recv()

    zero = jnp.zeros((fr, BLOCK), F32)

    def agg_body(t, sums):
        p = dot_nt(tab[slots[t]], tiles[t])
        r = tile_rows[t]
        return tuple(jnp.where(r == b, s + p, s) for b, s in enumerate(sums))

    sums = lax.fori_loop(0, tile_count, agg_body, (zero,) * nb, unroll=8)
    for b in range(nb):
        agg[b // vb, :, (b % vb) * BLOCK : (b % vb + 1) * BLOCK] = sums[b].astype(BF16)

    agg_in = []
    for i, p in enumerate(y_peers):
        agg_in.append(
            remote(agg.at[p], xg.at[fy, 1], agg_sem.at[0, i], agg_sem.at[1, i], (dom, p))
        )
        agg_in[-1].start()
    sends += agg_in
    xg[fy, 1] = agg[fy]

    own_feat.wait()
    own_cot.wait()
    for copy in feat_in + cot_in + agg_in:
        copy.wait_recv()

    both = xg[...].reshape(2 * in_dim, vc)
    pre = dot_nn(w_t[...], both) + jnp.concatenate([bias_mat[...]] * vb, axis=1)
    sigma = jax.nn.sigmoid(pre)
    cot = ct[...].reshape(hidden, vc).astype(F32)
    dpre = (cot * sigma * (1.0 + pre * (1.0 - sigma))).astype(BF16)
    grads = dot_nt(both, dpre)
    ones = jnp.ones((16, vc), BF16)
    bias_part = dot_nt(ones, dpre)
    row_tiles = in_dim // 8
    for kind in range(2):
        for rt in range(row_tiles):
            src = (rt * 8 // fr) * 2 * fr + kind * fr + (rt * 8) % fr
            for c in range(2):
                n = rt * 2 + c
                part[kind, n // tpq, (n % tpq) * 8 : (n % tpq + 1) * 8, :] = grads[
                    src : src + 8, c * 128 : (c + 1) * 128
                ]
        for n in range(xz):
            part[kind, n, 8 * tpq : 8 * tpq + 1, :] = bias_part[
                0:1, kind * 128 : (kind + 1) * 128
            ]
    swap = remote(part.at[1 - core], part_recv, core_sem.at[0], core_sem.at[1], sibling)
    swap.start()
    sends.append(swap)

    act[...] = (pre * sigma).astype(BF16).reshape(y_size, hr, vc)
    bk[...] = dot_nn(weights, dpre).astype(BF16).reshape(y_size, 2 * fr, vc)

    back_in = []
    for i, p in enumerate(y_peers):
        back_in.append(
            remote(bk.at[p], bkr.at[fy], back_sem.at[0, i], back_sem.at[1, i], (dom, p))
        )
        back_in[-1].start()
    sends += back_in
    bkr[fy] = bk[fy]

    swap.wait_recv()
    rs_src[...] = part[core] + part_recv[...]
    rs_in = []
    for i, p in enumerate(xz_peers):
        rs_in.append(
            remote(
                rs_src.at[p],
                rs_recv.at[q],
                rs_sem.at[0, i],
                rs_sem.at[1, i],
                (p * CORES + core, fy),
            )
        )
        rs_in[-1].start()
    sends += rs_in
    rs_recv[q] = rs_src[q]

    act_in = []
    for i, p in enumerate(y_peers):
        act_in.append(
            remote(
                act.at[p],
                activated.at[:, pl.ds(pl.multiple_of(fy * vc, vc), vc)],
                act_sem.at[0, i],
                act_sem.at[1, i],
                (dom, p),
            )
        )
        act_in[-1].start()
    sends += act_in
    own_act = pltpu.make_async_copy(
        act.at[fy], activated.at[:, pl.ds(pl.multiple_of(fy * vc, vc), vc)], own_sem.at[2]
    )
    own_act.start()

    for copy in back_in:
        copy.wait_recv()
    for b in range(nb):
        btab[b] = bkr[b // vb, fr : 2 * fr, (b % vb) * BLOCK : (b % vb + 1) * BLOCK]

    def far_body(t, sums):
        p = dot_nn(btab[tile_rows[t]], tiles[t])
        prod[t] = p
        s = slots[t] - nb
        return tuple(jnp.where(s == b, v + p, v) for b, v in enumerate(sums))

    sums = lax.fori_loop(0, tile_count, far_body, (zero,) * 16, unroll=8)
    for n in range(16):
        rb_send[n // 4, n % 4] = sums[n]
    ret = []
    for pos in range(4):
        to = lax.rem(dom + dom_size - offsets[pos], dom_size)
        ret.append(
            remote(
                rb_send.at[pos],
                rb_recv.at[pos],
                ret_sem.at[0, pos],
                ret_sem.at[1, pos],
                (to, fy),
            )
        )
        ret[-1].start()
    sends += ret

    for copy in rs_in:
        copy.wait_recv()
    total = rs_recv[0]
    for n in range(1, xz):
        total = total + rs_recv[n]
    y_src[...] = total
    y_recv[fy] = total
    y_in = []
    for i, p in enumerate(y_peers):
        y_in.append(
            remote(y_src, y_recv.at[fy], yr_sem.at[0, i], yr_sem.at[1, i], (dom, p))
        )
        y_in[-1].start()
    sends += y_in

    def near_body(t, sums):
        p = prod[t]
        s = slots[t]
        return tuple(jnp.where(s == b, v + p, v) for b, v in enumerate(sums))

    start = tuple(
        bkr[b // vb, 0:fr, (b % vb) * BLOCK : (b % vb + 1) * BLOCK].astype(F32)
        for b in range(nb)
    )
    sums = lax.fori_loop(0, tile_count, near_body, start, unroll=8)

    for copy in ret:
        copy.wait_recv()
    for pos in range(4):
        for c in range(4):
            term = rb_recv[pos, c]
            sums = tuple(
                jnp.where(owners[pos][c] == b, v + term, v) for b, v in enumerate(sums)
            )
    for b in range(nb):
        gf[:, b * BLOCK : (b + 1) * BLOCK] = sums[b].astype(BF16)
    stores = [pltpu.make_async_copy(gf, grad_features, local_sem.at[0])]
    stores[0].start()

    for copy in y_in:
        copy.wait_recv()
    total = y_recv[0]
    for n in range(1, y_size):
        total = total + y_recv[n]
    total = total * norm_scale
    g_full[core, q] = total[: 8 * tpq]
    b_full[core] = total[8 * tpq : 8 * tpq + 1]
    bias_swap = remote(
        b_full.at[core], b_full.at[core], core_sem.at[2], core_sem.at[3], sibling
    )
    bias_swap.start()
    sends.append(bias_swap)
    ag_in = []
    for i, p in enumerate(xz_peers):
        ag_in.append(
            remote(
                g_full.at[core, q],
                g_full.at[core, q],
                ag_sem.at[0, i],
                ag_sem.at[1, i],
                (p * CORES + core, fy),
            )
        )
        ag_in[-1].start()
    sends += ag_in
    swaps = []
    for dz in range(z_size):
        for copy in ag_in[max(dz * X_SIZE - 1, 0) : (dz + 1) * X_SIZE - 1]:
            copy.wait_recv()
        plane = pl.ds(lax.rem(my_z + z_size - dz, z_size) * X_SIZE, X_SIZE)
        swaps.append(
            remote(
                g_full.at[core, plane],
                g_full.at[core, plane],
                swap_sem.at[0, dz],
                swap_sem.at[1, dz],
                sibling,
            )
        )
        swaps[-1].start()
    sends += swaps
    bias_swap.wait_recv()
    for kind in range(2):
        gb[:, kind * 128 : (kind + 1) * 128] = b_full[kind]
    for copy in swaps:
        copy.wait_recv()
    for kind, out in ((0, gs), (1, gn)):
        for rt in range(row_tiles):
            for c in range(2):
                n = rt * 2 + c
                out[rt * 8 : (rt + 1) * 8, c * 128 : (c + 1) * 128] = g_full[
                    kind, n // tpq, (n % tpq) * 8 : (n % tpq + 1) * 8, :
                ]
    stores += [
        pltpu.make_async_copy(gs, grad_self, local_sem.at[1]),
        pltpu.make_async_copy(gn, grad_neigh, local_sem.at[2]),
        pltpu.make_async_copy(gb, grad_bias, local_sem.at[3]),
    ]
    for copy in stores[1:]:
        copy.start()
    own_act.wait()
    for copy in act_in:
        copy.wait_recv()
    for copy in stores:
        copy.wait()
    for copy in sends:
        copy.wait_send()


def place(*refs):
    sems = refs[10]
    copies = [pltpu.make_async_copy(refs[i], refs[5 + i], sems.at[i]) for i in range(5)]
    for copy in copies:
        copy.start()
    for copy in copies:
        copy.wait()


def local(
    features,
    self_weight,
    neigh_weight,
    bias_vector,
    tile_values,
    tile_rows,
    tile_cols,
    send_blocks,
    cotangent,
):
    dom_size = lax.axis_size("dom")
    y_size = lax.axis_size("feat")
    xz = dom_size // CORES
    fr, vertices = features.shape
    hr = cotangent.shape[0]
    in_dim, hidden = self_weight.shape
    tile_count = tile_values.shape[0]
    nb = vertices // BLOCK
    vc = vertices // y_size
    tpq = (in_dim // 8) * (hidden // 128) // xz
    ext = 8 * tpq + 1
    dims = (
        dom_size,
        y_size,
        nb,
        tile_count,
        in_dim,
        hidden,
        1.0 / math.sqrt(vertices * dom_size),
    )
    hbm = pl.BlockSpec(memory_space=pl.ANY)
    dma = pltpu.SemaphoreType.DMA
    outs = pl.pallas_call(
        functools.partial(kernel, dims),
        out_shape=(
            jax.ShapeDtypeStruct((hr, vertices), BF16),
            jax.ShapeDtypeStruct((fr, vertices), BF16),
            jax.ShapeDtypeStruct((in_dim, hidden), F32),
            jax.ShapeDtypeStruct((in_dim, hidden), F32),
            jax.ShapeDtypeStruct((1, hidden), F32),
        ),
        in_specs=[hbm] * 9,
        out_specs=(hbm,) * 5,
        scratch_shapes=[
            pltpu.SMEM((tile_count,), jnp.int32),
            pltpu.SMEM((tile_count,), jnp.int32),
            pltpu.SMEM((1, 4, dom_size), jnp.int32),
            pltpu.SMEM((tile_count,), jnp.int32),
            pltpu.VMEM((fr, vertices), BF16),
            pltpu.VMEM((in_dim, hidden), F32),
            pltpu.VMEM((in_dim, hidden), F32),
            pltpu.VMEM((1, hidden), F32),
            pltpu.VMEM((fr, vertices), BF16),
            pltpu.VMEM((tile_count, BLOCK, BLOCK), BF16),
            pltpu.VMEM((in_dim, hidden), BF16),
            pltpu.VMEM((in_dim, hidden), BF16),
            pltpu.VMEM((y_size, 2, fr, hidden), BF16),
            pltpu.VMEM((hidden, 2 * in_dim), BF16),
            pltpu.VMEM((1, hidden), F32),
            pltpu.VMEM((hidden, 128), F32),
            pltpu.VMEM((y_size, 2, fr, vc), BF16),
            pltpu.VMEM((y_size, hr, vc), BF16),
            pltpu.VMEM((nb, fr, BLOCK), BF16),
            pltpu.VMEM((nb + 16, fr, BLOCK), BF16),
            pltpu.VMEM((4, 4, fr, BLOCK), BF16),
            pltpu.VMEM((y_size, fr, vc), BF16),
            pltpu.VMEM((y_size, hr, vc), BF16),
            pltpu.VMEM((y_size, 2 * fr, vc), BF16),
            pltpu.VMEM((y_size, 2 * fr, vc), BF16),
            pltpu.VMEM((nb, fr, BLOCK), BF16),
            pltpu.VMEM((tile_count, fr, BLOCK), F32),
            pltpu.VMEM((4, 4, fr, BLOCK), F32),
            pltpu.VMEM((4, 4, fr, BLOCK), F32),
            pltpu.VMEM((2, xz, ext, 128), F32),
            pltpu.VMEM((xz, ext, 128), F32),
            pltpu.VMEM((xz, ext, 128), F32),
            pltpu.VMEM((xz, ext, 128), F32),
            pltpu.VMEM((ext, 128), F32),
            pltpu.VMEM((y_size, ext, 128), F32),
            pltpu.VMEM((2, xz, 8 * tpq, 128), F32),
            pltpu.VMEM((2, 1, 128), F32),
            dma((8,)),
            dma((3,)),
            dma((2, 4)),
            dma((2, y_size - 1)),
            dma((2, y_size - 1)),
            dma((2, y_size - 1)),
            dma((2, y_size - 1)),
            dma((2, y_size - 1)),
            dma((2, 4)),
            dma((6,)),
            dma((2, xz - 1)),
            dma((2, y_size - 1)),
            dma((2, xz - 1)),
            dma((2, xz // X_SIZE)),
        ],
        compiler_params=pltpu.CompilerParams(
            collective_id=0, has_side_effects=True, vmem_limit_bytes=56 * 1024 * 1024
        ),
        name="graph_layer",
    )(
        tile_rows,
        tile_cols,
        send_blocks.transpose(0, 2, 1),
        features,
        self_weight,
        neigh_weight,
        bias_vector.reshape(1, hidden),
        tile_values,
        cotangent,
    )
    outs = pl.pallas_call(
        place,
        out_shape=tuple(jax.ShapeDtypeStruct(o.shape, o.dtype) for o in outs),
        in_specs=[hbm] * 5,
        out_specs=(hbm,) * 5,
        scratch_shapes=[dma((5,))],
        compiler_params=pltpu.CompilerParams(vmem_limit_bytes=56 * 1024 * 1024),
        name="place_outputs",
    )(*outs)
    activated, grad_features, grad_self, grad_neigh, grad_bias = outs
    return (activated, grad_features, grad_self, grad_neigh, grad_bias.reshape(hidden))


def solution(mesh):
    in_specs = (
        P("feat", "dom"),
        P(),
        P(),
        P(),
        P("dom", None, None),
        P("dom"),
        P("dom"),
        P("dom", None, None),
        P("feat", "dom"),
    )
    out_specs = (P("feat", "dom"), P("feat", "dom"), P(), P(), P())
    return jax.shard_map(local, mesh=mesh, in_specs=in_specs, out_specs=out_specs, check_vma=False)
```

```python
import functools
import math

import jax
import jax.numpy as jnp
from jax import lax
from jax.experimental import pallas as pl
from jax.experimental.pallas import tpu as pltpu
from jax.sharding import PartitionSpec as P

X_SIZE = 4
CORES = 2
BLOCK = 128
MESH = pl.DeviceIdType.MESH
F32 = jnp.float32
BF16 = jnp.bfloat16


def remote(src, dst, send_sem, recv_sem, device):
    return pltpu.make_async_remote_copy(
        src_ref=src,
        dst_ref=dst,
        send_sem=send_sem,
        recv_sem=recv_sem,
        device_id=device,
        device_id_type=MESH,
    )


def dot_nt(a, b):
    return lax.dot_general(a, b, (((1,), (1,)), ((), ())), preferred_element_type=F32)


def dot_nn(a, b):
    return lax.dot_general(a, b, (((1,), (0,)), ((), ())), preferred_element_type=F32)


def drain(ref, sem):
    pltpu.make_async_copy(ref, ref, sem).wait()


def one_hot(ids, nb, fr, base, out):
    rows = nb * fr
    per = 128 // fr
    lane = lax.broadcasted_iota(jnp.int32, (1, 128), 1)
    row = lax.broadcasted_iota(jnp.int32, (rows, 128), 0)
    for group in range(out.shape[1] // 128):
        key = jnp.zeros((1, 128), jnp.int32)
        for u in range(per):
            key = jnp.where(lane // fr == u, (ids[group * per + u] - base) * fr, key)
        key = key + lane % fr
        out[:, group * 128 : (group + 1) * 128] = jnp.where(row == key, 1.0, 0.0).astype(BF16)


def split(value):
    high = value.astype(BF16)
    return high, (value - high.astype(F32)).astype(BF16)


def kernel(
    dims,
    rows_in,
    cols_in,
    blocks_in,
    features,
    self_weight,
    neigh_weight,
    bias,
    tile_values,
    cotangent,
    activated,
    grad_features,
    grad_self,
    grad_neigh,
    grad_bias,
    tile_rows,
    tile_cols,
    send_blocks,
    slots,
    gf,
    gs,
    gn,
    gb,
    fv,
    tiles,
    w_self,
    w_neigh,
    w_cat,
    w_t,
    bias_row,
    bias_mat,
    xg,
    ct,
    own_tab,
    tab,
    stage,
    agg,
    act,
    bk,
    bkr,
    btab,
    prod,
    by_row,
    by_far,
    by_near,
    rb_send,
    rb_recv,
    part_own,
    part_send,
    part_recv,
    rs_src,
    rs_recv,
    y_src,
    y_recv,
    g_full,
    b_full,
    local_sem,
    send_sem,
    recv_sem,
    plane_sem,
):
    dom_size, y_size, nb, tile_count, in_dim, hidden, norm_scale = dims
    z_size = dom_size // (X_SIZE * CORES)
    xz = X_SIZE * z_size
    fr = in_dim // y_size
    hr = hidden // y_size
    vb = nb // y_size
    vc = vb * BLOCK
    tpq = (in_dim // 8) * (hidden // 128) // xz
    row_tiles = in_dim // 8
    others = y_size - 1

    dom = lax.axis_index("dom")
    fy = lax.axis_index("feat")
    core = lax.rem(dom, CORES)
    q = dom // CORES
    my_z = q // X_SIZE
    my_x = lax.rem(q, X_SIZE)

    offsets = (1, 2, dom_size - 1, dom_size // 2)
    y_peers = [lax.rem(fy + i, y_size) for i in range(1, y_size)]
    sibling = (q * CORES + 1 - core, fy)
    xz_peers = []
    for dz in range(z_size):
        for dx in range(X_SIZE):
            if dz or dx:
                pz = lax.rem(my_z + dz, z_size)
                px = lax.rem(my_x + dx, X_SIZE)
                xz_peers.append((dz, pz * X_SIZE + px))

    def columns(ref, y):
        return ref.at[:, pl.ds(pl.multiple_of(y * vc, vc), vc)]

    loads = [
        pltpu.make_async_copy(src, dst, local_sem.at[i])
        for i, (src, dst) in enumerate(
            (
                (blocks_in, send_blocks),
                (features, fv),
                (cols_in, tile_cols),
                (rows_in, tile_rows),
                (self_weight, w_self),
                (neigh_weight, w_neigh),
                (bias, bias_row),
                (tile_values, tiles),
            )
        )
    ]
    for copy in loads:
        copy.start()

    barrier = pltpu.get_barrier_semaphore()
    greet = [(dom, p) for p in y_peers]
    for off in (1, 2, dom_size - 1, dom_size - 2, dom_size // 2):
        greet.append((lax.rem(dom + off, dom_size), fy))
    greet.append(sibling)
    greet += [(p * CORES + core, fy) for _, p in xz_peers]
    for device in greet:
        pl.semaphore_signal(barrier, inc=1, device_id=device, device_id_type=MESH)

    loads[0].wait()
    owners = []
    for pos in range(4):
        to = lax.rem(dom + offsets[pos], dom_size)
        owners.append([send_blocks[0, c, to] for c in range(4)])
    loads[1].wait()
    for b in range(nb):
        own_tab[b] = fv[:, b * BLOCK : (b + 1) * BLOCK]
    for pos in range(4):
        for c in range(4):
            stage[pos, c] = own_tab[jnp.maximum(owners[pos][c], 0)]

    pl.semaphore_wait(barrier, len(greet))

    for pos in range(4):
        to = lax.rem(dom + offsets[pos], dom_size)
        remote(
            stage.at[pos],
            tab.at[pl.ds(nb + 4 * pos, 4)],
            send_sem.at[0],
            recv_sem.at[0],
            (to, fy),
        ).start()
    for p in y_peers:
        remote(columns(fv, p), xg.at[fy, 0], send_sem.at[1], recv_sem.at[1], (dom, p)).start()
    for p in y_peers:
        remote(columns(cotangent, p), ct.at[fy], send_sem.at[2], recv_sem.at[2], (dom, p)).start()
    own_cot = pltpu.make_async_copy(columns(cotangent, fy), ct.at[fy], local_sem.at[8])
    own_cot.start()
    xg[fy, 0] = fv[:, pl.ds(pl.multiple_of(fy * vc, vc), vc)]

    for copy in loads[2:]:
        copy.wait()

    def slot_body(t, carry):
        col = tile_cols[t]
        far = jnp.maximum(col - nb, 0)
        back = lax.rem(dom + dom_size - far // 4, dom_size)
        place = jnp.where(
            back == offsets[0],
            0,
            jnp.where(back == offsets[1], 1, jnp.where(back == offsets[2], 2, 3)),
        )
        slots[t] = jnp.where(col < nb, col, nb + place * 4 + lax.rem(far, 4))
        return carry

    lax.fori_loop(0, tile_count, slot_body, 0, unroll=4)
    for b in range(nb):
        tab[b] = fv[:, b * BLOCK : (b + 1) * BLOCK]
    one_hot(tile_rows, nb, fr, 0, by_row)

    drain(stage, recv_sem.at[0])

    def agg_body(t, carry):
        prod[t] = dot_nt(tab[slots[t]], tiles[t])
        return carry

    lax.fori_loop(0, tile_count, agg_body, 0, unroll=tile_count)
    high, low = split(prod[...].reshape(tile_count * fr, BLOCK))
    sums = (dot_nn(by_row[...], high) + dot_nn(by_row[...], low)).astype(BF16)
    for b in range(nb):
        agg[b // vb, :, (b % vb) * BLOCK : (b % vb + 1) * BLOCK] = sums[b * fr : (b + 1) * fr]
    for p in y_peers:
        remote(agg.at[p], xg.at[fy, 1], send_sem.at[3], recv_sem.at[3], (dom, p)).start()
    xg[fy, 1] = agg[fy]

    for y in range(y_size):
        w_cat[y, 0] = w_self[y * fr : (y + 1) * fr, :]
        w_cat[y, 1] = w_neigh[y * fr : (y + 1) * fr, :]
    weights = w_cat[...].reshape(2 * in_dim, hidden)
    w_t[...] = weights.astype(F32).T.astype(BF16)
    bias_mat[...] = jnp.broadcast_to(bias_row[...], (128, hidden)).T
    one_hot(slots, 16, fr, nb, by_far)
    one_hot(slots, nb, fr, 0, by_near)

    own_cot.wait()
    drain(xg.at[0:others, 0], recv_sem.at[1])
    drain(ct.at[0:others], recv_sem.at[2])
    drain(agg.at[0:others], recv_sem.at[3])

    both = xg[...].reshape(2 * in_dim, vc)
    pre = dot_nn(w_t[...], both) + jnp.concatenate([bias_mat[...]] * vb, axis=1)
    sigma = jax.nn.sigmoid(pre)
    cot = ct[...].reshape(hidden, vc).astype(F32)
    dpre = (cot * sigma * (1.0 + pre * (1.0 - sigma))).astype(BF16)

    bias_part = dot_nt(jnp.ones((16, vc), BF16), dpre)
    for kind, out in ((1 - core, part_send), (core, part_own)):
        grads = dot_nt(xg[:, kind].reshape(in_dim, vc), dpre)
        half = jnp.where(kind == 0, bias_part[0:1, 0:128], bias_part[0:1, 128:256])
        for rt in range(row_tiles):
            for c in range(2):
                n = rt * 2 + c
                out[n // tpq, (n % tpq) * 8 : (n % tpq + 1) * 8, :] = grads[
                    rt * 8 : (rt + 1) * 8, c * 128 : (c + 1) * 128
                ]
        for n in range(xz):
            out[n, 8 * tpq : 8 * tpq + 1, :] = half
        if out is part_send:
            swap = remote(part_send, part_recv, send_sem.at[4], recv_sem.at[4], sibling)
            swap.start()
    bk[...] = dot_nn(weights, dpre).astype(BF16).reshape(y_size, 2 * fr, vc)
    for p in y_peers:
        remote(bk.at[p], bkr.at[fy], send_sem.at[5], recv_sem.at[5], (dom, p)).start()
    bkr[fy] = bk[fy]
    act[...] = (pre * sigma).astype(BF16).reshape(y_size, hr, vc)

    swap.wait_recv()
    rs_src[...] = part_own[...] + part_recv[...]
    for _, p in xz_peers:
        remote(
            rs_src.at[p], rs_recv.at[q], send_sem.at[6], recv_sem.at[6], (p * CORES + core, fy)
        ).start()
    rs_recv[q] = rs_src[q]

    drain(bkr.at[0:others], recv_sem.at[5])
    for b in range(nb):
        btab[b] = bkr[b // vb, fr : 2 * fr, (b % vb) * BLOCK : (b % vb + 1) * BLOCK]

    def spread_body(t, carry):
        prod[t] = dot_nn(btab[tile_rows[t]], tiles[t])
        return carry

    lax.fori_loop(0, tile_count, spread_body, 0, unroll=tile_count)
    high, low = split(prod[...].reshape(tile_count * fr, BLOCK))
    sums = dot_nn(by_far[...], high) + dot_nn(by_far[...], low)
    for n in range(16):
        rb_send[n // 4, n % 4] = sums[n * fr : (n + 1) * fr]
    for pos in range(4):
        to = lax.rem(dom + dom_size - offsets[pos], dom_size)
        remote(
            rb_send.at[pos], rb_recv.at[pos], send_sem.at[7], recv_sem.at[7], (to, fy)
        ).start()

    drain(rs_recv.at[0 : xz - 1], recv_sem.at[6])
    total = rs_recv[0]
    for n in range(1, xz):
        total = total + rs_recv[n]
    y_src[...] = total
    y_recv[fy] = total
    for p in y_peers:
        remote(y_src, y_recv.at[fy], send_sem.at[8], recv_sem.at[8], (dom, p)).start()
    for p in y_peers:
        remote(
            act.at[p], columns(activated, fy), send_sem.at[9], recv_sem.at[9], (dom, p)
        ).start()
    own_act = pltpu.make_async_copy(act.at[fy], columns(activated, fy), local_sem.at[9])
    own_act.start()

    near = dot_nn(by_near[...], high) + dot_nn(by_near[...], low)

    drain(y_recv.at[0:others], recv_sem.at[8])
    total = y_recv[0]
    for n in range(1, y_size):
        total = total + y_recv[n]
    total = total * norm_scale
    g_full[core, q] = total[: 8 * tpq]
    b_full[core] = total[8 * tpq : 8 * tpq + 1]
    for dz, p in xz_peers:
        remote(
            g_full.at[core, q],
            g_full.at[core, q],
            send_sem.at[10],
            plane_sem.at[dz],
            (p * CORES + core, fy),
        ).start()
    bias_swap = remote(
        b_full.at[core], b_full.at[core], send_sem.at[11], recv_sem.at[9 + 1], sibling
    )
    bias_swap.start()

    drain(rb_recv, recv_sem.at[7])
    sums = [
        near[b * fr : (b + 1) * fr]
        + bkr[b // vb, 0:fr, (b % vb) * BLOCK : (b % vb + 1) * BLOCK].astype(F32)
        for b in range(nb)
    ]
    for pos in range(4):
        for c in range(4):
            term = rb_recv[pos, c]
            sums = [jnp.where(owners[pos][c] == b, v + term, v) for b, v in enumerate(sums)]
    for b in range(nb):
        gf[:, b * BLOCK : (b + 1) * BLOCK] = sums[b].astype(BF16)
    stores = [pltpu.make_async_copy(gf, grad_features, local_sem.at[0])]
    stores[0].start()

    for dz in range(z_size):
        drain(g_full.at[0, 0 : X_SIZE - (dz == 0)], plane_sem.at[dz])
        plane = pl.ds(lax.rem(my_z + z_size - dz, z_size) * X_SIZE, X_SIZE)
        remote(
            g_full.at[core, plane],
            g_full.at[core, plane],
            send_sem.at[12],
            recv_sem.at[11],
            sibling,
        ).start()
    bias_swap.wait_recv()
    for kind in range(2):
        gb[:, kind * 128 : (kind + 1) * 128] = b_full[kind]
    stores.append(pltpu.make_async_copy(gb, grad_bias, local_sem.at[1]))
    stores[1].start()
    drain(g_full.at[0], recv_sem.at[11])
    for kind, out, dst in ((0, gs, grad_self), (1, gn, grad_neigh)):
        for rt in range(row_tiles):
            for c in range(2):
                n = rt * 2 + c
                out[rt * 8 : (rt + 1) * 8, c * 128 : (c + 1) * 128] = g_full[
                    kind, n // tpq, (n % tpq) * 8 : (n % tpq + 1) * 8, :
                ]
        stores.append(pltpu.make_async_copy(out, dst, local_sem.at[2 + kind]))
        stores[-1].start()
    own_act.wait()
    drain(activated.at[:, 0 : others * vc], recv_sem.at[9])

    drain(stage, send_sem.at[0])
    drain(xg.at[0:others, 0], send_sem.at[1])
    drain(ct.at[0:others], send_sem.at[2])
    drain(agg.at[0:others], send_sem.at[3])
    swap.wait_send()
    drain(bkr.at[0:others], send_sem.at[5])
    drain(rs_recv.at[0 : xz - 1], send_sem.at[6])
    drain(rb_recv, send_sem.at[7])
    drain(y_recv.at[0:others], send_sem.at[8])
    drain(activated.at[:, 0 : others * vc], send_sem.at[9])
    drain(g_full.at[0, 0 : xz - 1], send_sem.at[10])
    bias_swap.wait_send()
    drain(g_full.at[0], send_sem.at[12])
    for copy in stores:
        copy.wait()


def place(*refs):
    count = len(refs) // 3
    sems = refs[-1]
    ins, outs, held = refs[:count], refs[count : 2 * count], refs[2 * count : 3 * count]
    first = [pltpu.make_async_copy(ins[i], held[i], sems.at[0, i]) for i in range(count)]
    second = [pltpu.make_async_copy(held[i], outs[i], sems.at[1, i]) for i in range(count)]
    for copy in first:
        copy.start()
    for a, b in zip(first, second):
        a.wait()
        b.start()
    for copy in second:
        copy.wait()


def local(
    features,
    self_weight,
    neigh_weight,
    bias_vector,
    tile_values,
    tile_rows,
    tile_cols,
    send_blocks,
    cotangent,
):
    dom_size = lax.axis_size("dom")
    y_size = lax.axis_size("feat")
    xz = dom_size // CORES
    fr, vertices = features.shape
    hr = cotangent.shape[0]
    in_dim, hidden = self_weight.shape
    tile_count = tile_values.shape[0]
    nb = vertices // BLOCK
    vc = vertices // y_size
    tpq = (in_dim // 8) * (hidden // 128) // xz
    ext = 8 * tpq + 1
    dims = (
        dom_size,
        y_size,
        nb,
        tile_count,
        in_dim,
        hidden,
        1.0 / math.sqrt(vertices * dom_size),
    )
    hbm = pl.BlockSpec(memory_space=pl.ANY)
    dma = pltpu.SemaphoreType.DMA
    outs = pl.pallas_call(
        functools.partial(kernel, dims),
        out_shape=(
            jax.ShapeDtypeStruct((hr, vertices), BF16),
            jax.ShapeDtypeStruct((fr, vertices), BF16),
            jax.ShapeDtypeStruct((in_dim, hidden), F32),
            jax.ShapeDtypeStruct((in_dim, hidden), F32),
            jax.ShapeDtypeStruct((1, hidden), F32),
        ),
        in_specs=[hbm] * 9,
        out_specs=(hbm,) * 5,
        scratch_shapes=[
            pltpu.SMEM((tile_count,), jnp.int32),
            pltpu.SMEM((tile_count,), jnp.int32),
            pltpu.SMEM((1, 4, dom_size), jnp.int32),
            pltpu.SMEM((tile_count,), jnp.int32),
            pltpu.VMEM((fr, vertices), BF16),
            pltpu.VMEM((in_dim, hidden), F32),
            pltpu.VMEM((in_dim, hidden), F32),
            pltpu.VMEM((1, hidden), F32),
            pltpu.VMEM((fr, vertices), BF16),
            pltpu.VMEM((tile_count, BLOCK, BLOCK), BF16),
            pltpu.VMEM((in_dim, hidden), BF16),
            pltpu.VMEM((in_dim, hidden), BF16),
            pltpu.VMEM((y_size, 2, fr, hidden), BF16),
            pltpu.VMEM((hidden, 2 * in_dim), BF16),
            pltpu.VMEM((1, hidden), F32),
            pltpu.VMEM((hidden, 128), F32),
            pltpu.VMEM((y_size, 2, fr, vc), BF16),
            pltpu.VMEM((y_size, hr, vc), BF16),
            pltpu.VMEM((nb, fr, BLOCK), BF16),
            pltpu.VMEM((nb + 16, fr, BLOCK), BF16),
            pltpu.VMEM((4, 4, fr, BLOCK), BF16),
            pltpu.VMEM((y_size, fr, vc), BF16),
            pltpu.VMEM((y_size, hr, vc), BF16),
            pltpu.VMEM((y_size, 2 * fr, vc), BF16),
            pltpu.VMEM((y_size, 2 * fr, vc), BF16),
            pltpu.VMEM((nb, fr, BLOCK), BF16),
            pltpu.VMEM((tile_count, fr, BLOCK), F32),
            pltpu.VMEM((nb * fr, tile_count * fr), BF16),
            pltpu.VMEM((16 * fr, tile_count * fr), BF16),
            pltpu.VMEM((nb * fr, tile_count * fr), BF16),
            pltpu.VMEM((4, 4, fr, BLOCK), F32),
            pltpu.VMEM((4, 4, fr, BLOCK), F32),
            pltpu.VMEM((xz, ext, 128), F32),
            pltpu.VMEM((xz, ext, 128), F32),
            pltpu.VMEM((xz, ext, 128), F32),
            pltpu.VMEM((xz, ext, 128), F32),
            pltpu.VMEM((xz, ext, 128), F32),
            pltpu.VMEM((ext, 128), F32),
            pltpu.VMEM((y_size, ext, 128), F32),
            pltpu.VMEM((2, xz, 8 * tpq, 128), F32),
            pltpu.VMEM((2, 1, 128), F32),
            dma((10,)),
            dma((13,)),
            dma((12,)),
            dma((xz // X_SIZE,)),
        ],
        compiler_params=pltpu.CompilerParams(
            collective_id=0, has_side_effects=True, vmem_limit_bytes=56 * 1024 * 1024
        ),
        name="graph_layer",
    )(
        tile_rows,
        tile_cols,
        send_blocks.transpose(0, 2, 1),
        features,
        self_weight,
        neigh_weight,
        bias_vector.reshape(1, hidden),
        tile_values,
        cotangent,
    )
    outs = pl.pallas_call(
        place,
        out_shape=tuple(jax.ShapeDtypeStruct(o.shape, o.dtype) for o in outs),
        in_specs=[hbm] * 5,
        out_specs=(hbm,) * 5,
        scratch_shapes=[pltpu.VMEM(o.shape, o.dtype) for o in outs] + [dma((2, 5))],
        compiler_params=pltpu.CompilerParams(vmem_limit_bytes=56 * 1024 * 1024),
        name="place_outputs",
    )(*outs)
    activated, grad_features, grad_self, grad_neigh, grad_bias = outs
    return (activated, grad_features, grad_self, grad_neigh, grad_bias.reshape(hidden))


def solution(mesh):
    in_specs = (
        P("feat", "dom"),
        P(),
        P(),
        P(),
        P("dom", None, None),
        P("dom"),
        P("dom"),
        P("dom", None, None),
        P("feat", "dom"),
    )
    out_specs = (P("feat", "dom"), P("feat", "dom"), P(), P(), P())
    return jax.shard_map(local, mesh=mesh, in_specs=in_specs, out_specs=out_specs, check_vma=False)
```

```python
import functools
import math

import jax
import jax.numpy as jnp
from jax import lax
from jax.experimental import pallas as pl
from jax.experimental.pallas import tpu as pltpu
from jax.sharding import PartitionSpec as P

X_SIZE = 4
CORES = 2
BLOCK = 128
MESH = pl.DeviceIdType.MESH
F32 = jnp.float32
BF16 = jnp.bfloat16


def remote(src, dst, send_sem, recv_sem, device):
    return pltpu.make_async_remote_copy(
        src_ref=src,
        dst_ref=dst,
        send_sem=send_sem,
        recv_sem=recv_sem,
        device_id=device,
        device_id_type=MESH,
    )


def dot_nt(a, b):
    return lax.dot_general(a, b, (((1,), (1,)), ((), ())), preferred_element_type=F32)


def dot_nn(a, b):
    return lax.dot_general(a, b, (((1,), (0,)), ((), ())), preferred_element_type=F32)


def ring(step, size):
    return min(step, size - step)


def drain(ref, sem):
    pltpu.make_async_copy(ref, ref, sem).wait()


def one_hot(ids, nb, fr, base, out):
    rows = nb * fr
    per = 128 // fr
    lane = lax.broadcasted_iota(jnp.int32, (1, 128), 1)
    row = lax.broadcasted_iota(jnp.int32, (rows, 128), 0)
    for group in range(out.shape[1] // 128):
        key = jnp.zeros((1, 128), jnp.int32)
        for u in range(per):
            key = jnp.where(lane // fr == u, (ids[group * per + u] - base) * fr, key)
        key = key + lane % fr
        out[:, group * 128 : (group + 1) * 128] = jnp.where(row == key, 1.0, 0.0).astype(BF16)


def split(value):
    high = value.astype(BF16)
    return high, (value - high.astype(F32)).astype(BF16)


def kernel(
    dims,
    rows_in,
    cols_in,
    blocks_in,
    features,
    self_weight,
    neigh_weight,
    bias,
    tile_values,
    cotangent,
    activated,
    grad_features,
    grad_tiles,
    grad_bias,
    tile_rows,
    tile_cols,
    send_blocks,
    slots,
    gf,
    gb,
    fv,
    tiles,
    w_self,
    w_neigh,
    wt_self,
    wt_neigh,
    bias_row,
    bias_mat,
    xg,
    pre_self,
    ct,
    own_tab,
    tab,
    stage,
    agg,
    act,
    bk,
    bkr,
    btab,
    prod,
    by_row,
    by_far,
    by_near,
    rb_send,
    rb_recv,
    part_own,
    part_send,
    part_recv,
    rs_src,
    rs_recv,
    y_src,
    y_recv,
    g_half,
    b_full,
    local_sem,
    send_sem,
    recv_sem,
    plane_sem,
):
    dom_size, y_size, nb, tile_count, in_dim, hidden, norm_scale = dims
    z_size = dom_size // (X_SIZE * CORES)
    xz = X_SIZE * z_size
    fr = in_dim // y_size
    hr = hidden // y_size
    vb = nb // y_size
    vc = vb * BLOCK
    tpq = (in_dim // 8) * (hidden // 128) // xz
    row_tiles = in_dim // 8
    others = y_size - 1

    dom = lax.axis_index("dom")
    fy = lax.axis_index("feat")
    core = lax.rem(dom, CORES)
    q = dom // CORES
    my_z = q // X_SIZE
    my_x = lax.rem(q, X_SIZE)

    offsets = (1, 2, dom_size - 1, dom_size // 2)
    y_steps = sorted(range(1, y_size), key=lambda d: -ring(d, y_size))
    y_peers = [lax.rem(fy + d, y_size) for d in y_steps]
    sibling = (q * CORES + 1 - core, fy)
    xz_steps = [(dz, dx) for dz in range(z_size) for dx in range(X_SIZE) if dz or dx]
    xz_steps.sort(key=lambda d: -ring(d[0], z_size) - ring(d[1], X_SIZE))
    xz_peers = [
        (dz, lax.rem(my_z + dz, z_size) * X_SIZE + lax.rem(my_x + dx, X_SIZE))
        for dz, dx in xz_steps
    ]

    def columns(ref, y):
        return ref.at[:, pl.ds(pl.multiple_of(y * vc, vc), vc)]

    loads = [
        pltpu.make_async_copy(src, dst, local_sem.at[i])
        for i, (src, dst) in enumerate(
            (
                (blocks_in, send_blocks),
                (features, fv),
                (cols_in, tile_cols),
                (rows_in, tile_rows),
                (self_weight, w_self),
                (neigh_weight, w_neigh),
                (bias, bias_row),
                (tile_values, tiles),
            )
        )
    ]
    for copy in loads:
        copy.start()

    barrier = pltpu.get_barrier_semaphore()
    greet = [(p * CORES + core, fy) for _, p in xz_peers]
    greet += [(dom, p) for p in y_peers]
    for off in (dom_size // 2, 1, 2, dom_size - 1, dom_size - 2):
        greet.append((lax.rem(dom + off, dom_size), fy))
    greet.append(sibling)
    for device in greet:
        pl.semaphore_signal(barrier, inc=1, device_id=device, device_id_type=MESH)

    loads[0].wait()
    owners = []
    for pos in range(4):
        to = lax.rem(dom + offsets[pos], dom_size)
        owners.append([send_blocks[0, c, to] for c in range(4)])
    loads[1].wait()
    for b in range(nb):
        own_tab[b] = fv[:, b * BLOCK : (b + 1) * BLOCK]
    for pos in range(4):
        for c in range(4):
            stage[pos, c] = own_tab[jnp.maximum(owners[pos][c], 0)]

    pl.semaphore_wait(barrier, len(greet))

    for pos in (3, 1, 0, 2):
        to = lax.rem(dom + offsets[pos], dom_size)
        remote(
            stage.at[pos],
            tab.at[pl.ds(nb + 4 * pos, 4)],
            send_sem.at[0],
            recv_sem.at[0],
            (to, fy),
        ).start()
    for p in y_peers:
        remote(columns(fv, p), xg.at[0, fy], send_sem.at[1], recv_sem.at[1], (dom, p)).start()
    for p in y_peers:
        remote(columns(cotangent, p), ct.at[fy], send_sem.at[2], recv_sem.at[2], (dom, p)).start()
    own_cot = pltpu.make_async_copy(columns(cotangent, fy), ct.at[fy], local_sem.at[8])
    own_cot.start()
    xg[0, fy] = fv[:, pl.ds(pl.multiple_of(fy * vc, vc), vc)]

    for copy in loads[2:]:
        copy.wait()

    def slot_body(t, carry):
        col = tile_cols[t]
        far = jnp.maximum(col - nb, 0)
        back = lax.rem(dom + dom_size - far // 4, dom_size)
        place = jnp.where(
            back == offsets[0],
            0,
            jnp.where(back == offsets[1], 1, jnp.where(back == offsets[2], 2, 3)),
        )
        slots[t] = jnp.where(col < nb, col, nb + place * 4 + lax.rem(far, 4))
        return carry

    lax.fori_loop(0, tile_count, slot_body, 0, unroll=4)
    for b in range(nb):
        tab[b] = fv[:, b * BLOCK : (b + 1) * BLOCK]
    one_hot(tile_rows, nb, fr, 0, by_row)

    drain(stage, recv_sem.at[0])

    def agg_body(t, carry):
        prod[t] = dot_nt(tab[slots[t]], tiles[t])
        return carry

    lax.fori_loop(0, tile_count, agg_body, 0, unroll=tile_count)
    high, low = split(prod[...].reshape(tile_count * fr, BLOCK))
    sums = (dot_nn(by_row[...], high) + dot_nn(by_row[...], low)).astype(BF16)
    for b in range(nb):
        agg[b // vb, :, (b % vb) * BLOCK : (b % vb + 1) * BLOCK] = sums[b * fr : (b + 1) * fr]
    for p in y_peers:
        remote(agg.at[p], xg.at[1, fy], send_sem.at[3], recv_sem.at[3], (dom, p)).start()
    xg[1, fy] = agg[fy]

    for src, dst in ((w_self, wt_self), (w_neigh, wt_neigh)):
        dst[...] = src[...].astype(F32).T.astype(BF16)
    bias_mat[...] = jnp.broadcast_to(bias_row[...], (128, hidden)).T
    one_hot(slots, 16, fr, nb, by_far)
    one_hot(slots, nb, fr, 0, by_near)

    drain(xg.at[0, 0:others], recv_sem.at[1])
    early = dot_nn(wt_self[...], xg[0].reshape(in_dim, vc))
    pre_self[...] = early + jnp.concatenate([bias_mat[...]] * vb, axis=1)
    own_cot.wait()
    drain(ct.at[0:others], recv_sem.at[2])
    drain(agg.at[0:others], recv_sem.at[3])
    pre = pre_self[...] + dot_nn(wt_neigh[...], xg[1].reshape(in_dim, vc))
    sigma = jax.nn.sigmoid(pre)
    cot = ct[...].reshape(hidden, vc).astype(F32)
    dpre = (cot * sigma * (1.0 + pre * (1.0 - sigma))).astype(BF16)

    bias_part = dot_nt(jnp.ones((16, vc), BF16), dpre)
    for kind, out in ((1 - core, part_send), (core, part_own)):
        grads = dot_nt(xg[kind].reshape(in_dim, vc), dpre)
        half = jnp.where(kind == 0, bias_part[0:1, 0:128], bias_part[0:1, 128:256])
        for rt in range(row_tiles):
            for c in range(2):
                n = rt * 2 + c
                out[n // tpq, (n % tpq) * 8 : (n % tpq + 1) * 8, :] = grads[
                    rt * 8 : (rt + 1) * 8, c * 128 : (c + 1) * 128
                ]
        for n in range(xz):
            out[n, 8 * tpq : 8 * tpq + 1, :] = half
        if out is part_send:
            swap = remote(part_send, part_recv, send_sem.at[4], recv_sem.at[4], sibling)
            swap.start()
    bk[:, 0:fr] = dot_nn(w_self[...], dpre).astype(BF16).reshape(y_size, fr, vc)
    bk[:, fr : 2 * fr] = dot_nn(w_neigh[...], dpre).astype(BF16).reshape(y_size, fr, vc)
    for p in y_peers:
        remote(bk.at[p], bkr.at[fy], send_sem.at[5], recv_sem.at[5], (dom, p)).start()
    bkr[fy] = bk[fy]
    act[...] = (pre * sigma).astype(BF16).reshape(y_size, hr, vc)

    swap.wait_recv()
    rs_src[...] = part_own[...] + part_recv[...]
    for _, p in xz_peers:
        remote(
            rs_src.at[p], rs_recv.at[q], send_sem.at[6], recv_sem.at[6], (p * CORES + core, fy)
        ).start()
    rs_recv[q] = rs_src[q]

    drain(bkr.at[0:others], recv_sem.at[5])
    for b in range(nb):
        btab[b] = bkr[b // vb, fr : 2 * fr, (b % vb) * BLOCK : (b % vb + 1) * BLOCK]

    def spread_body(t, carry):
        prod[t] = dot_nn(btab[tile_rows[t]], tiles[t])
        return carry

    lax.fori_loop(0, tile_count, spread_body, 0, unroll=tile_count)
    high, low = split(prod[...].reshape(tile_count * fr, BLOCK))
    sums = dot_nn(by_far[...], high) + dot_nn(by_far[...], low)
    for n in range(16):
        rb_send[n // 4, n % 4] = sums[n * fr : (n + 1) * fr]
    for pos in (3, 1, 0, 2):
        to = lax.rem(dom + dom_size - offsets[pos], dom_size)
        remote(
            rb_send.at[pos], rb_recv.at[pos], send_sem.at[7], recv_sem.at[7], (to, fy)
        ).start()

    drain(rs_recv.at[0 : xz - 1], recv_sem.at[6])
    total = rs_recv[0]
    for n in range(1, xz):
        total = total + rs_recv[n]
    y_src[...] = total
    y_recv[fy] = total
    for p in y_peers:
        remote(y_src, y_recv.at[fy], send_sem.at[8], recv_sem.at[8], (dom, p)).start()
    for p in y_peers:
        remote(
            act.at[p], columns(activated, fy), send_sem.at[9], recv_sem.at[9], (dom, p)
        ).start()
    own_act = pltpu.make_async_copy(act.at[fy], columns(activated, fy), local_sem.at[9])
    own_act.start()

    near = dot_nn(by_near[...], high) + dot_nn(by_near[...], low)

    drain(y_recv.at[0:others], recv_sem.at[8])
    total = y_recv[0]
    for n in range(1, y_size):
        total = total + y_recv[n]
    total = total * norm_scale
    g_half[q] = total[: 8 * tpq]
    b_full[core] = total[8 * tpq : 8 * tpq + 1]
    for dz, p in xz_peers:
        remote(
            g_half.at[q],
            g_half.at[q],
            send_sem.at[10],
            plane_sem.at[dz],
            (p * CORES + core, fy),
        ).start()
    bias_swap = remote(
        b_full.at[core], b_full.at[core], send_sem.at[11], recv_sem.at[9 + 1], sibling
    )
    bias_swap.start()

    drain(rb_recv, recv_sem.at[7])
    sums = [
        near[b * fr : (b + 1) * fr]
        + bkr[b // vb, 0:fr, (b % vb) * BLOCK : (b % vb + 1) * BLOCK].astype(F32)
        for b in range(nb)
    ]
    for pos in range(4):
        for c in range(4):
            term = rb_recv[pos, c]
            sums = [jnp.where(owners[pos][c] == b, v + term, v) for b, v in enumerate(sums)]
    for b in range(nb):
        gf[:, b * BLOCK : (b + 1) * BLOCK] = sums[b].astype(BF16)
    stores = [pltpu.make_async_copy(gf, grad_features, local_sem.at[0])]
    stores[0].start()

    bias_swap.wait_recv()
    for kind in range(2):
        gb[:, kind * 128 : (kind + 1) * 128] = b_full[kind]
    stores.append(pltpu.make_async_copy(gb, grad_bias, local_sem.at[1]))
    stores[1].start()

    for dz in sorted(range(z_size), key=lambda d: ring(d, z_size)):
        drain(g_half.at[0 : X_SIZE - (dz == 0)], plane_sem.at[dz])
        plane = pl.ds(lax.rem(my_z + z_size - dz, z_size) * X_SIZE, X_SIZE)
        remote(
            g_half.at[plane],
            grad_tiles.at[core, plane],
            send_sem.at[12],
            recv_sem.at[11],
            sibling,
        ).start()
    stores.append(pltpu.make_async_copy(g_half, grad_tiles.at[core], local_sem.at[2]))
    stores[2].start()
    own_act.wait()
    drain(activated.at[:, 0 : others * vc], recv_sem.at[9])
    drain(g_half, recv_sem.at[11])

    drain(stage, send_sem.at[0])
    drain(xg.at[0, 0:others], send_sem.at[1])
    drain(ct.at[0:others], send_sem.at[2])
    drain(agg.at[0:others], send_sem.at[3])
    swap.wait_send()
    drain(bkr.at[0:others], send_sem.at[5])
    drain(rs_recv.at[0 : xz - 1], send_sem.at[6])
    drain(rb_recv, send_sem.at[7])
    drain(y_recv.at[0:others], send_sem.at[8])
    drain(activated.at[:, 0 : others * vc], send_sem.at[9])
    drain(g_half.at[0 : xz - 1], send_sem.at[10])
    bias_swap.wait_send()
    drain(g_half, send_sem.at[12])
    for copy in stores:
        copy.wait()


def place(*refs):
    ins, outs, held, (gs, gn, sems) = refs[0:4], refs[4:9], refs[9:13], refs[13:16]
    first = [pltpu.make_async_copy(ins[i], held[i], sems.at[0, i]) for i in range(4)]
    ready = (held[0], held[1], gs, gn, held[3])
    second = [pltpu.make_async_copy(ready[i], outs[i], sems.at[1, i]) for i in range(5)]
    for copy in first:
        copy.start()
    first[2].wait()
    tiles = held[2]
    rows = tiles.shape[2]
    for kind, out in ((0, gs), (1, gn)):
        for n in range(2 * out.shape[0] // 8):
            rt, c, part = n // 2, n % 2, (n % (rows // 8)) * 8
            out[rt * 8 : (rt + 1) * 8, c * 128 : (c + 1) * 128] = tiles[
                kind, n // (rows // 8), part : part + 8, :
            ]
        second[2 + kind].start()
    for i, o in ((0, 0), (1, 1), (3, 4)):
        first[i].wait()
        second[o].start()
    for copy in second:
        copy.wait()


def local(
    features,
    self_weight,
    neigh_weight,
    bias_vector,
    tile_values,
    tile_rows,
    tile_cols,
    send_blocks,
    cotangent,
):
    dom_size = lax.axis_size("dom")
    y_size = lax.axis_size("feat")
    xz = dom_size // CORES
    fr, vertices = features.shape
    hr = cotangent.shape[0]
    in_dim, hidden = self_weight.shape
    tile_count = tile_values.shape[0]
    nb = vertices // BLOCK
    vc = vertices // y_size
    tpq = (in_dim // 8) * (hidden // 128) // xz
    ext = 8 * tpq + 1
    dims = (
        dom_size,
        y_size,
        nb,
        tile_count,
        in_dim,
        hidden,
        1.0 / math.sqrt(vertices * dom_size),
    )
    hbm = pl.BlockSpec(memory_space=pl.ANY)
    dma = pltpu.SemaphoreType.DMA
    outs = pl.pallas_call(
        functools.partial(kernel, dims),
        out_shape=(
            jax.ShapeDtypeStruct((hr, vertices), BF16),
            jax.ShapeDtypeStruct((fr, vertices), BF16),
            jax.ShapeDtypeStruct((2, xz, 8 * tpq, 128), F32),
            jax.ShapeDtypeStruct((1, hidden), F32),
        ),
        in_specs=[hbm] * 9,
        out_specs=(hbm,) * 4,
        scratch_shapes=[
            pltpu.SMEM((tile_count,), jnp.int32),
            pltpu.SMEM((tile_count,), jnp.int32),
            pltpu.SMEM((1, 4, dom_size), jnp.int32),
            pltpu.SMEM((tile_count,), jnp.int32),
            pltpu.VMEM((fr, vertices), BF16),
            pltpu.VMEM((1, hidden), F32),
            pltpu.VMEM((fr, vertices), BF16),
            pltpu.VMEM((tile_count, BLOCK, BLOCK), BF16),
            pltpu.VMEM((in_dim, hidden), BF16),
            pltpu.VMEM((in_dim, hidden), BF16),
            pltpu.VMEM((hidden, in_dim), BF16),
            pltpu.VMEM((hidden, in_dim), BF16),
            pltpu.VMEM((1, hidden), F32),
            pltpu.VMEM((hidden, 128), F32),
            pltpu.VMEM((2, y_size, fr, vc), BF16),
            pltpu.VMEM((hidden, vc), F32),
            pltpu.VMEM((y_size, hr, vc), BF16),
            pltpu.VMEM((nb, fr, BLOCK), BF16),
            pltpu.VMEM((nb + 16, fr, BLOCK), BF16),
            pltpu.VMEM((4, 4, fr, BLOCK), BF16),
            pltpu.VMEM((y_size, fr, vc), BF16),
            pltpu.VMEM((y_size, hr, vc), BF16),
            pltpu.VMEM((y_size, 2 * fr, vc), BF16),
            pltpu.VMEM((y_size, 2 * fr, vc), BF16),
            pltpu.VMEM((nb, fr, BLOCK), BF16),
            pltpu.VMEM((tile_count, fr, BLOCK), F32),
            pltpu.VMEM((nb * fr, tile_count * fr), BF16),
            pltpu.VMEM((16 * fr, tile_count * fr), BF16),
            pltpu.VMEM((nb * fr, tile_count * fr), BF16),
            pltpu.VMEM((4, 4, fr, BLOCK), F32),
            pltpu.VMEM((4, 4, fr, BLOCK), F32),
            pltpu.VMEM((xz, ext, 128), F32),
            pltpu.VMEM((xz, ext, 128), F32),
            pltpu.VMEM((xz, ext, 128), F32),
            pltpu.VMEM((xz, ext, 128), F32),
            pltpu.VMEM((xz, ext, 128), F32),
            pltpu.VMEM((ext, 128), F32),
            pltpu.VMEM((y_size, ext, 128), F32),
            pltpu.VMEM((xz, 8 * tpq, 128), F32),
            pltpu.VMEM((2, 1, 128), F32),
            dma((10,)),
            dma((13,)),
            dma((12,)),
            dma((xz // X_SIZE,)),
        ],
        compiler_params=pltpu.CompilerParams(
            collective_id=0, has_side_effects=True, vmem_limit_bytes=56 * 1024 * 1024
        ),
        name="graph_layer",
    )(
        tile_rows,
        tile_cols,
        send_blocks.transpose(0, 2, 1),
        features,
        self_weight,
        neigh_weight,
        bias_vector.reshape(1, hidden),
        tile_values,
        cotangent,
    )
    weight = jax.ShapeDtypeStruct((in_dim, hidden), F32)
    outs = pl.pallas_call(
        place,
        out_shape=(
            jax.ShapeDtypeStruct((hr, vertices), BF16),
            jax.ShapeDtypeStruct((fr, vertices), BF16),
            weight,
            weight,
            jax.ShapeDtypeStruct((1, hidden), F32),
        ),
        in_specs=[hbm] * 4,
        out_specs=(hbm,) * 5,
        scratch_shapes=[pltpu.VMEM(o.shape, o.dtype) for o in outs]
        + [pltpu.VMEM((in_dim, hidden), F32)] * 2
        + [dma((2, 5))],
        compiler_params=pltpu.CompilerParams(vmem_limit_bytes=56 * 1024 * 1024),
        name="place_outputs",
    )(*outs)
    activated, grad_features, grad_self, grad_neigh, grad_bias = outs
    return (activated, grad_features, grad_self, grad_neigh, grad_bias.reshape(hidden))


def solution(mesh):
    in_specs = (
        P("feat", "dom"),
        P(),
        P(),
        P(),
        P("dom", None, None),
        P("dom"),
        P("dom"),
        P("dom", None, None),
        P("feat", "dom"),
    )
    out_specs = (P("feat", "dom"), P("feat", "dom"), P(), P(), P())
    return jax.shard_map(local, mesh=mesh, in_specs=in_specs, out_specs=out_specs, check_vma=False)
```

```python
import functools
import math

import jax
import jax.numpy as jnp
from jax import lax
from jax.experimental import pallas as pl
from jax.experimental.pallas import tpu as pltpu
from jax.sharding import PartitionSpec as P

X_SIZE = 4
CORES = 2
BLOCK = 128
MESH = pl.DeviceIdType.MESH
F32 = jnp.float32
BF16 = jnp.bfloat16


def remote(src, dst, send_sem, recv_sem, device):
    return pltpu.make_async_remote_copy(
        src_ref=src,
        dst_ref=dst,
        send_sem=send_sem,
        recv_sem=recv_sem,
        device_id=device,
        device_id_type=MESH,
    )


def dot_nt(a, b):
    return lax.dot_general(a, b, (((1,), (1,)), ((), ())), preferred_element_type=F32)


def dot_nn(a, b):
    return lax.dot_general(a, b, (((1,), (0,)), ((), ())), preferred_element_type=F32)


def ring(step, size):
    return min(step, size - step)


def drain(ref, sem):
    pltpu.make_async_copy(ref, ref, sem).wait()


def one_hot(ids, nb, fr, base, out):
    rows = nb * fr
    per = 128 // fr
    lane = lax.broadcasted_iota(jnp.int32, (1, 128), 1)
    row = lax.broadcasted_iota(jnp.int32, (rows, 128), 0)
    for group in range(out.shape[1] // 128):
        key = jnp.zeros((1, 128), jnp.int32)
        for u in range(per):
            key = jnp.where(lane // fr == u, (ids[group * per + u] - base) * fr, key)
        key = key + lane % fr
        out[:, group * 128 : (group + 1) * 128] = jnp.where(row == key, 1.0, 0.0).astype(BF16)


def split(value):
    high = value.astype(BF16)
    return jnp.concatenate([high, (value - high.astype(F32)).astype(BF16)], axis=1)


def added(one_hots, parts):
    both = dot_nn(one_hots[...], parts[...].reshape(one_hots.shape[1], 2 * BLOCK))
    return both[:, :BLOCK] + both[:, BLOCK:]


def kernel(
    dims,
    rows_in,
    cols_in,
    blocks_in,
    features,
    self_weight,
    neigh_weight,
    bias,
    tile_values,
    cotangent,
    activated,
    grad_features,
    grad_tiles,
    grad_bias,
    tile_rows,
    tile_cols,
    send_blocks,
    slots,
    gf,
    gb,
    fv,
    tiles,
    w_self,
    w_neigh,
    wt_self,
    wt_neigh,
    bias_row,
    bias_mat,
    xg,
    pre_self,
    ct,
    own_tab,
    tab,
    stage,
    agg,
    act,
    bk,
    bkr,
    btab,
    prod,
    by_row,
    by_far,
    by_near,
    rb_send,
    rb_recv,
    part_own,
    part_send,
    part_recv,
    rs_src,
    rs_recv,
    y_src,
    y_recv,
    g_half,
    b_full,
    z_sem,
    local_sem,
    send_sem,
    recv_sem,
    plane_sem,
):
    dom_size, y_size, nb, tile_count, in_dim, hidden, norm_scale = dims
    z_size = dom_size // (X_SIZE * CORES)
    xz = X_SIZE * z_size
    fr = in_dim // y_size
    hr = hidden // y_size
    vb = nb // y_size
    vc = vb * BLOCK
    tpq = (in_dim // 8) * (hidden // 128) // xz
    row_tiles = in_dim // 8
    others = y_size - 1

    dom = lax.axis_index("dom")
    fy = lax.axis_index("feat")
    core = lax.rem(dom, CORES)
    q = dom // CORES
    my_z = q // X_SIZE
    my_x = lax.rem(q, X_SIZE)

    offsets = (1, 2, dom_size - 1, dom_size // 2)
    y_steps = sorted(range(1, y_size), key=lambda d: -ring(d, y_size))
    y_peers = [lax.rem(fy + d, y_size) for d in y_steps]
    sibling = (q * CORES + 1 - core, fy)
    xz_steps = [(dz, dx) for dz in range(z_size) for dx in range(X_SIZE) if dz or dx]
    xz_steps.sort(key=lambda d: -ring(d[0], z_size) - ring(d[1], X_SIZE))
    xz_peers = [
        (dz, lax.rem(my_z + dz, z_size) * X_SIZE + lax.rem(my_x + dx, X_SIZE))
        for dz, dx in xz_steps
    ]

    def columns(ref, y):
        return ref.at[:, pl.ds(pl.multiple_of(y * vc, vc), vc)]

    loads = [
        pltpu.make_async_copy(src, dst, local_sem.at[i])
        for i, (src, dst) in enumerate(
            (
                (blocks_in, send_blocks),
                (features, fv),
                (cols_in, tile_cols),
                (rows_in, tile_rows),
                (self_weight, w_self),
                (neigh_weight, w_neigh),
                (bias, bias_row),
                (tile_values, tiles),
            )
        )
    ]
    barrier = pltpu.get_barrier_semaphore()
    z_peers = [
        ((lax.rem(my_z + d, z_size) * X_SIZE + my_x) * CORES + core, fy)
        for d in sorted(range(1, z_size), key=lambda d: -ring(d, z_size))
    ]
    greet = z_peers + [(dom, p) for p in y_peers]
    for off in (1, dom_size - 1, 2, dom_size - 2):
        greet.append((lax.rem(dom + off, dom_size), fy))
    for d in range(1, X_SIZE):
        greet.append(((my_z * X_SIZE + lax.rem(my_x + d, X_SIZE)) * CORES + core, fy))
    greet.append(sibling)
    for device in greet:
        pl.semaphore_signal(barrier, inc=1, device_id=device, device_id_type=MESH)
    for copy in loads:
        copy.start()

    loads[0].wait()
    owners = []
    for pos in range(4):
        to = lax.rem(dom + offsets[pos], dom_size)
        owners.append([send_blocks[0, c, to] for c in range(4)])
    loads[1].wait()
    for b in range(nb):
        own_tab[b] = fv[:, b * BLOCK : (b + 1) * BLOCK]
    for pos in range(4):
        for c in range(4):
            stage[pos, c] = own_tab[jnp.maximum(owners[pos][c], 0)]

    pl.semaphore_wait(barrier, len(greet))

    for pos in (3, 1, 0, 2):
        to = lax.rem(dom + offsets[pos], dom_size)
        remote(
            stage.at[pos],
            tab.at[pl.ds(nb + 4 * pos, 4)],
            send_sem.at[0],
            recv_sem.at[0],
            (to, fy),
        ).start()
    for p in y_peers:
        remote(columns(fv, p), xg.at[0, fy], send_sem.at[1], recv_sem.at[1], (dom, p)).start()
    for p in y_peers:
        remote(columns(cotangent, p), ct.at[fy], send_sem.at[2], recv_sem.at[2], (dom, p)).start()
    own_cot = pltpu.make_async_copy(columns(cotangent, fy), ct.at[fy], local_sem.at[8])
    own_cot.start()
    for device in z_peers:
        pl.semaphore_signal(z_sem, inc=1, device_id=device, device_id_type=MESH)
    xg[0, fy] = fv[:, pl.ds(pl.multiple_of(fy * vc, vc), vc)]

    for copy in loads[2:]:
        copy.wait()

    def slot_body(t, carry):
        col = tile_cols[t]
        far = jnp.maximum(col - nb, 0)
        back = lax.rem(dom + dom_size - far // 4, dom_size)
        place = jnp.where(
            back == offsets[0],
            0,
            jnp.where(back == offsets[1], 1, jnp.where(back == offsets[2], 2, 3)),
        )
        slots[t] = jnp.where(col < nb, col, nb + place * 4 + lax.rem(far, 4))
        return carry

    lax.fori_loop(0, tile_count, slot_body, 0, unroll=4)
    for b in range(nb):
        tab[b] = fv[:, b * BLOCK : (b + 1) * BLOCK]
    one_hot(tile_rows, nb, fr, 0, by_row)

    drain(stage, recv_sem.at[0])

    def agg_body(t, carry):
        prod[t] = split(dot_nt(tab[slots[t]], tiles[t]))
        return carry

    lax.fori_loop(0, tile_count, agg_body, 0, unroll=tile_count)
    sums = added(by_row, prod).astype(BF16)
    for b in range(nb):
        agg[b // vb, :, (b % vb) * BLOCK : (b % vb + 1) * BLOCK] = sums[b * fr : (b + 1) * fr]
    for p in y_peers:
        remote(agg.at[p], xg.at[1, fy], send_sem.at[3], recv_sem.at[3], (dom, p)).start()
    xg[1, fy] = agg[fy]

    for src, dst in ((w_self, wt_self), (w_neigh, wt_neigh)):
        dst[...] = src[...].astype(F32).T.astype(BF16)
    bias_mat[...] = jnp.broadcast_to(bias_row[...], (128, hidden)).T
    one_hot(slots, 16, fr, nb, by_far)
    one_hot(slots, nb, fr, 0, by_near)

    drain(xg.at[0, 0:others], recv_sem.at[1])
    early = dot_nn(wt_self[...], xg[0].reshape(in_dim, vc))
    pre_self[...] = early + jnp.concatenate([bias_mat[...]] * vb, axis=1)
    own_cot.wait()
    drain(ct.at[0:others], recv_sem.at[2])
    drain(agg.at[0:others], recv_sem.at[3])
    pre = pre_self[...] + dot_nn(wt_neigh[...], xg[1].reshape(in_dim, vc))
    sigma = jax.nn.sigmoid(pre)
    cot = ct[...].reshape(hidden, vc).astype(F32)
    dpre = (cot * sigma * (1.0 + pre * (1.0 - sigma))).astype(BF16)

    bias_part = dot_nt(jnp.ones((16, vc), BF16), dpre)
    for kind, out in ((1 - core, part_send), (core, part_own)):
        grads = dot_nt(xg[kind].reshape(in_dim, vc), dpre)
        half = jnp.where(kind == 0, bias_part[0:1, 0:128], bias_part[0:1, 128:256])
        for rt in range(row_tiles):
            for c in range(2):
                n = rt * 2 + c
                out[n // tpq, (n % tpq) * 8 : (n % tpq + 1) * 8, :] = grads[
                    rt * 8 : (rt + 1) * 8, c * 128 : (c + 1) * 128
                ]
        for n in range(xz):
            out[n, 8 * tpq : 8 * tpq + 1, :] = half
        if out is part_send:
            swap = remote(part_send, part_recv, send_sem.at[4], recv_sem.at[4], sibling)
            swap.start()
    bk[:, 0:fr] = dot_nn(w_self[...], dpre).astype(BF16).reshape(y_size, fr, vc)
    bk[:, fr : 2 * fr] = dot_nn(w_neigh[...], dpre).astype(BF16).reshape(y_size, fr, vc)
    for p in y_peers:
        remote(bk.at[p], bkr.at[fy], send_sem.at[5], recv_sem.at[5], (dom, p)).start()
    bkr[fy] = bk[fy]
    act[...] = (pre * sigma).astype(BF16).reshape(y_size, hr, vc)

    swap.wait_recv()
    pl.semaphore_wait(z_sem, z_size - 1)
    rs_src[...] = part_own[...] + part_recv[...]
    for _, p in xz_peers:
        remote(
            rs_src.at[p], rs_recv.at[q], send_sem.at[6], recv_sem.at[6], (p * CORES + core, fy)
        ).start()
    rs_recv[q] = rs_src[q]

    drain(bkr.at[0:others], recv_sem.at[5])
    for b in range(nb):
        btab[b] = bkr[b // vb, fr : 2 * fr, (b % vb) * BLOCK : (b % vb + 1) * BLOCK]

    def spread_body(t, carry):
        prod[t] = split(dot_nn(btab[tile_rows[t]], tiles[t]))
        return carry

    lax.fori_loop(0, tile_count, spread_body, 0, unroll=tile_count)
    sums = added(by_far, prod)
    for n in range(16):
        rb_send[n // 4, n % 4] = sums[n * fr : (n + 1) * fr]
    for pos in (3, 1, 0, 2):
        to = lax.rem(dom + dom_size - offsets[pos], dom_size)
        remote(
            rb_send.at[pos], rb_recv.at[pos], send_sem.at[7], recv_sem.at[7], (to, fy)
        ).start()

    drain(rs_recv.at[0 : xz - 1], recv_sem.at[6])
    total = rs_recv[0]
    for n in range(1, xz):
        total = total + rs_recv[n]
    y_src[...] = total
    y_recv[fy] = total
    for p in y_peers:
        remote(y_src, y_recv.at[fy], send_sem.at[8], recv_sem.at[8], (dom, p)).start()
    for p in y_peers:
        remote(
            act.at[p], columns(activated, fy), send_sem.at[9], recv_sem.at[9], (dom, p)
        ).start()
    own_act = pltpu.make_async_copy(act.at[fy], columns(activated, fy), local_sem.at[9])
    own_act.start()

    near = added(by_near, prod)

    drain(y_recv.at[0:others], recv_sem.at[8])
    total = y_recv[0]
    for n in range(1, y_size):
        total = total + y_recv[n]
    total = total * norm_scale
    g_half[q] = total[: 8 * tpq]
    b_full[core] = total[8 * tpq : 8 * tpq + 1]
    for dz, p in xz_peers:
        remote(
            g_half.at[q],
            g_half.at[q],
            send_sem.at[10],
            plane_sem.at[dz],
            (p * CORES + core, fy),
        ).start()
    bias_swap = remote(
        b_full.at[core], b_full.at[core], send_sem.at[11], recv_sem.at[9 + 1], sibling
    )
    bias_swap.start()

    drain(rb_recv, recv_sem.at[7])
    sums = [
        near[b * fr : (b + 1) * fr]
        + bkr[b // vb, 0:fr, (b % vb) * BLOCK : (b % vb + 1) * BLOCK].astype(F32)
        for b in range(nb)
    ]
    for pos in range(4):
        for c in range(4):
            term = rb_recv[pos, c]
            sums = [jnp.where(owners[pos][c] == b, v + term, v) for b, v in enumerate(sums)]
    for b in range(nb):
        gf[:, b * BLOCK : (b + 1) * BLOCK] = sums[b].astype(BF16)
    stores = [pltpu.make_async_copy(gf, grad_features, local_sem.at[0])]
    stores[0].start()

    bias_swap.wait_recv()
    for kind in range(2):
        gb[:, kind * 128 : (kind + 1) * 128] = b_full[kind]
    stores.append(pltpu.make_async_copy(gb, grad_bias, local_sem.at[1]))
    stores[1].start()

    for dz in sorted(range(z_size), key=lambda d: ring(d, z_size)):
        drain(g_half.at[0 : X_SIZE - (dz == 0)], plane_sem.at[dz])
        plane = pl.ds(lax.rem(my_z + z_size - dz, z_size) * X_SIZE, X_SIZE)
        remote(
            g_half.at[plane],
            grad_tiles.at[core, plane],
            send_sem.at[12],
            recv_sem.at[11],
            sibling,
        ).start()
    stores.append(pltpu.make_async_copy(g_half, grad_tiles.at[core], local_sem.at[2]))
    stores[2].start()
    own_act.wait()
    drain(activated.at[:, 0 : others * vc], recv_sem.at[9])
    drain(g_half, recv_sem.at[11])

    drain(stage, send_sem.at[0])
    drain(xg.at[0, 0:others], send_sem.at[1])
    drain(ct.at[0:others], send_sem.at[2])
    drain(agg.at[0:others], send_sem.at[3])
    swap.wait_send()
    drain(bkr.at[0:others], send_sem.at[5])
    drain(rs_recv.at[0 : xz - 1], send_sem.at[6])
    drain(rb_recv, send_sem.at[7])
    drain(y_recv.at[0:others], send_sem.at[8])
    drain(activated.at[:, 0 : others * vc], send_sem.at[9])
    drain(g_half.at[0 : xz - 1], send_sem.at[10])
    bias_swap.wait_send()
    drain(g_half, send_sem.at[12])
    for copy in stores:
        copy.wait()


def place(*refs):
    ins, outs, held, (gs, gn, sems) = refs[0:4], refs[4:9], refs[9:13], refs[13:16]
    first = [pltpu.make_async_copy(ins[i], held[i], sems.at[0, i]) for i in range(4)]
    ready = (held[0], held[1], gs, gn, held[3])
    second = [pltpu.make_async_copy(ready[i], outs[i], sems.at[1, i]) for i in range(5)]
    for copy in first:
        copy.start()
    first[2].wait()
    tiles = held[2]
    rows = tiles.shape[2]
    for kind, out in ((0, gs), (1, gn)):
        for n in range(2 * out.shape[0] // 8):
            rt, c, part = n // 2, n % 2, (n % (rows // 8)) * 8
            out[rt * 8 : (rt + 1) * 8, c * 128 : (c + 1) * 128] = tiles[
                kind, n // (rows // 8), part : part + 8, :
            ]
        second[2 + kind].start()
    for i, o in ((0, 0), (1, 1), (3, 4)):
        first[i].wait()
        second[o].start()
    for copy in second:
        copy.wait()


def local(
    features,
    self_weight,
    neigh_weight,
    bias_vector,
    tile_values,
    tile_rows,
    tile_cols,
    send_blocks,
    cotangent,
):
    dom_size = lax.axis_size("dom")
    y_size = lax.axis_size("feat")
    xz = dom_size // CORES
    fr, vertices = features.shape
    hr = cotangent.shape[0]
    in_dim, hidden = self_weight.shape
    tile_count = tile_values.shape[0]
    nb = vertices // BLOCK
    vc = vertices // y_size
    tpq = (in_dim // 8) * (hidden // 128) // xz
    ext = 8 * tpq + 1
    dims = (
        dom_size,
        y_size,
        nb,
        tile_count,
        in_dim,
        hidden,
        1.0 / math.sqrt(vertices * dom_size),
    )
    hbm = pl.BlockSpec(memory_space=pl.ANY)
    dma = pltpu.SemaphoreType.DMA
    outs = pl.pallas_call(
        functools.partial(kernel, dims),
        out_shape=(
            jax.ShapeDtypeStruct((hr, vertices), BF16),
            jax.ShapeDtypeStruct((fr, vertices), BF16),
            jax.ShapeDtypeStruct((2, xz, 8 * tpq, 128), F32),
            jax.ShapeDtypeStruct((1, hidden), F32),
        ),
        in_specs=[hbm] * 9,
        out_specs=(hbm,) * 4,
        scratch_shapes=[
            pltpu.SMEM((tile_count,), jnp.int32),
            pltpu.SMEM((tile_count,), jnp.int32),
            pltpu.SMEM((1, 4, dom_size), jnp.int32),
            pltpu.SMEM((tile_count,), jnp.int32),
            pltpu.VMEM((fr, vertices), BF16),
            pltpu.VMEM((1, hidden), F32),
            pltpu.VMEM((fr, vertices), BF16),
            pltpu.VMEM((tile_count, BLOCK, BLOCK), BF16),
            pltpu.VMEM((in_dim, hidden), BF16),
            pltpu.VMEM((in_dim, hidden), BF16),
            pltpu.VMEM((hidden, in_dim), BF16),
            pltpu.VMEM((hidden, in_dim), BF16),
            pltpu.VMEM((1, hidden), F32),
            pltpu.VMEM((hidden, 128), F32),
            pltpu.VMEM((2, y_size, fr, vc), BF16),
            pltpu.VMEM((hidden, vc), F32),
            pltpu.VMEM((y_size, hr, vc), BF16),
            pltpu.VMEM((nb, fr, BLOCK), BF16),
            pltpu.VMEM((nb + 16, fr, BLOCK), BF16),
            pltpu.VMEM((4, 4, fr, BLOCK), BF16),
            pltpu.VMEM((y_size, fr, vc), BF16),
            pltpu.VMEM((y_size, hr, vc), BF16),
            pltpu.VMEM((y_size, 2 * fr, vc), BF16),
            pltpu.VMEM((y_size, 2 * fr, vc), BF16),
            pltpu.VMEM((nb, fr, BLOCK), BF16),
            pltpu.VMEM((tile_count, fr, 2 * BLOCK), BF16),
            pltpu.VMEM((nb * fr, tile_count * fr), BF16),
            pltpu.VMEM((16 * fr, tile_count * fr), BF16),
            pltpu.VMEM((nb * fr, tile_count * fr), BF16),
            pltpu.VMEM((4, 4, fr, BLOCK), F32),
            pltpu.VMEM((4, 4, fr, BLOCK), F32),
            pltpu.VMEM((xz, ext, 128), F32),
            pltpu.VMEM((xz, ext, 128), F32),
            pltpu.VMEM((xz, ext, 128), F32),
            pltpu.VMEM((xz, ext, 128), F32),
            pltpu.VMEM((xz, ext, 128), F32),
            pltpu.VMEM((ext, 128), F32),
            pltpu.VMEM((y_size, ext, 128), F32),
            pltpu.VMEM((xz, 8 * tpq, 128), F32),
            pltpu.VMEM((2, 1, 128), F32),
            pltpu.SemaphoreType.REGULAR,
            dma((10,)),
            dma((13,)),
            dma((12,)),
            dma((xz // X_SIZE,)),
        ],
        compiler_params=pltpu.CompilerParams(
            collective_id=0, has_side_effects=True, vmem_limit_bytes=56 * 1024 * 1024
        ),
        name="graph_layer",
    )(
        tile_rows,
        tile_cols,
        send_blocks.transpose(0, 2, 1),
        features,
        self_weight,
        neigh_weight,
        bias_vector.reshape(1, hidden),
        tile_values,
        cotangent,
    )
    weight = jax.ShapeDtypeStruct((in_dim, hidden), F32)
    outs = pl.pallas_call(
        place,
        out_shape=(
            jax.ShapeDtypeStruct((hr, vertices), BF16),
            jax.ShapeDtypeStruct((fr, vertices), BF16),
            weight,
            weight,
            jax.ShapeDtypeStruct((1, hidden), F32),
        ),
        in_specs=[hbm] * 4,
        out_specs=(hbm,) * 5,
        scratch_shapes=[pltpu.VMEM(o.shape, o.dtype) for o in outs]
        + [pltpu.VMEM((in_dim, hidden), F32)] * 2
        + [dma((2, 5))],
        compiler_params=pltpu.CompilerParams(vmem_limit_bytes=56 * 1024 * 1024),
        name="place_outputs",
    )(*outs)
    activated, grad_features, grad_self, grad_neigh, grad_bias = outs
    return (activated, grad_features, grad_self, grad_neigh, grad_bias.reshape(hidden))


def solution(mesh):
    in_specs = (
        P("feat", "dom"),
        P(),
        P(),
        P(),
        P("dom", None, None),
        P("dom"),
        P("dom"),
        P("dom", None, None),
        P("feat", "dom"),
    )
    out_specs = (P("feat", "dom"), P("feat", "dom"), P(), P(), P())
    return jax.shard_map(local, mesh=mesh, in_specs=in_specs, out_specs=out_specs, check_vma=False)
```

```python
import functools
import math

import jax
import jax.numpy as jnp
from jax import lax
from jax.experimental import pallas as pl
from jax.experimental.pallas import tpu as pltpu
from jax.sharding import PartitionSpec as P

X_SIZE = 4
CORES = 2
BLOCK = 128
MESH = pl.DeviceIdType.MESH
F32 = jnp.float32
BF16 = jnp.bfloat16


def remote(src, dst, send_sem, recv_sem, device):
    return pltpu.make_async_remote_copy(
        src_ref=src,
        dst_ref=dst,
        send_sem=send_sem,
        recv_sem=recv_sem,
        device_id=device,
        device_id_type=MESH,
    )


def dot_nt(a, b):
    return lax.dot_general(a, b, (((1,), (1,)), ((), ())), preferred_element_type=F32)


def dot_nn(a, b):
    return lax.dot_general(a, b, (((1,), (0,)), ((), ())), preferred_element_type=F32)


def ring(step, size):
    return min(step, size - step)


def drain(ref, sem):
    pltpu.make_async_copy(ref, ref, sem).wait()


def one_hot(ids, nb, fr, base, out):
    rows = nb * fr
    per = 128 // fr
    lane = lax.broadcasted_iota(jnp.int32, (1, 128), 1)
    row = lax.broadcasted_iota(jnp.int32, (rows, 128), 0)
    for group in range(out.shape[1] // 128):
        key = jnp.zeros((1, 128), jnp.int32)
        for u in range(per):
            key = jnp.where(lane // fr == u, (ids[group * per + u] - base) * fr, key)
        key = key + lane % fr
        out[:, group * 128 : (group + 1) * 128] = jnp.where(row == key, 1.0, 0.0).astype(BF16)


def split(value):
    high = value.astype(BF16)
    return jnp.concatenate([high, (value - high.astype(F32)).astype(BF16)], axis=1)


def added(one_hots, parts):
    both = dot_nn(one_hots[...], parts[...].reshape(one_hots.shape[1], 2 * BLOCK))
    return both[:, :BLOCK] + both[:, BLOCK:]


def kernel(
    dims,
    rows_in,
    cols_in,
    blocks_in,
    features,
    self_weight,
    neigh_weight,
    bias,
    tile_values,
    cotangent,
    activated,
    grad_features,
    grad_tiles,
    grad_bias,
    tile_rows,
    tile_cols,
    send_blocks,
    slots,
    gf,
    gb,
    fv,
    tiles,
    w_self,
    w_neigh,
    wt_self,
    wt_neigh,
    bias_row,
    bias_mat,
    xg,
    pre_self,
    ct,
    own_tab,
    tab,
    stage,
    agg,
    act,
    bk,
    bkr,
    btab,
    prod,
    by_row,
    by_far,
    by_near,
    rb_send,
    rb_recv,
    part_own,
    part_send,
    part_recv,
    rs_src,
    rs_recv,
    y_src,
    y_recv,
    g_half,
    b_full,
    z_sem,
    local_sem,
    send_sem,
    recv_sem,
    plane_sem,
):
    dom_size, y_size, nb, tile_count, in_dim, hidden, norm_scale = dims
    z_size = dom_size // (X_SIZE * CORES)
    xz = X_SIZE * z_size
    fr = in_dim // y_size
    hr = hidden // y_size
    vb = nb // y_size
    vc = vb * BLOCK
    tpq = (in_dim // 8) * (hidden // 128) // xz
    row_tiles = in_dim // 8
    others = y_size - 1

    dom = lax.axis_index("dom")
    fy = lax.axis_index("feat")
    core = lax.rem(dom, CORES)
    q = dom // CORES
    my_z = q // X_SIZE
    my_x = lax.rem(q, X_SIZE)

    offsets = (1, 2, dom_size - 1, dom_size // 2)
    y_steps = sorted(range(1, y_size), key=lambda d: -ring(d, y_size))
    y_peers = [lax.rem(fy + d, y_size) for d in y_steps]
    sibling = (q * CORES + 1 - core, fy)
    xz_steps = [(dz, dx) for dz in range(z_size) for dx in range(X_SIZE) if dz or dx]
    xz_steps.sort(key=lambda d: -ring(d[0], z_size) - ring(d[1], X_SIZE))
    xz_peers = [
        (dz, lax.rem(my_z + dz, z_size) * X_SIZE + lax.rem(my_x + dx, X_SIZE))
        for dz, dx in xz_steps
    ]

    def columns(ref, y):
        return ref.at[:, pl.ds(pl.multiple_of(y * vc, vc), vc)]

    loads = [
        pltpu.make_async_copy(src, dst, local_sem.at[i])
        for i, (src, dst) in enumerate(
            (
                (blocks_in, send_blocks),
                (features, fv),
                (cols_in, tile_cols),
                (rows_in, tile_rows),
                (self_weight, w_self),
                (neigh_weight, w_neigh),
                (bias, bias_row),
                (tile_values, tiles),
            )
        )
    ]
    barrier = pltpu.get_barrier_semaphore()
    z_peers = [
        ((lax.rem(my_z + d, z_size) * X_SIZE + my_x) * CORES + core, fy)
        for d in sorted(range(1, z_size), key=lambda d: -ring(d, z_size))
    ]
    greet = z_peers + [(dom, p) for p in y_peers]
    for off in (1, dom_size - 1, 2, dom_size - 2):
        greet.append((lax.rem(dom + off, dom_size), fy))
    for d in range(1, X_SIZE):
        greet.append(((my_z * X_SIZE + lax.rem(my_x + d, X_SIZE)) * CORES + core, fy))
    greet.append(sibling)
    for device in greet:
        pl.semaphore_signal(barrier, inc=1, device_id=device, device_id_type=MESH)
    for copy in loads:
        copy.start()

    loads[0].wait()
    owners = []
    for pos in range(4):
        to = lax.rem(dom + offsets[pos], dom_size)
        owners.append([send_blocks[0, c, to] for c in range(4)])
    loads[1].wait()
    for b in range(nb):
        own_tab[b] = fv[:, b * BLOCK : (b + 1) * BLOCK]
    for pos in range(4):
        for c in range(4):
            stage[pos, c] = own_tab[jnp.maximum(owners[pos][c], 0)]

    pl.semaphore_wait(barrier, len(greet))

    for pos in (3, 1, 0, 2):
        to = lax.rem(dom + offsets[pos], dom_size)
        remote(
            stage.at[pos],
            tab.at[pl.ds(nb + 4 * pos, 4)],
            send_sem.at[0],
            recv_sem.at[0],
            (to, fy),
        ).start()
    for p in y_peers:
        remote(columns(fv, p), xg.at[0, fy], send_sem.at[1], recv_sem.at[1], (dom, p)).start()
    for p in y_peers:
        remote(columns(cotangent, p), ct.at[fy], send_sem.at[2], recv_sem.at[2], (dom, p)).start()
    own_cot = pltpu.make_async_copy(columns(cotangent, fy), ct.at[fy], local_sem.at[8])
    own_cot.start()
    for device in z_peers:
        pl.semaphore_signal(z_sem, inc=1, device_id=device, device_id_type=MESH)
    xg[0, fy] = fv[:, pl.ds(pl.multiple_of(fy * vc, vc), vc)]

    for copy in loads[2:]:
        copy.wait()

    def slot_body(t, carry):
        col = tile_cols[t]
        far = jnp.maximum(col - nb, 0)
        back = lax.rem(dom + dom_size - far // 4, dom_size)
        place = jnp.where(
            back == offsets[0],
            0,
            jnp.where(back == offsets[1], 1, jnp.where(back == offsets[2], 2, 3)),
        )
        slots[t] = jnp.where(col < nb, col, nb + place * 4 + lax.rem(far, 4))
        return carry

    lax.fori_loop(0, tile_count, slot_body, 0, unroll=4)
    for b in range(nb):
        tab[b] = fv[:, b * BLOCK : (b + 1) * BLOCK]
    one_hot(tile_rows, nb, fr, 0, by_row)

    drain(stage, recv_sem.at[0])

    def agg_body(t, carry):
        prod[t] = split(dot_nt(tab[slots[t]], tiles[t]))
        return carry

    lax.fori_loop(0, tile_count, agg_body, 0, unroll=tile_count)
    sums = added(by_row, prod).astype(BF16)
    for b in range(nb):
        agg[b // vb, :, (b % vb) * BLOCK : (b % vb + 1) * BLOCK] = sums[b * fr : (b + 1) * fr]
    for p in y_peers:
        remote(agg.at[p], xg.at[1, fy], send_sem.at[3], recv_sem.at[3], (dom, p)).start()
    xg[1, fy] = agg[fy]

    for src, dst in ((w_self, wt_self), (w_neigh, wt_neigh)):
        dst[...] = src[...].astype(F32).T.astype(BF16)
    bias_mat[...] = jnp.broadcast_to(bias_row[...], (128, hidden)).T
    one_hot(slots, 16, fr, nb, by_far)
    one_hot(slots, nb, fr, 0, by_near)

    drain(xg.at[0, 0:others], recv_sem.at[1])
    early = dot_nn(wt_self[...], xg[0].reshape(in_dim, vc))
    pre_self[...] = early + jnp.concatenate([bias_mat[...]] * vb, axis=1)
    own_cot.wait()
    drain(ct.at[0:others], recv_sem.at[2])
    drain(agg.at[0:others], recv_sem.at[3])
    pre = pre_self[...] + dot_nn(wt_neigh[...], xg[1].reshape(in_dim, vc))
    sigma = jax.nn.sigmoid(pre)
    cot = ct[...].reshape(hidden, vc).astype(F32)
    dpre = (cot * sigma * (1.0 + pre * (1.0 - sigma))).astype(BF16)

    bias_part = dot_nt(jnp.ones((16, vc), BF16), dpre)
    for kind, out in ((1 - core, part_send), (core, part_own)):
        grads = dot_nt(xg[kind].reshape(in_dim, vc), dpre)
        half = jnp.where(kind == 0, bias_part[0:1, 0:128], bias_part[0:1, 128:256])
        for rt in range(row_tiles):
            for c in range(2):
                n = rt * 2 + c
                out[n // tpq, (n % tpq) * 8 : (n % tpq + 1) * 8, :] = grads[
                    rt * 8 : (rt + 1) * 8, c * 128 : (c + 1) * 128
                ]
        for n in range(xz):
            out[n, 8 * tpq : 8 * tpq + 1, :] = half
        if out is part_send:
            swap = remote(part_send, part_recv, send_sem.at[4], recv_sem.at[4], sibling)
            swap.start()
    bk[:, 0:fr] = dot_nn(w_self[...], dpre).astype(BF16).reshape(y_size, fr, vc)
    bk[:, fr : 2 * fr] = dot_nn(w_neigh[...], dpre).astype(BF16).reshape(y_size, fr, vc)
    for p in y_peers:
        remote(bk.at[p], bkr.at[fy], send_sem.at[5], recv_sem.at[5], (dom, p)).start()
    bkr[fy] = bk[fy]
    act[...] = (pre * sigma).astype(BF16).reshape(y_size, hr, vc)

    swap.wait_recv()
    pl.semaphore_wait(z_sem, z_size - 1)
    rs_src[...] = part_own[...] + part_recv[...]
    for _, p in xz_peers:
        remote(
            rs_src.at[p], rs_recv.at[q], send_sem.at[6], recv_sem.at[6], (p * CORES + core, fy)
        ).start()
    rs_recv[q] = rs_src[q]

    drain(bkr.at[0:others], recv_sem.at[5])
    for b in range(nb):
        btab[b] = bkr[b // vb, fr : 2 * fr, (b % vb) * BLOCK : (b % vb + 1) * BLOCK]

    def spread_body(t, carry):
        prod[t] = split(dot_nn(btab[tile_rows[t]], tiles[t]))
        return carry

    lax.fori_loop(0, tile_count, spread_body, 0, unroll=tile_count)
    sums = added(by_far, prod)
    for n in range(16):
        rb_send[n // 4, n % 4] = sums[n * fr : (n + 1) * fr]
    for pos in (3, 1, 0, 2):
        to = lax.rem(dom + dom_size - offsets[pos], dom_size)
        remote(
            rb_send.at[pos], rb_recv.at[pos], send_sem.at[7], recv_sem.at[7], (to, fy)
        ).start()

    drain(rs_recv.at[0 : xz - 1], recv_sem.at[6])
    total = rs_recv[0]
    for n in range(1, xz):
        total = total + rs_recv[n]
    y_src[...] = total
    y_recv[fy] = total
    for p in y_peers:
        remote(y_src, y_recv.at[fy], send_sem.at[8], recv_sem.at[8], (dom, p)).start()
    for p in y_peers:
        remote(
            act.at[p], columns(activated, fy), send_sem.at[9], recv_sem.at[9], (dom, p)
        ).start()
    own_act = pltpu.make_async_copy(act.at[fy], columns(activated, fy), local_sem.at[9])
    own_act.start()

    near = added(by_near, prod)

    drain(y_recv.at[0:others], recv_sem.at[8])
    total = y_recv[0]
    for n in range(1, y_size):
        total = total + y_recv[n]
    total = total * norm_scale
    g_half[q] = total[: 8 * tpq]
    b_full[core] = total[8 * tpq : 8 * tpq + 1]
    for dz, p in xz_peers:
        remote(
            g_half.at[q],
            g_half.at[q],
            send_sem.at[10],
            plane_sem.at[dz],
            (p * CORES + core, fy),
        ).start()
    bias_swap = remote(
        b_full.at[core], b_full.at[core], send_sem.at[11], recv_sem.at[9 + 1], sibling
    )
    bias_swap.start()

    drain(rb_recv, recv_sem.at[7])
    sums = [
        near[b * fr : (b + 1) * fr]
        + bkr[b // vb, 0:fr, (b % vb) * BLOCK : (b % vb + 1) * BLOCK].astype(F32)
        for b in range(nb)
    ]
    for pos in range(4):
        for c in range(4):
            term = rb_recv[pos, c]
            sums = [jnp.where(owners[pos][c] == b, v + term, v) for b, v in enumerate(sums)]
    for b in range(nb):
        gf[:, b * BLOCK : (b + 1) * BLOCK] = sums[b].astype(BF16)
    stores = [pltpu.make_async_copy(gf, grad_features, local_sem.at[0])]
    stores[0].start()

    bias_swap.wait_recv()
    for kind in range(2):
        gb[:, kind * 128 : (kind + 1) * 128] = b_full[kind]
    stores.append(pltpu.make_async_copy(gb, grad_bias, local_sem.at[1]))
    stores[1].start()

    for dz in sorted(range(z_size), key=lambda d: ring(d, z_size)):
        drain(g_half.at[0 : X_SIZE - (dz == 0)], plane_sem.at[dz])
        plane = pl.ds(lax.rem(my_z + z_size - dz, z_size) * X_SIZE, X_SIZE)
        remote(
            g_half.at[plane],
            grad_tiles.at[core, plane],
            send_sem.at[12],
            recv_sem.at[11],
            sibling,
        ).start()
    stores.append(pltpu.make_async_copy(g_half, grad_tiles.at[core], local_sem.at[2]))
    stores[2].start()
    own_act.wait()
    drain(activated.at[:, 0 : others * vc], recv_sem.at[9])
    drain(g_half, recv_sem.at[11])

    drain(stage, send_sem.at[0])
    drain(xg.at[0, 0:others], send_sem.at[1])
    drain(ct.at[0:others], send_sem.at[2])
    drain(agg.at[0:others], send_sem.at[3])
    swap.wait_send()
    drain(bkr.at[0:others], send_sem.at[5])
    drain(rs_recv.at[0 : xz - 1], send_sem.at[6])
    drain(rb_recv, send_sem.at[7])
    drain(y_recv.at[0:others], send_sem.at[8])
    drain(activated.at[:, 0 : others * vc], send_sem.at[9])
    drain(g_half.at[0 : xz - 1], send_sem.at[10])
    bias_swap.wait_send()
    drain(g_half, send_sem.at[12])
    for copy in stores:
        copy.wait()


def place(*refs):
    ins, outs, (gs, gn, sems) = refs[0:4], refs[4:9], refs[9:12]
    tiles = ins[2]
    ready = (ins[0], ins[1], gs, gn, ins[3])
    copies = [pltpu.make_async_copy(ready[i], outs[i], sems.at[i]) for i in range(5)]
    for i in (0, 1, 4):
        copies[i].start()
    rows = tiles.shape[2]
    for kind, out in ((0, gs), (1, gn)):
        for n in range(2 * out.shape[0] // 8):
            rt, c, part = n // 2, n % 2, (n % (rows // 8)) * 8
            out[rt * 8 : (rt + 1) * 8, c * 128 : (c + 1) * 128] = tiles[
                kind, n // (rows // 8), part : part + 8, :
            ]
        copies[2 + kind].start()
    for copy in copies:
        copy.wait()


def local(
    features,
    self_weight,
    neigh_weight,
    bias_vector,
    tile_values,
    tile_rows,
    tile_cols,
    send_blocks,
    cotangent,
):
    dom_size = lax.axis_size("dom")
    y_size = lax.axis_size("feat")
    xz = dom_size // CORES
    fr, vertices = features.shape
    hr = cotangent.shape[0]
    in_dim, hidden = self_weight.shape
    tile_count = tile_values.shape[0]
    nb = vertices // BLOCK
    vc = vertices // y_size
    tpq = (in_dim // 8) * (hidden // 128) // xz
    ext = 8 * tpq + 1
    dims = (
        dom_size,
        y_size,
        nb,
        tile_count,
        in_dim,
        hidden,
        1.0 / math.sqrt(vertices * dom_size),
    )
    hbm = pl.BlockSpec(memory_space=pl.ANY)
    dma = pltpu.SemaphoreType.DMA
    outs = pl.pallas_call(
        functools.partial(kernel, dims),
        out_shape=(
            jax.ShapeDtypeStruct((hr, vertices), BF16),
            jax.ShapeDtypeStruct((fr, vertices), BF16),
            jax.ShapeDtypeStruct((2, xz, 8 * tpq, 128), F32),
            jax.ShapeDtypeStruct((1, hidden), F32),
        ),
        in_specs=[hbm] * 9,
        out_specs=(hbm,) * 4,
        scratch_shapes=[
            pltpu.SMEM((tile_count,), jnp.int32),
            pltpu.SMEM((tile_count,), jnp.int32),
            pltpu.SMEM((1, 4, dom_size), jnp.int32),
            pltpu.SMEM((tile_count,), jnp.int32),
            pltpu.VMEM((fr, vertices), BF16),
            pltpu.VMEM((1, hidden), F32),
            pltpu.VMEM((fr, vertices), BF16),
            pltpu.VMEM((tile_count, BLOCK, BLOCK), BF16),
            pltpu.VMEM((in_dim, hidden), BF16),
            pltpu.VMEM((in_dim, hidden), BF16),
            pltpu.VMEM((hidden, in_dim), BF16),
            pltpu.VMEM((hidden, in_dim), BF16),
            pltpu.VMEM((1, hidden), F32),
            pltpu.VMEM((hidden, 128), F32),
            pltpu.VMEM((2, y_size, fr, vc), BF16),
            pltpu.VMEM((hidden, vc), F32),
            pltpu.VMEM((y_size, hr, vc), BF16),
            pltpu.VMEM((nb, fr, BLOCK), BF16),
            pltpu.VMEM((nb + 16, fr, BLOCK), BF16),
            pltpu.VMEM((4, 4, fr, BLOCK), BF16),
            pltpu.VMEM((y_size, fr, vc), BF16),
            pltpu.VMEM((y_size, hr, vc), BF16),
            pltpu.VMEM((y_size, 2 * fr, vc), BF16),
            pltpu.VMEM((y_size, 2 * fr, vc), BF16),
            pltpu.VMEM((nb, fr, BLOCK), BF16),
            pltpu.VMEM((tile_count, fr, 2 * BLOCK), BF16),
            pltpu.VMEM((nb * fr, tile_count * fr), BF16),
            pltpu.VMEM((16 * fr, tile_count * fr), BF16),
            pltpu.VMEM((nb * fr, tile_count * fr), BF16),
            pltpu.VMEM((4, 4, fr, BLOCK), F32),
            pltpu.VMEM((4, 4, fr, BLOCK), F32),
            pltpu.VMEM((xz, ext, 128), F32),
            pltpu.VMEM((xz, ext, 128), F32),
            pltpu.VMEM((xz, ext, 128), F32),
            pltpu.VMEM((xz, ext, 128), F32),
            pltpu.VMEM((xz, ext, 128), F32),
            pltpu.VMEM((ext, 128), F32),
            pltpu.VMEM((y_size, ext, 128), F32),
            pltpu.VMEM((xz, 8 * tpq, 128), F32),
            pltpu.VMEM((2, 1, 128), F32),
            pltpu.SemaphoreType.REGULAR,
            dma((10,)),
            dma((13,)),
            dma((12,)),
            dma((xz // X_SIZE,)),
        ],
        compiler_params=pltpu.CompilerParams(
            collective_id=0, has_side_effects=True, vmem_limit_bytes=24 * 1024 * 1024
        ),
        name="graph_layer",
    )(
        *[
            pltpu.with_memory_space_constraint(operand, pltpu.HBM)
            for operand in (
                tile_rows,
                tile_cols,
                send_blocks.transpose(0, 2, 1),
                features,
                self_weight,
                neigh_weight,
                bias_vector.reshape(1, hidden),
                tile_values,
                cotangent,
            )
        ]
    )
    weight = jax.ShapeDtypeStruct((in_dim, hidden), F32)
    outs = pl.pallas_call(
        place,
        out_shape=(
            jax.ShapeDtypeStruct((hr, vertices), BF16),
            jax.ShapeDtypeStruct((fr, vertices), BF16),
            weight,
            weight,
            jax.ShapeDtypeStruct((1, hidden), F32),
        ),
        in_specs=[hbm, hbm, pl.BlockSpec(memory_space=pltpu.VMEM), hbm],
        out_specs=(hbm,) * 5,
        scratch_shapes=[
            pltpu.VMEM((in_dim, hidden), F32),
            pltpu.VMEM((in_dim, hidden), F32),
            dma((5,)),
        ],
        compiler_params=pltpu.CompilerParams(vmem_limit_bytes=8 * 1024 * 1024),
        name="place_outputs",
    )(*outs)
    activated, grad_features, grad_self, grad_neigh, grad_bias = outs
    return (activated, grad_features, grad_self, grad_neigh, grad_bias.reshape(hidden))


def solution(mesh):
    in_specs = (
        P("feat", "dom"),
        P(),
        P(),
        P(),
        P("dom", None, None),
        P("dom"),
        P("dom"),
        P("dom", None, None),
        P("feat", "dom"),
    )
    out_specs = (P("feat", "dom"), P("feat", "dom"), P(), P(), P())
    return jax.shard_map(local, mesh=mesh, in_specs=in_specs, out_specs=out_specs, check_vma=False)
```

```python
import functools
import math

import jax
import jax.numpy as jnp
from jax import lax
from jax.experimental import pallas as pl
from jax.experimental.pallas import tpu as pltpu
from jax.sharding import PartitionSpec as P

X_SIZE = 4
CORES = 2
BLOCK = 128
MESH = pl.DeviceIdType.MESH
F32 = jnp.float32
BF16 = jnp.bfloat16


def remote(src, dst, send_sem, recv_sem, device):
    return pltpu.make_async_remote_copy(
        src_ref=src,
        dst_ref=dst,
        send_sem=send_sem,
        recv_sem=recv_sem,
        device_id=device,
        device_id_type=MESH,
    )


def dot_nt(a, b):
    return lax.dot_general(a, b, (((1,), (1,)), ((), ())), preferred_element_type=F32)


def dot_nn(a, b):
    return lax.dot_general(a, b, (((1,), (0,)), ((), ())), preferred_element_type=F32)


def ring(step, size):
    return min(step, size - step)


def drain(ref, sem):
    pltpu.make_async_copy(ref, ref, sem).wait()


def one_hot(ids, nb, fr, base, out):
    rows = nb * fr
    per = 128 // fr
    lane = lax.broadcasted_iota(jnp.int32, (1, 128), 1)
    row = lax.broadcasted_iota(jnp.int32, (rows, 128), 0)
    for group in range(out.shape[1] // 128):
        key = jnp.zeros((1, 128), jnp.int32)
        for u in range(per):
            key = jnp.where(lane // fr == u, (ids[group * per + u] - base) * fr, key)
        key = key + lane % fr
        out[:, group * 128 : (group + 1) * 128] = jnp.where(row == key, 1.0, 0.0).astype(BF16)


def split(value):
    high = value.astype(BF16)
    return jnp.concatenate([high, (value - high.astype(F32)).astype(BF16)], axis=1)


def added(one_hots, parts):
    both = dot_nn(one_hots[...], parts[...].reshape(one_hots.shape[1], 2 * BLOCK))
    return both[:, :BLOCK] + both[:, BLOCK:]


def kernel(
    dims,
    rows_in,
    cols_in,
    blocks_in,
    features,
    self_weight,
    neigh_weight,
    bias,
    tile_values,
    cotangent,
    activated,
    grad_features,
    grad_tiles,
    grad_bias,
    tile_rows,
    tile_cols,
    send_blocks,
    slots,
    gf,
    gb,
    fv,
    tiles,
    w_self,
    w_neigh,
    wt_self,
    wt_neigh,
    bias_row,
    bias_mat,
    xg,
    pre_self,
    ct,
    own_tab,
    tab,
    stage,
    agg,
    act,
    bk,
    bkr,
    btab,
    prod,
    by_row,
    by_far,
    by_near,
    rb_send,
    rb_recv,
    part,
    rs_recv,
    t_src,
    t_core,
    y_src,
    y_recv,
    g_src,
    b_src,
    b_core,
    b_y,
    b_z,
    b_x,
    z_sem,
    local_sem,
    send_sem,
    recv_sem,
):
    dom_size, y_size, nb, tile_count, in_dim, hidden, norm_scale = dims
    z_size = dom_size // (X_SIZE * CORES)
    xz = X_SIZE * z_size
    fr = in_dim // y_size
    hr = hidden // y_size
    vb = nb // y_size
    vc = vb * BLOCK
    col_tiles = hidden // 128
    tpq = (2 * in_dim // 16) * col_tiles // xz
    others = y_size - 1

    dom = lax.axis_index("dom")
    fy = lax.axis_index("feat")
    core = lax.rem(dom, CORES)
    q = dom // CORES
    my_z = q // X_SIZE
    my_x = lax.rem(q, X_SIZE)

    offsets = (1, 2, dom_size - 1, dom_size // 2)
    y_steps = sorted(range(1, y_size), key=lambda d: -ring(d, y_size))
    y_peers = [lax.rem(fy + d, y_size) for d in y_steps]
    sibling = (q * CORES + 1 - core, fy)
    xz_steps = [(dz, dx) for dz in range(z_size) for dx in range(X_SIZE) if dz or dx]
    xz_steps.sort(key=lambda d: -ring(d[0], z_size) - ring(d[1], X_SIZE))
    xz_peers = [
        lax.rem(my_z + dz, z_size) * X_SIZE + lax.rem(my_x + dx, X_SIZE)
        for dz, dx in xz_steps
    ]

    def columns(ref, y):
        return ref.at[:, pl.ds(pl.multiple_of(y * vc, vc), vc)]

    loads = [
        pltpu.make_async_copy(src, dst, local_sem.at[i])
        for i, (src, dst) in enumerate(
            (
                (blocks_in, send_blocks),
                (features, fv),
                (cols_in, tile_cols),
                (rows_in, tile_rows),
                (self_weight, w_self),
                (neigh_weight, w_neigh),
                (bias, bias_row),
                (tile_values, tiles),
            )
        )
    ]
    barrier = pltpu.get_barrier_semaphore()
    z_peers = [
        ((lax.rem(my_z + d, z_size) * X_SIZE + my_x) * CORES + core, fy)
        for d in sorted(range(1, z_size), key=lambda d: -ring(d, z_size))
    ]
    greet = z_peers + [(dom, p) for p in y_peers]
    for off in (1, dom_size - 1, 2, dom_size - 2):
        greet.append((lax.rem(dom + off, dom_size), fy))
    x_peers = [
        ((my_z * X_SIZE + lax.rem(my_x + d, X_SIZE)) * CORES + core, fy) for d in range(1, X_SIZE)
    ]
    greet += x_peers
    greet.append(sibling)
    for device in greet:
        pl.semaphore_signal(barrier, inc=1, device_id=device, device_id_type=MESH)
    for copy in loads:
        copy.start()

    loads[0].wait()
    owners = []
    for pos in range(4):
        to = lax.rem(dom + offsets[pos], dom_size)
        owners.append([send_blocks[0, c, to] for c in range(4)])
    loads[1].wait()
    for b in range(nb):
        own_tab[b] = fv[:, b * BLOCK : (b + 1) * BLOCK]
    for pos in range(4):
        for c in range(4):
            stage[pos, c] = own_tab[jnp.maximum(owners[pos][c], 0)]

    pl.semaphore_wait(barrier, len(greet))

    for pos in (3, 1, 0, 2):
        to = lax.rem(dom + offsets[pos], dom_size)
        remote(
            stage.at[pos],
            tab.at[pl.ds(nb + 4 * pos, 4)],
            send_sem.at[0],
            recv_sem.at[0],
            (to, fy),
        ).start()
    for p in y_peers:
        remote(columns(fv, p), xg.at[0, fy], send_sem.at[1], recv_sem.at[1], (dom, p)).start()
    for p in y_peers:
        remote(columns(cotangent, p), ct.at[fy], send_sem.at[2], recv_sem.at[2], (dom, p)).start()
    own_cot = pltpu.make_async_copy(columns(cotangent, fy), ct.at[fy], local_sem.at[8])
    own_cot.start()
    for device in z_peers:
        pl.semaphore_signal(z_sem, inc=1, device_id=device, device_id_type=MESH)
    xg[0, fy] = fv[:, pl.ds(pl.multiple_of(fy * vc, vc), vc)]

    for copy in loads[2:]:
        copy.wait()

    def slot_body(t, carry):
        col = tile_cols[t]
        far = jnp.maximum(col - nb, 0)
        back = lax.rem(dom + dom_size - far // 4, dom_size)
        place = jnp.where(
            back == offsets[0],
            0,
            jnp.where(back == offsets[1], 1, jnp.where(back == offsets[2], 2, 3)),
        )
        slots[t] = jnp.where(col < nb, col, nb + place * 4 + lax.rem(far, 4))
        return carry

    lax.fori_loop(0, tile_count, slot_body, 0, unroll=4)
    for b in range(nb):
        tab[b] = fv[:, b * BLOCK : (b + 1) * BLOCK]
    one_hot(tile_rows, nb, fr, 0, by_row)

    drain(stage, recv_sem.at[0])

    def agg_body(t, carry):
        prod[t] = split(dot_nt(tab[slots[t]], tiles[t]))
        return carry

    lax.fori_loop(0, tile_count, agg_body, 0, unroll=tile_count)
    sums = added(by_row, prod).astype(BF16)
    for b in range(nb):
        agg[b // vb, :, (b % vb) * BLOCK : (b % vb + 1) * BLOCK] = sums[b * fr : (b + 1) * fr]
    for p in y_peers:
        remote(agg.at[p], xg.at[1, fy], send_sem.at[3], recv_sem.at[3], (dom, p)).start()
    xg[1, fy] = agg[fy]

    for src, dst in ((w_self, wt_self), (w_neigh, wt_neigh)):
        dst[...] = src[...].astype(F32).T.astype(BF16)
    bias_mat[...] = jnp.broadcast_to(bias_row[...], (128, hidden)).T
    one_hot(slots, 16, fr, nb, by_far)
    one_hot(slots, nb, fr, 0, by_near)

    drain(xg.at[0, 0:others], recv_sem.at[1])
    early = dot_nn(wt_self[...], xg[0].reshape(in_dim, vc))
    pre_self[...] = early + jnp.concatenate([bias_mat[...]] * vb, axis=1)
    own_cot.wait()
    drain(ct.at[0:others], recv_sem.at[2])
    drain(agg.at[0:others], recv_sem.at[3])
    pre = pre_self[...] + dot_nn(wt_neigh[...], xg[1].reshape(in_dim, vc))
    sigma = jax.nn.sigmoid(pre)
    cot = ct[...].reshape(hidden, vc).astype(F32)
    dpre = (cot * sigma * (1.0 + pre * (1.0 - sigma))).astype(BF16)

    b_src[0] = dot_nt(jnp.ones((16, vc), BF16), dpre)[0:1]
    bias_swap = remote(b_src.at[0], b_core, send_sem.at[4], recv_sem.at[4], sibling)
    bias_swap.start()
    grads = dot_nt(xg[...].reshape(2 * in_dim, vc), dpre).astype(BF16)
    for rt in range(2 * in_dim // 16):
        for c in range(col_tiles):
            n = rt * col_tiles + c
            part[n // tpq, (n % tpq) * 16 : (n % tpq + 1) * 16, :] = grads[
                rt * 16 : (rt + 1) * 16, c * 128 : (c + 1) * 128
            ]
    pl.semaphore_wait(z_sem, z_size - 1)
    for p in xz_peers:
        remote(
            part.at[p], rs_recv.at[q], send_sem.at[6], recv_sem.at[6], (p * CORES + core, fy)
        ).start()
    rs_recv[q] = part[q]

    bk[:, 0:fr] = dot_nn(w_self[...], dpre).astype(BF16).reshape(y_size, fr, vc)
    bk[:, fr : 2 * fr] = dot_nn(w_neigh[...], dpre).astype(BF16).reshape(y_size, fr, vc)
    for p in y_peers:
        remote(bk.at[p], bkr.at[fy], send_sem.at[5], recv_sem.at[5], (dom, p)).start()
    bkr[fy] = bk[fy]
    act[...] = (pre * sigma).astype(BF16).reshape(y_size, hr, vc)

    bias_swap.wait_recv()
    b_sum = b_src[0] + b_core[...]
    b_src[1] = b_sum
    b_y[fy] = b_sum
    for p in y_peers:
        remote(b_src.at[1], b_y.at[fy], send_sem.at[10], recv_sem.at[10], (dom, p)).start()

    drain(rs_recv.at[0 : xz - 1], recv_sem.at[6])
    total = rs_recv[0].astype(F32)
    for n in range(1, xz):
        total = total + rs_recv[n].astype(F32)
    t_src[...] = total
    swap = remote(t_src, t_core, send_sem.at[12], recv_sem.at[12], sibling)
    swap.start()
    drain(b_y.at[0:others], recv_sem.at[10])
    b_sum = b_y[0]
    for n in range(1, y_size):
        b_sum = b_sum + b_y[n]
    b_src[2] = b_sum
    b_z[my_z] = b_sum
    for device in z_peers:
        remote(b_src.at[2], b_z.at[my_z], send_sem.at[11], recv_sem.at[11], device).start()
    swap.wait_recv()
    total = total + t_core[...]
    y_src[...] = total
    y_recv[fy] = total
    for p in y_peers:
        remote(y_src, y_recv.at[fy], send_sem.at[8], recv_sem.at[8], (dom, p)).start()
    for p in y_peers:
        remote(
            act.at[p], columns(activated, fy), send_sem.at[9], recv_sem.at[9], (dom, p)
        ).start()
    own_act = pltpu.make_async_copy(act.at[fy], columns(activated, fy), local_sem.at[9])
    own_act.start()

    drain(bkr.at[0:others], recv_sem.at[5])
    for b in range(nb):
        btab[b] = bkr[b // vb, fr : 2 * fr, (b % vb) * BLOCK : (b % vb + 1) * BLOCK]

    def spread_body(t, carry):
        prod[t] = split(dot_nn(btab[tile_rows[t]], tiles[t]))
        return carry

    lax.fori_loop(0, tile_count, spread_body, 0, unroll=tile_count)
    sums = added(by_far, prod)
    for n in range(16):
        rb_send[n // 4, n % 4] = sums[n * fr : (n + 1) * fr]
    for pos in (3, 1, 0, 2):
        to = lax.rem(dom + dom_size - offsets[pos], dom_size)
        remote(
            rb_send.at[pos], rb_recv.at[pos], send_sem.at[7], recv_sem.at[7], (to, fy)
        ).start()

    near = added(by_near, prod)

    drain(y_recv.at[0:others], recv_sem.at[8])
    total = y_recv[0]
    for n in range(1, y_size):
        total = total + y_recv[n]
    g_src[...] = (total * norm_scale).astype(BF16)
    for p in xz_peers:
        remote(
            g_src, grad_tiles.at[q], send_sem.at[13], recv_sem.at[13], (p * CORES + core, fy)
        ).start()
    stores = [pltpu.make_async_copy(g_src, grad_tiles.at[q], local_sem.at[2])]
    drain(b_z.at[0 : z_size - 1], recv_sem.at[11])
    b_sum = b_z[0]
    for n in range(1, z_size):
        b_sum = b_sum + b_z[n]
    b_src[3] = b_sum
    b_x[my_x] = b_sum
    for device in x_peers:
        remote(b_src.at[3], b_x.at[my_x], send_sem.at[14], recv_sem.at[14], device).start()

    drain(rb_recv, recv_sem.at[7])
    sums = [
        near[b * fr : (b + 1) * fr]
        + bkr[b // vb, 0:fr, (b % vb) * BLOCK : (b % vb + 1) * BLOCK].astype(F32)
        for b in range(nb)
    ]
    for pos in range(4):
        for c in range(4):
            term = rb_recv[pos, c]
            sums = [jnp.where(owners[pos][c] == b, v + term, v) for b, v in enumerate(sums)]
    for b in range(nb):
        gf[:, b * BLOCK : (b + 1) * BLOCK] = sums[b].astype(BF16)
    stores.append(pltpu.make_async_copy(gf, grad_features, local_sem.at[0]))
    for copy in stores:
        copy.start()

    drain(b_x.at[0 : X_SIZE - 1], recv_sem.at[14])
    b_sum = b_x[0]
    for n in range(1, X_SIZE):
        b_sum = b_sum + b_x[n]
    gb[...] = b_sum * norm_scale
    stores.append(pltpu.make_async_copy(gb, grad_bias, local_sem.at[1]))
    stores[-1].start()
    own_act.wait()
    drain(activated.at[:, 0 : others * vc], recv_sem.at[9])
    drain(grad_tiles.at[0 : xz - 1], recv_sem.at[13])

    drain(stage, send_sem.at[0])
    drain(xg.at[0, 0:others], send_sem.at[1])
    drain(ct.at[0:others], send_sem.at[2])
    drain(agg.at[0:others], send_sem.at[3])
    bias_swap.wait_send()
    drain(bkr.at[0:others], send_sem.at[5])
    drain(rs_recv.at[0 : xz - 1], send_sem.at[6])
    drain(rb_recv, send_sem.at[7])
    drain(y_recv.at[0:others], send_sem.at[8])
    drain(activated.at[:, 0 : others * vc], send_sem.at[9])
    drain(b_y.at[0:others], send_sem.at[10])
    drain(b_z.at[0 : z_size - 1], send_sem.at[11])
    swap.wait_send()
    drain(rs_recv.at[0 : xz - 1], send_sem.at[13])
    drain(b_x.at[0 : X_SIZE - 1], send_sem.at[14])
    for copy in stores:
        copy.wait()


def place(*refs):
    ins, outs, (gs, gn, sems) = refs[0:4], refs[4:9], refs[9:12]
    tiles = ins[2]
    ready = (ins[0], ins[1], gs, gn, ins[3])
    copies = [pltpu.make_async_copy(ready[i], outs[i], sems.at[i]) for i in range(5)]
    for i in (0, 1, 4):
        copies[i].start()
    in_dim, hidden = gs.shape
    tpq = tiles.shape[1] // 16
    for kind, out in ((0, gs), (1, gn)):
        for r in range(in_dim // 16):
            for c in range(hidden // 128):
                n = (kind * in_dim // 16 + r) * (hidden // 128) + c
                out[r * 16 : (r + 1) * 16, c * 128 : (c + 1) * 128] = tiles[
                    n // tpq, (n % tpq) * 16 : (n % tpq + 1) * 16, :
                ].astype(F32)
        copies[2 + kind].start()
    for copy in copies:
        copy.wait()


def local(
    features,
    self_weight,
    neigh_weight,
    bias_vector,
    tile_values,
    tile_rows,
    tile_cols,
    send_blocks,
    cotangent,
):
    dom_size = lax.axis_size("dom")
    y_size = lax.axis_size("feat")
    xz = dom_size // CORES
    fr, vertices = features.shape
    hr = cotangent.shape[0]
    in_dim, hidden = self_weight.shape
    tile_count = tile_values.shape[0]
    nb = vertices // BLOCK
    vc = vertices // y_size
    rows = (2 * in_dim * hidden) // (128 * xz)
    dims = (
        dom_size,
        y_size,
        nb,
        tile_count,
        in_dim,
        hidden,
        1.0 / math.sqrt(vertices * dom_size),
    )
    hbm = pl.BlockSpec(memory_space=pl.ANY)
    dma = pltpu.SemaphoreType.DMA
    outs = pl.pallas_call(
        functools.partial(kernel, dims),
        out_shape=(
            jax.ShapeDtypeStruct((hr, vertices), BF16),
            jax.ShapeDtypeStruct((fr, vertices), BF16),
            jax.ShapeDtypeStruct((xz, rows, 128), BF16),
            jax.ShapeDtypeStruct((1, hidden), F32),
        ),
        in_specs=[hbm] * 9,
        out_specs=(hbm,) * 4,
        scratch_shapes=[
            pltpu.SMEM((tile_count,), jnp.int32),
            pltpu.SMEM((tile_count,), jnp.int32),
            pltpu.SMEM((1, 4, dom_size), jnp.int32),
            pltpu.SMEM((tile_count,), jnp.int32),
            pltpu.VMEM((fr, vertices), BF16),
            pltpu.VMEM((1, hidden), F32),
            pltpu.VMEM((fr, vertices), BF16),
            pltpu.VMEM((tile_count, BLOCK, BLOCK), BF16),
            pltpu.VMEM((in_dim, hidden), BF16),
            pltpu.VMEM((in_dim, hidden), BF16),
            pltpu.VMEM((hidden, in_dim), BF16),
            pltpu.VMEM((hidden, in_dim), BF16),
            pltpu.VMEM((1, hidden), F32),
            pltpu.VMEM((hidden, 128), F32),
            pltpu.VMEM((2, y_size, fr, vc), BF16),
            pltpu.VMEM((hidden, vc), F32),
            pltpu.VMEM((y_size, hr, vc), BF16),
            pltpu.VMEM((nb, fr, BLOCK), BF16),
            pltpu.VMEM((nb + 16, fr, BLOCK), BF16),
            pltpu.VMEM((4, 4, fr, BLOCK), BF16),
            pltpu.VMEM((y_size, fr, vc), BF16),
            pltpu.VMEM((y_size, hr, vc), BF16),
            pltpu.VMEM((y_size, 2 * fr, vc), BF16),
            pltpu.VMEM((y_size, 2 * fr, vc), BF16),
            pltpu.VMEM((nb, fr, BLOCK), BF16),
            pltpu.VMEM((tile_count, fr, 2 * BLOCK), BF16),
            pltpu.VMEM((nb * fr, tile_count * fr), BF16),
            pltpu.VMEM((16 * fr, tile_count * fr), BF16),
            pltpu.VMEM((nb * fr, tile_count * fr), BF16),
            pltpu.VMEM((4, 4, fr, BLOCK), F32),
            pltpu.VMEM((4, 4, fr, BLOCK), F32),
            pltpu.VMEM((xz, rows, 128), BF16),
            pltpu.VMEM((xz, rows, 128), BF16),
            pltpu.VMEM((rows, 128), F32),
            pltpu.VMEM((rows, 128), F32),
            pltpu.VMEM((rows, 128), F32),
            pltpu.VMEM((y_size, rows, 128), F32),
            pltpu.VMEM((rows, 128), BF16),
            pltpu.VMEM((4, 1, hidden), F32),
            pltpu.VMEM((1, hidden), F32),
            pltpu.VMEM((y_size, 1, hidden), F32),
            pltpu.VMEM((xz // X_SIZE, 1, hidden), F32),
            pltpu.VMEM((X_SIZE, 1, hidden), F32),
            pltpu.SemaphoreType.REGULAR,
            dma((10,)),
            dma((15,)),
            dma((15,)),
        ],
        compiler_params=pltpu.CompilerParams(
            collective_id=0, has_side_effects=True, vmem_limit_bytes=24 * 1024 * 1024
        ),
        name="graph_layer",
    )(
        *[
            pltpu.with_memory_space_constraint(operand, pltpu.HBM)
            for operand in (
                tile_rows,
                tile_cols,
                send_blocks.transpose(0, 2, 1),
                features,
                self_weight,
                neigh_weight,
                bias_vector.reshape(1, hidden),
                tile_values,
                cotangent,
            )
        ]
    )
    weight = jax.ShapeDtypeStruct((in_dim, hidden), F32)
    outs = pl.pallas_call(
        place,
        out_shape=(
            jax.ShapeDtypeStruct((hr, vertices), BF16),
            jax.ShapeDtypeStruct((fr, vertices), BF16),
            weight,
            weight,
            jax.ShapeDtypeStruct((1, hidden), F32),
        ),
        in_specs=[hbm, hbm, pl.BlockSpec(memory_space=pltpu.VMEM), hbm],
        out_specs=(hbm,) * 5,
        scratch_shapes=[
            pltpu.VMEM((in_dim, hidden), F32),
            pltpu.VMEM((in_dim, hidden), F32),
            dma((5,)),
        ],
        compiler_params=pltpu.CompilerParams(vmem_limit_bytes=8 * 1024 * 1024),
        name="place_outputs",
    )(*outs)
    activated, grad_features, grad_self, grad_neigh, grad_bias = outs
    return (activated, grad_features, grad_self, grad_neigh, grad_bias.reshape(hidden))


def solution(mesh):
    in_specs = (
        P("feat", "dom"),
        P(),
        P(),
        P(),
        P("dom", None, None),
        P("dom"),
        P("dom"),
        P("dom", None, None),
        P("feat", "dom"),
    )
    out_specs = (P("feat", "dom"), P("feat", "dom"), P(), P(), P())
    return jax.shard_map(local, mesh=mesh, in_specs=in_specs, out_specs=out_specs, check_vma=False)
```

```python
import functools
import math

import jax
import jax.numpy as jnp
from jax import lax
from jax.experimental import pallas as pl
from jax.experimental.pallas import tpu as pltpu
from jax.sharding import PartitionSpec as P

X_SIZE = 4
CORES = 2
BLOCK = 128
MESH = pl.DeviceIdType.MESH
F32 = jnp.float32
BF16 = jnp.bfloat16


def remote(src, dst, send_sem, recv_sem, device):
    return pltpu.make_async_remote_copy(
        src_ref=src,
        dst_ref=dst,
        send_sem=send_sem,
        recv_sem=recv_sem,
        device_id=device,
        device_id_type=MESH,
    )


def dot_nt(a, b):
    return lax.dot_general(a, b, (((1,), (1,)), ((), ())), preferred_element_type=F32)


def dot_nn(a, b):
    return lax.dot_general(a, b, (((1,), (0,)), ((), ())), preferred_element_type=F32)


def ring(step, size):
    return min(step, size - step)


def drain(ref, sem):
    pltpu.make_async_copy(ref, ref, sem).wait()


def one_hot(ids, nb, fr, base, out):
    rows = nb * fr
    per = 128 // fr
    lane = lax.broadcasted_iota(jnp.int32, (1, 128), 1)
    row = lax.broadcasted_iota(jnp.int32, (rows, 128), 0)
    for group in range(out.shape[1] // 128):
        key = jnp.zeros((1, 128), jnp.int32)
        for u in range(per):
            key = jnp.where(lane // fr == u, (ids[group * per + u] - base) * fr, key)
        key = key + lane % fr
        out[:, group * 128 : (group + 1) * 128] = jnp.where(row == key, 1.0, 0.0).astype(BF16)


def split(value):
    high = value.astype(BF16)
    return jnp.concatenate([high, (value - high.astype(F32)).astype(BF16)], axis=1)


def added(one_hots, parts):
    both = dot_nn(one_hots[...], parts[...].reshape(one_hots.shape[1], 2 * BLOCK))
    return both[:, :BLOCK] + both[:, BLOCK:]


def kernel(
    dims,
    rows_in,
    cols_in,
    blocks_in,
    features,
    self_weight,
    neigh_weight,
    bias,
    tile_values,
    cotangent,
    activated,
    grad_features,
    grad_tiles,
    grad_bias,
    tile_rows,
    tile_cols,
    send_blocks,
    slots,
    gf,
    gb,
    fv,
    tiles,
    w_self,
    w_neigh,
    wt_self,
    wt_neigh,
    bias_row,
    bias_mat,
    xg,
    pre_self,
    ct,
    own_tab,
    tab,
    stage,
    agg,
    act,
    bk,
    bkr,
    btab,
    prod,
    by_row,
    by_far,
    by_near,
    rb_send,
    rb_recv,
    part,
    rs_recv,
    t_src,
    t_core,
    y_src,
    y_recv,
    g_src,
    b_src,
    b_core,
    b_y,
    b_z,
    b_x,
    z_sem,
    local_sem,
    send_sem,
    recv_sem,
):
    dom_size, y_size, nb, tile_count, in_dim, hidden, norm_scale = dims
    z_size = dom_size // (X_SIZE * CORES)
    xz = X_SIZE * z_size
    fr = in_dim // y_size
    hr = hidden // y_size
    vb = nb // y_size
    vc = vb * BLOCK
    col_tiles = hidden // 128
    tpq = (2 * in_dim // 16) * col_tiles // xz
    others = y_size - 1

    dom = lax.axis_index("dom")
    fy = lax.axis_index("feat")
    core = lax.rem(dom, CORES)
    q = dom // CORES
    my_z = q // X_SIZE
    my_x = lax.rem(q, X_SIZE)

    offsets = (1, 2, dom_size - 1, dom_size // 2)
    y_steps = sorted(range(1, y_size), key=lambda d: -ring(d, y_size))
    y_peers = [lax.rem(fy + d, y_size) for d in y_steps]
    sibling = (q * CORES + 1 - core, fy)
    xz_steps = [(dz, dx) for dz in range(z_size) for dx in range(X_SIZE) if dz or dx]
    xz_steps.sort(key=lambda d: -ring(d[0], z_size) - ring(d[1], X_SIZE))
    xz_peers = [
        lax.rem(my_z + dz, z_size) * X_SIZE + lax.rem(my_x + dx, X_SIZE)
        for dz, dx in xz_steps
    ]

    def columns(ref, y):
        return ref.at[:, pl.ds(pl.multiple_of(y * vc, vc), vc)]

    loads = [
        pltpu.make_async_copy(src, dst, local_sem.at[i])
        for i, (src, dst) in enumerate(
            (
                (blocks_in, send_blocks),
                (features, fv),
                (cols_in, tile_cols),
                (rows_in, tile_rows),
                (self_weight, w_self),
                (neigh_weight, w_neigh),
                (bias, bias_row),
                (tile_values, tiles),
            )
        )
    ]
    barrier = pltpu.get_barrier_semaphore()
    z_peers = [
        ((lax.rem(my_z + d, z_size) * X_SIZE + my_x) * CORES + core, fy)
        for d in sorted(range(1, z_size), key=lambda d: -ring(d, z_size))
    ]
    greet = z_peers + [(dom, p) for p in y_peers]
    for off in (1, dom_size - 1, 2, dom_size - 2):
        greet.append((lax.rem(dom + off, dom_size), fy))
    x_peers = [
        ((my_z * X_SIZE + lax.rem(my_x + d, X_SIZE)) * CORES + core, fy) for d in range(1, X_SIZE)
    ]
    greet += x_peers
    greet.append(sibling)
    for device in greet:
        pl.semaphore_signal(barrier, inc=1, device_id=device, device_id_type=MESH)
    for copy in loads:
        copy.start()

    loads[0].wait()
    owners = []
    for pos in range(4):
        to = lax.rem(dom + offsets[pos], dom_size)
        owners.append([send_blocks[0, c, to] for c in range(4)])
    loads[1].wait()
    for b in range(nb):
        own_tab[b] = fv[:, b * BLOCK : (b + 1) * BLOCK]
    for pos in range(4):
        for c in range(4):
            stage[pos, c] = own_tab[jnp.maximum(owners[pos][c], 0)]

    pl.semaphore_wait(barrier, len(greet))

    for pos in (3, 1, 0, 2):
        to = lax.rem(dom + offsets[pos], dom_size)
        remote(
            stage.at[pos],
            tab.at[pl.ds(nb + 4 * pos, 4)],
            send_sem.at[0],
            recv_sem.at[0],
            (to, fy),
        ).start()
    for p in y_peers:
        remote(columns(fv, p), xg.at[0, fy], send_sem.at[1], recv_sem.at[1], (dom, p)).start()
    for p in y_peers:
        remote(columns(cotangent, p), ct.at[fy], send_sem.at[2], recv_sem.at[2], (dom, p)).start()
    own_cot = pltpu.make_async_copy(columns(cotangent, fy), ct.at[fy], local_sem.at[8])
    own_cot.start()
    for device in z_peers:
        pl.semaphore_signal(z_sem, inc=1, device_id=device, device_id_type=MESH)
    xg[0, fy] = fv[:, pl.ds(pl.multiple_of(fy * vc, vc), vc)]

    for copy in loads[2:]:
        copy.wait()

    def slot_body(t, carry):
        col = tile_cols[t]
        far = jnp.maximum(col - nb, 0)
        back = lax.rem(dom + dom_size - far // 4, dom_size)
        place = jnp.where(
            back == offsets[0],
            0,
            jnp.where(back == offsets[1], 1, jnp.where(back == offsets[2], 2, 3)),
        )
        slots[t] = jnp.where(col < nb, col, nb + place * 4 + lax.rem(far, 4))
        return carry

    lax.fori_loop(0, tile_count, slot_body, 0, unroll=4)
    for b in range(nb):
        tab[b] = fv[:, b * BLOCK : (b + 1) * BLOCK]
    one_hot(tile_rows, nb, fr, 0, by_row)

    drain(stage, recv_sem.at[0])

    def agg_body(t, carry):
        prod[t] = split(dot_nt(tab[slots[t]], tiles[t]))
        return carry

    lax.fori_loop(0, tile_count, agg_body, 0, unroll=tile_count)
    sums = added(by_row, prod).astype(BF16)
    for b in range(nb):
        agg[b // vb, :, (b % vb) * BLOCK : (b % vb + 1) * BLOCK] = sums[b * fr : (b + 1) * fr]
    for p in y_peers:
        remote(agg.at[p], xg.at[1, fy], send_sem.at[3], recv_sem.at[3], (dom, p)).start()
    xg[1, fy] = agg[fy]

    for src, dst in ((w_self, wt_self), (w_neigh, wt_neigh)):
        dst[...] = src[...].astype(F32).T.astype(BF16)
    bias_mat[...] = jnp.broadcast_to(bias_row[...], (128, hidden)).T
    one_hot(slots, 16, fr, nb, by_far)
    one_hot(slots, nb, fr, 0, by_near)

    drain(xg.at[0, 0:others], recv_sem.at[1])
    early = dot_nn(wt_self[...], xg[0].reshape(in_dim, vc))
    pre_self[...] = early + jnp.concatenate([bias_mat[...]] * vb, axis=1)
    own_cot.wait()
    drain(ct.at[0:others], recv_sem.at[2])
    drain(agg.at[0:others], recv_sem.at[3])
    pre = pre_self[...] + dot_nn(wt_neigh[...], xg[1].reshape(in_dim, vc))
    sigma = jax.nn.sigmoid(pre)
    cot = ct[...].reshape(hidden, vc).astype(F32)
    dpre = (cot * sigma * (1.0 + pre * (1.0 - sigma))).astype(BF16)

    grads = dot_nt(xg[...].reshape(2 * in_dim, vc), dpre).astype(BF16)
    for rt in range(2 * in_dim // 16):
        for c in range(col_tiles):
            n = rt * col_tiles + c
            part[n // tpq, (n % tpq) * 16 : (n % tpq + 1) * 16, :] = grads[
                rt * 16 : (rt + 1) * 16, c * 128 : (c + 1) * 128
            ]
    pl.semaphore_wait(z_sem, z_size - 1)
    for p in xz_peers:
        remote(
            part.at[p], rs_recv.at[q], send_sem.at[6], recv_sem.at[6], (p * CORES + core, fy)
        ).start()
    rs_recv[q] = part[q]
    b_src[0] = dot_nt(jnp.ones((16, vc), BF16), dpre)[0:1]
    bias_swap = remote(b_src.at[0], b_core, send_sem.at[4], recv_sem.at[4], sibling)
    bias_swap.start()

    bk[:, 0:fr] = dot_nn(w_self[...], dpre).astype(BF16).reshape(y_size, fr, vc)
    bk[:, fr : 2 * fr] = dot_nn(w_neigh[...], dpre).astype(BF16).reshape(y_size, fr, vc)
    for p in y_peers:
        remote(bk.at[p], bkr.at[fy], send_sem.at[5], recv_sem.at[5], (dom, p)).start()
    bkr[fy] = bk[fy]
    act[...] = (pre * sigma).astype(BF16).reshape(y_size, hr, vc)

    bias_swap.wait_recv()
    b_sum = b_src[0] + b_core[...]
    b_src[1] = b_sum
    b_y[fy] = b_sum
    for p in y_peers:
        remote(b_src.at[1], b_y.at[fy], send_sem.at[10], recv_sem.at[10], (dom, p)).start()

    drain(rs_recv.at[0 : xz - 1], recv_sem.at[6])
    total = rs_recv[0].astype(F32)
    for n in range(1, xz):
        total = total + rs_recv[n].astype(F32)
    t_src[...] = total
    swap = remote(t_src, t_core, send_sem.at[12], recv_sem.at[12], sibling)
    swap.start()
    swap.wait_recv()
    total = total + t_core[...]
    y_src[...] = total
    y_recv[fy] = total
    for p in y_peers:
        remote(y_src, y_recv.at[fy], send_sem.at[8], recv_sem.at[8], (dom, p)).start()

    drain(b_y.at[0:others], recv_sem.at[10])
    b_sum = b_y[0]
    for n in range(1, y_size):
        b_sum = b_sum + b_y[n]
    b_src[2] = b_sum
    b_z[my_z] = b_sum
    for device in z_peers:
        remote(b_src.at[2], b_z.at[my_z], send_sem.at[11], recv_sem.at[11], device).start()

    drain(bkr.at[0:others], recv_sem.at[5])
    for b in range(nb):
        btab[b] = bkr[b // vb, fr : 2 * fr, (b % vb) * BLOCK : (b % vb + 1) * BLOCK]

    def spread_body(t, carry):
        prod[t] = split(dot_nn(btab[tile_rows[t]], tiles[t]))
        return carry

    lax.fori_loop(0, tile_count, spread_body, 0, unroll=tile_count)
    sums = added(by_far, prod)
    for n in range(16):
        rb_send[n // 4, n % 4] = sums[n * fr : (n + 1) * fr]
    for pos in (3, 1, 0, 2):
        to = lax.rem(dom + dom_size - offsets[pos], dom_size)
        remote(
            rb_send.at[pos], rb_recv.at[pos], send_sem.at[7], recv_sem.at[7], (to, fy)
        ).start()

    near = added(by_near, prod)

    drain(y_recv.at[0:others], recv_sem.at[8])
    total = y_recv[0]
    for n in range(1, y_size):
        total = total + y_recv[n]
    g_src[...] = (total * norm_scale).astype(BF16)
    for p in xz_peers:
        remote(
            g_src, grad_tiles.at[q], send_sem.at[13], recv_sem.at[13], (p * CORES + core, fy)
        ).start()
    for p in y_peers:
        remote(
            act.at[p], columns(activated, fy), send_sem.at[9], recv_sem.at[9], (dom, p)
        ).start()
    own_act = pltpu.make_async_copy(act.at[fy], columns(activated, fy), local_sem.at[9])
    own_act.start()
    stores = [pltpu.make_async_copy(g_src, grad_tiles.at[q], local_sem.at[2])]
    drain(b_z.at[0 : z_size - 1], recv_sem.at[11])
    b_sum = b_z[0]
    for n in range(1, z_size):
        b_sum = b_sum + b_z[n]
    b_src[3] = b_sum
    b_x[my_x] = b_sum
    for device in x_peers:
        remote(b_src.at[3], b_x.at[my_x], send_sem.at[14], recv_sem.at[14], device).start()

    drain(rb_recv, recv_sem.at[7])
    sums = [
        near[b * fr : (b + 1) * fr]
        + bkr[b // vb, 0:fr, (b % vb) * BLOCK : (b % vb + 1) * BLOCK].astype(F32)
        for b in range(nb)
    ]
    for pos in range(4):
        for c in range(4):
            term = rb_recv[pos, c]
            sums = [jnp.where(owners[pos][c] == b, v + term, v) for b, v in enumerate(sums)]
    for b in range(nb):
        gf[:, b * BLOCK : (b + 1) * BLOCK] = sums[b].astype(BF16)
    stores.append(pltpu.make_async_copy(gf, grad_features, local_sem.at[0]))
    for copy in stores:
        copy.start()

    drain(b_x.at[0 : X_SIZE - 1], recv_sem.at[14])
    b_sum = b_x[0]
    for n in range(1, X_SIZE):
        b_sum = b_sum + b_x[n]
    gb[...] = b_sum * norm_scale
    stores.append(pltpu.make_async_copy(gb, grad_bias, local_sem.at[1]))
    stores[-1].start()

    drain(stage, send_sem.at[0])
    drain(xg.at[0, 0:others], send_sem.at[1])
    drain(ct.at[0:others], send_sem.at[2])
    drain(agg.at[0:others], send_sem.at[3])
    bias_swap.wait_send()
    drain(bkr.at[0:others], send_sem.at[5])
    drain(rs_recv.at[0 : xz - 1], send_sem.at[6])
    drain(rb_recv, send_sem.at[7])
    drain(y_recv.at[0:others], send_sem.at[8])
    drain(b_y.at[0:others], send_sem.at[10])
    drain(b_z.at[0 : z_size - 1], send_sem.at[11])
    swap.wait_send()
    own_act.wait()
    drain(b_x.at[0 : X_SIZE - 1], send_sem.at[14])
    drain(activated.at[:, 0 : others * vc], send_sem.at[9])
    drain(rs_recv.at[0 : xz - 1], send_sem.at[13])
    drain(grad_tiles.at[0 : xz - 1], recv_sem.at[13])
    drain(activated.at[:, 0 : others * vc], recv_sem.at[9])
    for copy in stores:
        copy.wait()


def place(*refs):
    ins, outs, (gs, gn, sems) = refs[0:4], refs[4:9], refs[9:12]
    tiles = ins[2]
    ready = (ins[0], ins[1], gs, gn, ins[3])
    copies = [pltpu.make_async_copy(ready[i], outs[i], sems.at[i]) for i in range(5)]
    for i in (0, 1, 4):
        copies[i].start()
    in_dim, hidden = gs.shape
    tpq = tiles.shape[1] // 16
    for kind, out in ((0, gs), (1, gn)):
        for r in range(in_dim // 16):
            for c in range(hidden // 128):
                n = (kind * in_dim // 16 + r) * (hidden // 128) + c
                out[r * 16 : (r + 1) * 16, c * 128 : (c + 1) * 128] = tiles[
                    n // tpq, (n % tpq) * 16 : (n % tpq + 1) * 16, :
                ].astype(F32)
        copies[2 + kind].start()
    for copy in copies:
        copy.wait()


def local(
    features,
    self_weight,
    neigh_weight,
    bias_vector,
    tile_values,
    tile_rows,
    tile_cols,
    send_blocks,
    cotangent,
):
    dom_size = lax.axis_size("dom")
    y_size = lax.axis_size("feat")
    xz = dom_size // CORES
    fr, vertices = features.shape
    hr = cotangent.shape[0]
    in_dim, hidden = self_weight.shape
    tile_count = tile_values.shape[0]
    nb = vertices // BLOCK
    vc = vertices // y_size
    rows = (2 * in_dim * hidden) // (128 * xz)
    dims = (
        dom_size,
        y_size,
        nb,
        tile_count,
        in_dim,
        hidden,
        1.0 / math.sqrt(vertices * dom_size),
    )
    hbm = pl.BlockSpec(memory_space=pl.ANY)
    dma = pltpu.SemaphoreType.DMA
    outs = pl.pallas_call(
        functools.partial(kernel, dims),
        out_shape=(
            jax.ShapeDtypeStruct((hr, vertices), BF16),
            jax.ShapeDtypeStruct((fr, vertices), BF16),
            jax.ShapeDtypeStruct((xz, rows, 128), BF16),
            jax.ShapeDtypeStruct((1, hidden), F32),
        ),
        in_specs=[hbm] * 9,
        out_specs=(hbm,) * 4,
        scratch_shapes=[
            pltpu.SMEM((tile_count,), jnp.int32),
            pltpu.SMEM((tile_count,), jnp.int32),
            pltpu.SMEM((1, 4, dom_size), jnp.int32),
            pltpu.SMEM((tile_count,), jnp.int32),
            pltpu.VMEM((fr, vertices), BF16),
            pltpu.VMEM((1, hidden), F32),
            pltpu.VMEM((fr, vertices), BF16),
            pltpu.VMEM((tile_count, BLOCK, BLOCK), BF16),
            pltpu.VMEM((in_dim, hidden), BF16),
            pltpu.VMEM((in_dim, hidden), BF16),
            pltpu.VMEM((hidden, in_dim), BF16),
            pltpu.VMEM((hidden, in_dim), BF16),
            pltpu.VMEM((1, hidden), F32),
            pltpu.VMEM((hidden, 128), F32),
            pltpu.VMEM((2, y_size, fr, vc), BF16),
            pltpu.VMEM((hidden, vc), F32),
            pltpu.VMEM((y_size, hr, vc), BF16),
            pltpu.VMEM((nb, fr, BLOCK), BF16),
            pltpu.VMEM((nb + 16, fr, BLOCK), BF16),
            pltpu.VMEM((4, 4, fr, BLOCK), BF16),
            pltpu.VMEM((y_size, fr, vc), BF16),
            pltpu.VMEM((y_size, hr, vc), BF16),
            pltpu.VMEM((y_size, 2 * fr, vc), BF16),
            pltpu.VMEM((y_size, 2 * fr, vc), BF16),
            pltpu.VMEM((nb, fr, BLOCK), BF16),
            pltpu.VMEM((tile_count, fr, 2 * BLOCK), BF16),
            pltpu.VMEM((nb * fr, tile_count * fr), BF16),
            pltpu.VMEM((16 * fr, tile_count * fr), BF16),
            pltpu.VMEM((nb * fr, tile_count * fr), BF16),
            pltpu.VMEM((4, 4, fr, BLOCK), F32),
            pltpu.VMEM((4, 4, fr, BLOCK), F32),
            pltpu.VMEM((xz, rows, 128), BF16),
            pltpu.VMEM((xz, rows, 128), BF16),
            pltpu.VMEM((rows, 128), F32),
            pltpu.VMEM((rows, 128), F32),
            pltpu.VMEM((rows, 128), F32),
            pltpu.VMEM((y_size, rows, 128), F32),
            pltpu.VMEM((rows, 128), BF16),
            pltpu.VMEM((4, 1, hidden), F32),
            pltpu.VMEM((1, hidden), F32),
            pltpu.VMEM((y_size, 1, hidden), F32),
            pltpu.VMEM((xz // X_SIZE, 1, hidden), F32),
            pltpu.VMEM((X_SIZE, 1, hidden), F32),
            pltpu.SemaphoreType.REGULAR,
            dma((10,)),
            dma((15,)),
            dma((15,)),
        ],
        compiler_params=pltpu.CompilerParams(
            collective_id=0, has_side_effects=True, vmem_limit_bytes=24 * 1024 * 1024
        ),
        name="graph_layer",
    )(
        *[
            pltpu.with_memory_space_constraint(operand, pltpu.HBM)
            for operand in (
                tile_rows,
                tile_cols,
                send_blocks.transpose(0, 2, 1),
                features,
                self_weight,
                neigh_weight,
                bias_vector.reshape(1, hidden),
                tile_values,
                cotangent,
            )
        ]
    )
    weight = jax.ShapeDtypeStruct((in_dim, hidden), F32)
    outs = pl.pallas_call(
        place,
        out_shape=(
            jax.ShapeDtypeStruct((hr, vertices), BF16),
            jax.ShapeDtypeStruct((fr, vertices), BF16),
            weight,
            weight,
            jax.ShapeDtypeStruct((1, hidden), F32),
        ),
        in_specs=[hbm, hbm, pl.BlockSpec(memory_space=pltpu.VMEM), hbm],
        out_specs=(hbm,) * 5,
        scratch_shapes=[
            pltpu.VMEM((in_dim, hidden), F32),
            pltpu.VMEM((in_dim, hidden), F32),
            dma((5,)),
        ],
        compiler_params=pltpu.CompilerParams(vmem_limit_bytes=8 * 1024 * 1024),
        name="place_outputs",
    )(*outs)
    activated, grad_features, grad_self, grad_neigh, grad_bias = outs
    return (activated, grad_features, grad_self, grad_neigh, grad_bias.reshape(hidden))


def solution(mesh):
    in_specs = (
        P("feat", "dom"),
        P(),
        P(),
        P(),
        P("dom", None, None),
        P("dom"),
        P("dom"),
        P("dom", None, None),
        P("feat", "dom"),
    )
    out_specs = (P("feat", "dom"), P("feat", "dom"), P(), P(), P())
    return jax.shard_map(local, mesh=mesh, in_specs=in_specs, out_specs=out_specs, check_vma=False)
```

```python
import functools
import math

import jax
import jax.numpy as jnp
from jax import lax
from jax.experimental import pallas as pl
from jax.experimental.pallas import tpu as pltpu
from jax.sharding import PartitionSpec as P

X_SIZE = 4
CORES = 2
BLOCK = 128
MESH = pl.DeviceIdType.MESH
F32 = jnp.float32
BF16 = jnp.bfloat16


def remote(src, dst, send_sem, recv_sem, device):
    return pltpu.make_async_remote_copy(
        src_ref=src,
        dst_ref=dst,
        send_sem=send_sem,
        recv_sem=recv_sem,
        device_id=device,
        device_id_type=MESH,
    )


def dot_nt(a, b):
    return lax.dot_general(a, b, (((1,), (1,)), ((), ())), preferred_element_type=F32)


def dot_nn(a, b):
    return lax.dot_general(a, b, (((1,), (0,)), ((), ())), preferred_element_type=F32)


def ring(step, size):
    return min(step, size - step)


def drain(ref, sem):
    pltpu.make_async_copy(ref, ref, sem).wait()


def one_hot(ids, nb, fr, base, out):
    rows = nb * fr
    per = 128 // fr
    lane = lax.broadcasted_iota(jnp.int32, (1, 128), 1)
    row = lax.broadcasted_iota(jnp.int32, (rows, 128), 0)
    for group in range(out.shape[1] // 128):
        key = jnp.zeros((1, 128), jnp.int32)
        for u in range(per):
            key = jnp.where(lane // fr == u, (ids[group * per + u] - base) * fr, key)
        key = key + lane % fr
        out[:, group * 128 : (group + 1) * 128] = jnp.where(row == key, 1.0, 0.0).astype(BF16)


def split(value):
    high = value.astype(BF16)
    return jnp.concatenate([high, (value - high.astype(F32)).astype(BF16)], axis=1)


def added(one_hots, parts):
    both = dot_nn(one_hots[...], parts[...].reshape(one_hots.shape[1], 2 * BLOCK))
    return both[:, :BLOCK] + both[:, BLOCK:]


def kernel(
    dims,
    rows_in,
    cols_in,
    blocks_in,
    features,
    self_weight,
    neigh_weight,
    bias,
    tile_values,
    cotangent,
    activated,
    grad_features,
    grad_tiles,
    grad_bias,
    tile_rows,
    tile_cols,
    send_blocks,
    slots,
    gf,
    gb,
    fv,
    tiles,
    w_self,
    w_neigh,
    wt_self,
    wt_neigh,
    bias_row,
    bias_mat,
    xg,
    pre_self,
    ct,
    own_tab,
    tab,
    stage,
    agg,
    act,
    bk,
    bkr,
    btab,
    prod,
    by_row,
    by_far,
    by_near,
    rb_send,
    rb_recv,
    part,
    rs_recv,
    t_src,
    t_core,
    y_src,
    y_recv,
    g_src,
    b_src,
    b_core,
    b_y,
    b_z,
    b_x,
    z_sem,
    local_sem,
    send_sem,
    recv_sem,
):
    dom_size, y_size, nb, tile_count, in_dim, hidden, norm_scale = dims
    z_size = dom_size // (X_SIZE * CORES)
    xz = X_SIZE * z_size
    fr = in_dim // y_size
    hr = hidden // y_size
    vb = nb // y_size
    vc = vb * BLOCK
    col_tiles = hidden // 128
    tpq = (2 * in_dim // 16) * col_tiles // xz
    others = y_size - 1

    dom = lax.axis_index("dom")
    fy = lax.axis_index("feat")
    core = lax.rem(dom, CORES)
    q = dom // CORES
    my_z = q // X_SIZE
    my_x = lax.rem(q, X_SIZE)

    offsets = (1, 2, dom_size - 1, dom_size // 2)
    y_steps = sorted(range(1, y_size), key=lambda d: -ring(d, y_size))
    y_peers = [lax.rem(fy + d, y_size) for d in y_steps]
    sibling = (q * CORES + 1 - core, fy)
    xz_steps = [(dz, dx) for dz in range(z_size) for dx in range(X_SIZE) if dz or dx]
    xz_steps.sort(key=lambda d: -ring(d[0], z_size) - ring(d[1], X_SIZE))
    xz_peers = [
        lax.rem(my_z + dz, z_size) * X_SIZE + lax.rem(my_x + dx, X_SIZE)
        for dz, dx in xz_steps
    ]

    def columns(ref, y):
        return ref.at[:, pl.ds(pl.multiple_of(y * vc, vc), vc)]

    loads = [
        pltpu.make_async_copy(src, dst, local_sem.at[i])
        for i, (src, dst) in enumerate(
            (
                (blocks_in, send_blocks),
                (features, fv),
                (cols_in, tile_cols),
                (rows_in, tile_rows),
                (self_weight, w_self),
                (neigh_weight, w_neigh),
                (bias, bias_row),
                (tile_values, tiles),
            )
        )
    ]
    barrier = pltpu.get_barrier_semaphore()
    z_peers = [
        ((lax.rem(my_z + d, z_size) * X_SIZE + my_x) * CORES + core, fy)
        for d in sorted(range(1, z_size), key=lambda d: -ring(d, z_size))
    ]
    greet = [device for pair in zip(z_peers, [(dom, p) for p in y_peers]) for device in pair]
    greet += z_peers[y_size - 1 :] + [(dom, p) for p in y_peers[z_size - 1 :]]
    for off in (1, dom_size - 1, 2, dom_size - 2):
        greet.append((lax.rem(dom + off, dom_size), fy))
    x_peers = [
        ((my_z * X_SIZE + lax.rem(my_x + d, X_SIZE)) * CORES + core, fy) for d in range(1, X_SIZE)
    ]
    greet += x_peers
    greet.append(sibling)
    for device in greet:
        pl.semaphore_signal(barrier, inc=1, device_id=device, device_id_type=MESH)
    for copy in loads:
        copy.start()

    loads[0].wait()
    owners = []
    for pos in range(4):
        to = lax.rem(dom + offsets[pos], dom_size)
        owners.append([send_blocks[0, c, to] for c in range(4)])
    loads[1].wait()
    for b in range(nb):
        own_tab[b] = fv[:, b * BLOCK : (b + 1) * BLOCK]
    for pos in range(4):
        for c in range(4):
            stage[pos, c] = own_tab[jnp.maximum(owners[pos][c], 0)]

    pl.semaphore_wait(barrier, len(greet))

    for pos in (3, 1, 0, 2):
        to = lax.rem(dom + offsets[pos], dom_size)
        remote(
            stage.at[pos],
            tab.at[pl.ds(nb + 4 * pos, 4)],
            send_sem.at[0],
            recv_sem.at[0],
            (to, fy),
        ).start()
    for p in y_peers:
        remote(columns(fv, p), xg.at[0, fy], send_sem.at[1], recv_sem.at[1], (dom, p)).start()
    for p in y_peers:
        remote(columns(cotangent, p), ct.at[fy], send_sem.at[2], recv_sem.at[2], (dom, p)).start()
    own_cot = pltpu.make_async_copy(columns(cotangent, fy), ct.at[fy], local_sem.at[8])
    own_cot.start()
    for device in z_peers:
        pl.semaphore_signal(z_sem, inc=1, device_id=device, device_id_type=MESH)
    xg[0, fy] = fv[:, pl.ds(pl.multiple_of(fy * vc, vc), vc)]

    for copy in loads[2:]:
        copy.wait()

    def slot_body(t, carry):
        col = tile_cols[t]
        far = jnp.maximum(col - nb, 0)
        back = lax.rem(dom + dom_size - far // 4, dom_size)
        place = jnp.where(
            back == offsets[0],
            0,
            jnp.where(back == offsets[1], 1, jnp.where(back == offsets[2], 2, 3)),
        )
        slots[t] = jnp.where(col < nb, col, nb + place * 4 + lax.rem(far, 4))
        return carry

    lax.fori_loop(0, tile_count, slot_body, 0, unroll=4)
    for b in range(nb):
        tab[b] = fv[:, b * BLOCK : (b + 1) * BLOCK]
    one_hot(tile_rows, nb, fr, 0, by_row)

    drain(stage, recv_sem.at[0])

    def agg_body(t, carry):
        prod[t] = split(dot_nt(tab[slots[t]], tiles[t]))
        return carry

    lax.fori_loop(0, tile_count, agg_body, 0, unroll=tile_count)
    sums = added(by_row, prod).astype(BF16)
    for b in range(nb):
        agg[b // vb, :, (b % vb) * BLOCK : (b % vb + 1) * BLOCK] = sums[b * fr : (b + 1) * fr]
    for p in y_peers:
        remote(agg.at[p], xg.at[1, fy], send_sem.at[3], recv_sem.at[3], (dom, p)).start()
    xg[1, fy] = agg[fy]

    for src, dst in ((w_self, wt_self), (w_neigh, wt_neigh)):
        dst[...] = src[...].astype(F32).T.astype(BF16)
    bias_mat[...] = jnp.broadcast_to(bias_row[...], (128, hidden)).T
    one_hot(slots, 16, fr, nb, by_far)
    one_hot(slots, nb, fr, 0, by_near)

    drain(xg.at[0, 0:others], recv_sem.at[1])
    early = dot_nn(wt_self[...], xg[0].reshape(in_dim, vc))
    pre_self[...] = early + jnp.concatenate([bias_mat[...]] * vb, axis=1)
    own_cot.wait()
    drain(ct.at[0:others], recv_sem.at[2])
    drain(agg.at[0:others], recv_sem.at[3])
    pre = pre_self[...] + dot_nn(wt_neigh[...], xg[1].reshape(in_dim, vc))
    sigma = jax.nn.sigmoid(pre)
    cot = ct[...].reshape(hidden, vc).astype(F32)
    dpre = (cot * sigma * (1.0 + pre * (1.0 - sigma))).astype(BF16)

    grads = dot_nt(xg[...].reshape(2 * in_dim, vc), dpre).astype(BF16)
    for rt in range(2 * in_dim // 16):
        for c in range(col_tiles):
            n = rt * col_tiles + c
            part[n // tpq, (n % tpq) * 16 : (n % tpq + 1) * 16, :] = grads[
                rt * 16 : (rt + 1) * 16, c * 128 : (c + 1) * 128
            ]
    pl.semaphore_wait(z_sem, z_size - 1)
    for p in xz_peers:
        remote(
            part.at[p], rs_recv.at[q], send_sem.at[6], recv_sem.at[6], (p * CORES + core, fy)
        ).start()
    rs_recv[q] = part[q]
    b_src[0] = dot_nt(jnp.ones((16, vc), BF16), dpre)[0:1]
    bias_swap = remote(b_src.at[0], b_core, send_sem.at[4], recv_sem.at[4], sibling)
    bias_swap.start()

    bk[:, 0:fr] = dot_nn(w_self[...], dpre).astype(BF16).reshape(y_size, fr, vc)
    bk[:, fr : 2 * fr] = dot_nn(w_neigh[...], dpre).astype(BF16).reshape(y_size, fr, vc)
    for p in y_peers:
        remote(bk.at[p], bkr.at[fy], send_sem.at[5], recv_sem.at[5], (dom, p)).start()
    bkr[fy] = bk[fy]
    act[...] = (pre * sigma).astype(BF16).reshape(y_size, hr, vc)

    bias_swap.wait_recv()
    b_sum = b_src[0] + b_core[...]
    b_src[1] = b_sum
    b_y[fy] = b_sum
    for p in y_peers:
        remote(b_src.at[1], b_y.at[fy], send_sem.at[10], recv_sem.at[10], (dom, p)).start()

    drain(rs_recv.at[0 : xz - 1], recv_sem.at[6])
    total = rs_recv[0].astype(F32)
    for n in range(1, xz):
        total = total + rs_recv[n].astype(F32)
    t_src[...] = total
    swap = remote(t_src, t_core, send_sem.at[12], recv_sem.at[12], sibling)
    swap.start()
    swap.wait_recv()
    total = total + t_core[...]
    y_src[...] = total
    y_recv[fy] = total
    for p in y_peers:
        remote(y_src, y_recv.at[fy], send_sem.at[8], recv_sem.at[8], (dom, p)).start()

    drain(b_y.at[0:others], recv_sem.at[10])
    b_sum = b_y[0]
    for n in range(1, y_size):
        b_sum = b_sum + b_y[n]
    b_src[2] = b_sum
    b_z[my_z] = b_sum
    for device in z_peers:
        remote(b_src.at[2], b_z.at[my_z], send_sem.at[11], recv_sem.at[11], device).start()

    drain(bkr.at[0:others], recv_sem.at[5])
    for b in range(nb):
        btab[b] = bkr[b // vb, fr : 2 * fr, (b % vb) * BLOCK : (b % vb + 1) * BLOCK]

    def spread_body(t, carry):
        prod[t] = split(dot_nn(btab[tile_rows[t]], tiles[t]))
        return carry

    lax.fori_loop(0, tile_count, spread_body, 0, unroll=tile_count)
    sums = added(by_far, prod)
    for n in range(16):
        rb_send[n // 4, n % 4] = sums[n * fr : (n + 1) * fr]
    for pos in (3, 1, 0, 2):
        to = lax.rem(dom + dom_size - offsets[pos], dom_size)
        remote(
            rb_send.at[pos], rb_recv.at[pos], send_sem.at[7], recv_sem.at[7], (to, fy)
        ).start()

    near = added(by_near, prod)

    drain(y_recv.at[0:others], recv_sem.at[8])
    total = y_recv[0]
    for n in range(1, y_size):
        total = total + y_recv[n]
    g_src[...] = (total * norm_scale).astype(BF16)
    for p in xz_peers:
        remote(
            g_src, grad_tiles.at[q], send_sem.at[13], recv_sem.at[13], (p * CORES + core, fy)
        ).start()
    for p in y_peers:
        remote(
            act.at[p], columns(activated, fy), send_sem.at[9], recv_sem.at[9], (dom, p)
        ).start()
    own_act = pltpu.make_async_copy(act.at[fy], columns(activated, fy), local_sem.at[9])
    own_act.start()
    stores = [pltpu.make_async_copy(g_src, grad_tiles.at[q], local_sem.at[2])]
    drain(b_z.at[0 : z_size - 1], recv_sem.at[11])
    b_sum = b_z[0]
    for n in range(1, z_size):
        b_sum = b_sum + b_z[n]
    b_src[3] = b_sum
    b_x[my_x] = b_sum
    for device in x_peers:
        remote(b_src.at[3], b_x.at[my_x], send_sem.at[14], recv_sem.at[14], device).start()

    drain(rb_recv, recv_sem.at[7])
    sums = [
        near[b * fr : (b + 1) * fr]
        + bkr[b // vb, 0:fr, (b % vb) * BLOCK : (b % vb + 1) * BLOCK].astype(F32)
        for b in range(nb)
    ]
    for pos in range(4):
        for c in range(4):
            term = rb_recv[pos, c]
            sums = [jnp.where(owners[pos][c] == b, v + term, v) for b, v in enumerate(sums)]
    for b in range(nb):
        gf[:, b * BLOCK : (b + 1) * BLOCK] = sums[b].astype(BF16)
    stores.append(pltpu.make_async_copy(gf, grad_features, local_sem.at[0]))
    for copy in stores:
        copy.start()

    drain(b_x.at[0 : X_SIZE - 1], recv_sem.at[14])
    b_sum = b_x[0]
    for n in range(1, X_SIZE):
        b_sum = b_sum + b_x[n]
    gb[...] = b_sum * norm_scale
    stores.append(pltpu.make_async_copy(gb, grad_bias, local_sem.at[1]))
    stores[-1].start()

    drain(stage, send_sem.at[0])
    drain(xg.at[0, 0:others], send_sem.at[1])
    drain(ct.at[0:others], send_sem.at[2])
    drain(agg.at[0:others], send_sem.at[3])
    bias_swap.wait_send()
    drain(bkr.at[0:others], send_sem.at[5])
    drain(rs_recv.at[0 : xz - 1], send_sem.at[6])
    drain(rb_recv, send_sem.at[7])
    drain(y_recv.at[0:others], send_sem.at[8])
    drain(b_y.at[0:others], send_sem.at[10])
    drain(b_z.at[0 : z_size - 1], send_sem.at[11])
    swap.wait_send()
    own_act.wait()
    drain(b_x.at[0 : X_SIZE - 1], send_sem.at[14])
    drain(activated.at[:, 0 : others * vc], send_sem.at[9])
    drain(rs_recv.at[0 : xz - 1], send_sem.at[13])
    drain(grad_tiles.at[0 : xz - 1], recv_sem.at[13])
    drain(activated.at[:, 0 : others * vc], recv_sem.at[9])
    for copy in stores:
        copy.wait()


def place(*refs):
    ins, outs, (gs, gn, sems) = refs[0:4], refs[4:9], refs[9:12]
    tiles = ins[2]
    ready = (ins[0], ins[1], gs, gn, ins[3])
    copies = [pltpu.make_async_copy(ready[i], outs[i], sems.at[i]) for i in range(5)]
    for i in (0, 1, 4):
        copies[i].start()
    in_dim, hidden = gs.shape
    tpq = tiles.shape[1] // 16
    for kind, out in ((0, gs), (1, gn)):
        for r in range(in_dim // 16):
            for c in range(hidden // 128):
                n = (kind * in_dim // 16 + r) * (hidden // 128) + c
                out[r * 16 : (r + 1) * 16, c * 128 : (c + 1) * 128] = tiles[
                    n // tpq, (n % tpq) * 16 : (n % tpq + 1) * 16, :
                ].astype(F32)
        copies[2 + kind].start()
    for copy in copies:
        copy.wait()


def local(
    features,
    self_weight,
    neigh_weight,
    bias_vector,
    tile_values,
    tile_rows,
    tile_cols,
    send_blocks,
    cotangent,
):
    dom_size = lax.axis_size("dom")
    y_size = lax.axis_size("feat")
    xz = dom_size // CORES
    fr, vertices = features.shape
    hr = cotangent.shape[0]
    in_dim, hidden = self_weight.shape
    tile_count = tile_values.shape[0]
    nb = vertices // BLOCK
    vc = vertices // y_size
    rows = (2 * in_dim * hidden) // (128 * xz)
    dims = (
        dom_size,
        y_size,
        nb,
        tile_count,
        in_dim,
        hidden,
        1.0 / math.sqrt(vertices * dom_size),
    )
    hbm = pl.BlockSpec(memory_space=pl.ANY)
    dma = pltpu.SemaphoreType.DMA
    outs = pl.pallas_call(
        functools.partial(kernel, dims),
        out_shape=(
            jax.ShapeDtypeStruct((hr, vertices), BF16),
            jax.ShapeDtypeStruct((fr, vertices), BF16),
            jax.ShapeDtypeStruct((xz, rows, 128), BF16),
            jax.ShapeDtypeStruct((1, hidden), F32),
        ),
        in_specs=[hbm] * 9,
        out_specs=(hbm,) * 4,
        scratch_shapes=[
            pltpu.SMEM((tile_count,), jnp.int32),
            pltpu.SMEM((tile_count,), jnp.int32),
            pltpu.SMEM((1, 4, dom_size), jnp.int32),
            pltpu.SMEM((tile_count,), jnp.int32),
            pltpu.VMEM((fr, vertices), BF16),
            pltpu.VMEM((1, hidden), F32),
            pltpu.VMEM((fr, vertices), BF16),
            pltpu.VMEM((tile_count, BLOCK, BLOCK), BF16),
            pltpu.VMEM((in_dim, hidden), BF16),
            pltpu.VMEM((in_dim, hidden), BF16),
            pltpu.VMEM((hidden, in_dim), BF16),
            pltpu.VMEM((hidden, in_dim), BF16),
            pltpu.VMEM((1, hidden), F32),
            pltpu.VMEM((hidden, 128), F32),
            pltpu.VMEM((2, y_size, fr, vc), BF16),
            pltpu.VMEM((hidden, vc), F32),
            pltpu.VMEM((y_size, hr, vc), BF16),
            pltpu.VMEM((nb, fr, BLOCK), BF16),
            pltpu.VMEM((nb + 16, fr, BLOCK), BF16),
            pltpu.VMEM((4, 4, fr, BLOCK), BF16),
            pltpu.VMEM((y_size, fr, vc), BF16),
            pltpu.VMEM((y_size, hr, vc), BF16),
            pltpu.VMEM((y_size, 2 * fr, vc), BF16),
            pltpu.VMEM((y_size, 2 * fr, vc), BF16),
            pltpu.VMEM((nb, fr, BLOCK), BF16),
            pltpu.VMEM((tile_count, fr, 2 * BLOCK), BF16),
            pltpu.VMEM((nb * fr, tile_count * fr), BF16),
            pltpu.VMEM((16 * fr, tile_count * fr), BF16),
            pltpu.VMEM((nb * fr, tile_count * fr), BF16),
            pltpu.VMEM((4, 4, fr, BLOCK), F32),
            pltpu.VMEM((4, 4, fr, BLOCK), F32),
            pltpu.VMEM((xz, rows, 128), BF16),
            pltpu.VMEM((xz, rows, 128), BF16),
            pltpu.VMEM((rows, 128), F32),
            pltpu.VMEM((rows, 128), F32),
            pltpu.VMEM((rows, 128), F32),
            pltpu.VMEM((y_size, rows, 128), F32),
            pltpu.VMEM((rows, 128), BF16),
            pltpu.VMEM((4, 1, hidden), F32),
            pltpu.VMEM((1, hidden), F32),
            pltpu.VMEM((y_size, 1, hidden), F32),
            pltpu.VMEM((xz // X_SIZE, 1, hidden), F32),
            pltpu.VMEM((X_SIZE, 1, hidden), F32),
            pltpu.SemaphoreType.REGULAR,
            dma((10,)),
            dma((15,)),
            dma((15,)),
        ],
        compiler_params=pltpu.CompilerParams(
            collective_id=0, has_side_effects=True, vmem_limit_bytes=24 * 1024 * 1024
        ),
        name="graph_layer",
    )(
        *[
            pltpu.with_memory_space_constraint(operand, pltpu.HBM)
            for operand in (
                tile_rows,
                tile_cols,
                send_blocks.transpose(0, 2, 1),
                features,
                self_weight,
                neigh_weight,
                bias_vector.reshape(1, hidden),
                tile_values,
                cotangent,
            )
        ]
    )
    weight = jax.ShapeDtypeStruct((in_dim, hidden), F32)
    outs = pl.pallas_call(
        place,
        out_shape=(
            jax.ShapeDtypeStruct((hr, vertices), BF16),
            jax.ShapeDtypeStruct((fr, vertices), BF16),
            weight,
            weight,
            jax.ShapeDtypeStruct((1, hidden), F32),
        ),
        in_specs=[hbm, hbm, pl.BlockSpec(memory_space=pltpu.VMEM), hbm],
        out_specs=(hbm,) * 5,
        scratch_shapes=[
            pltpu.VMEM((in_dim, hidden), F32),
            pltpu.VMEM((in_dim, hidden), F32),
            dma((5,)),
        ],
        compiler_params=pltpu.CompilerParams(vmem_limit_bytes=8 * 1024 * 1024),
        name="place_outputs",
    )(*outs)
    activated, grad_features, grad_self, grad_neigh, grad_bias = outs
    return (activated, grad_features, grad_self, grad_neigh, grad_bias.reshape(hidden))


def solution(mesh):
    in_specs = (
        P("feat", "dom"),
        P(),
        P(),
        P(),
        P("dom", None, None),
        P("dom"),
        P("dom"),
        P("dom", None, None),
        P("feat", "dom"),
    )
    out_specs = (P("feat", "dom"), P("feat", "dom"), P(), P(), P())
    return jax.shard_map(local, mesh=mesh, in_specs=in_specs, out_specs=out_specs, check_vma=False)
```
